32 devices in a mesh: seq: 8 (over y, x, core), fsdp: 4 (over z).
Axes of the slice: x: 2, y: 2, z: 4, core: 2. Of those that a mesh axis runs over, the one named last changes fastest.
Arguments:
- tokens_in: bfloat16 [8, 1024, 2048], P('fsdp', 'seq'), may hold values from -6 to 6
- segments: int32 [8, 1024], P('fsdp'), may hold values from 0 to 2, as said below
- routes: int32 [8, 1024, 6], P('fsdp', 'seq'), may hold values from 0 to 15, all different within a row; in each aligned block of 128 rows (0 to 127, 128 to 255, ..., all dimensions but the last counted through in order) at most 64 rows name the same one
- cotangent: bfloat16 [8, 1024, 2048], P('fsdp', 'seq'), may hold values from -6 to 6
- g_attn: bfloat16 [2048], P(('seq', 'fsdp')), may hold values from 0.5 to 1.5
- g_kv: bfloat16 [512], P(('seq', 'fsdp')), may hold values from 0.5 to 1.5
- g_moe: bfloat16 [2048], P(('seq', 'fsdp')), may hold values from 0.5 to 1.5
- w_query: bfloat16 [2048, 3072], P(('seq', 'fsdp')), may hold values from -0.125 to 0.125
- w_kv_down: bfloat16 [2048, 576], P(('seq', 'fsdp')), may hold values from -0.125 to 0.125
- w_kv_up: bfloat16 [512, 4096], P(None, ('seq', 'fsdp')), may hold values from -0.25 to 0.25
- w_out: bfloat16 [2048, 2048], P(None, ('seq', 'fsdp')), may hold values from -0.5 to 0.5
- w_router: bfloat16 [2048, 16], P(('seq', 'fsdp')), may hold values from -0.0625 to 0.0625
- w_shared_gate: bfloat16 [2048, 2816], P(('seq', 'fsdp')), may hold values from -0.125 to 0.125
- w_shared_up: bfloat16 [2048, 2816], P(('seq', 'fsdp')), may hold values from -0.125 to 0.125
- w_shared_down: bfloat16 [2816, 2048], P(None, ('seq', 'fsdp')), may hold values from -0.109375 to 0.109375
- w_expert_gate: bfloat16 [32, 2048, 704], P(('seq', 'fsdp')), may hold values from -0.125 to 0.125
- w_expert_up: bfloat16 [32, 2048, 704], P(('seq', 'fsdp')), may hold values from -0.125 to 0.125
- w_expert_down: bfloat16 [32, 704, 2048], P(('seq', 'fsdp')), may hold values from -6 to 6
Outputs:
- output: bfloat16 [8, 1024, 2048], P('fsdp', 'seq')
- input_grad: float32 [8, 1024, 2048], P('fsdp', 'seq')
- grad_g_attn: float32 [2048], P(('seq', 'fsdp'))
- grad_g_kv: float32 [512], P(('seq', 'fsdp'))
- grad_g_moe: float32 [2048], P(('seq', 'fsdp'))
- grad_query: float32 [2048, 3072], P(('seq', 'fsdp'))
- grad_kv_down: float32 [2048, 576], P(('seq', 'fsdp'))
- grad_kv_up: float32 [512, 4096], P(None, ('seq', 'fsdp'))
- grad_out: float32 [2048, 2048], P(None, ('seq', 'fsdp'))
- grad_router: float32 [2048, 16], P(('seq', 'fsdp'))
- grad_shared_gate: float32 [2048, 2816], P(('seq', 'fsdp'))
- grad_shared_up: float32 [2048, 2816], P(('seq', 'fsdp'))
- grad_shared_down: float32 [2816, 2048], P(None, ('seq', 'fsdp'))
- grad_expert_gate: float32 [32, 2048, 704], P(('seq', 'fsdp'))
- grad_expert_up: float32 [32, 2048, 704], P(('seq', 'fsdp'))
- grad_expert_down: float32 [32, 704, 2048], P(('seq', 'fsdp'))
The draws below stay inside these ranges and needn't reach their ends.
Inputs may be any that keep to these rules, and one draw needn't show every extreme that they name: `segments`: along each sequence the numbers start at 0 and never fall; of the 2 sequences of each index of fsdp, one, drawn from the seed, is a single document numbered 0; each other sequence has three documents, numbered 0, 1 and 2, the first two of 33 to 400 tokens each and the third holding the rest. `routes`: a token's 6 experts differ; within the 128 tokens of one sequence on one device of seq, no expert is named more than 64 times, a bound that some block reaches.
All inputs are finite; a program needn't handle non-finite values.
Results may differ from the reference program's by a relative error of at most 0.023.
Values may be sent and summed in bfloat16 or wider, within the bound.
No kernel may reach another device: no remote copies, remote signals or barrier semaphores. Data moves between devices by JAX's collectives and lax.ppermute only.
A program may use at most 448 MiB of HBM per device.

```python
import math
import jax
import jax.numpy as jnp
import numpy as np
from jax import lax

D = 2048
HEADS = 16
NOPE = 128
ROPE = 64
VDIM = 128
KVR = 512
FFE = 1408
TOP = 6
MB = 2
LENGTH = 1024
TOK = 128
SEQS = 8
EXPERTS = 16
FFS = 2816
HALF = 704
CAP = 64
DEVICES = 32


def draw_segments(key, part):
    key = jax.random.fold_in(key, 11)
    lengths = jax.random.randint(jax.random.fold_in(key, 1), (SEQS, 2), LENGTH // 32 + 1, LENGTH * 25 // 64 + 1)
    ends = jnp.cumsum(lengths, axis=1)
    places = jnp.arange(LENGTH)
    numbers = jnp.sum((ends[:, None, :] <= places[None, :, None]).astype(jnp.int32), axis=2)
    chosen = jax.random.randint(jax.random.fold_in(key, 2), (SEQS // MB,), 0, MB)
    single = jnp.arange(SEQS) % MB == jnp.repeat(chosen, MB)
    return jnp.where(single[:, None], 0, numbers).astype(jnp.int32)


def block_scale(rng, shape, cuts, smallest, largest):
    loudness = 1.0
    for position, shards_of in cuts:
        steps = jax.random.uniform(jax.random.fold_in(jax.random.fold_in(rng, 6), position), (shards_of,), jnp.float32, smallest / len(cuts), largest / len(cuts))
        loudness = loudness * jnp.repeat(jnp.exp(steps), shape[position] // shards_of).reshape((-1,) + (1,) * (len(shape) - 1 - position))
    return loudness


def routed_block(rng, own, number, rows, count, top, bound, skew):
    order = jax.random.permutation(rng, count)
    crowded, ordinary = portions_of(count, rows * top, bound, skew, True), portions_of(count, rows * top, bound, skew, False)
    places = jnp.arange(count)

    def named(sizes, turn):
        used = int((sizes > 0).sum())
        fixed = max(1, used // 4)
        moved = fixed + (places - fixed + turn * (used - fixed)) % max(1, count - fixed)
        return jnp.zeros((count,), jnp.int32).at[order[jnp.where(places < fixed, places, moved)]].set(jnp.asarray(sizes, jnp.int32))

    sizes = jnp.where(number % 4 == 0, named(crowded, number // 4), named(ordinary, number - number // 4 - 1))
    mixed = jax.random.permutation(jax.random.fold_in(own, 3), count)
    donor, receiver = mixed[0:count // 2 * 2:2], mixed[1:count // 2 * 2:2]
    margin = jnp.minimum(sizes[donor] - 1, bound - sizes[receiver]) // 2
    margin = jnp.where((donor == order[0]) | (receiver == order[0]) | (sizes[receiver] == 0), 0, jnp.maximum(margin, 0))
    moved = jax.random.randint(jax.random.fold_in(own, 4), (count // 2,), 0, 1 << 20) % (margin + 1)
    sizes = sizes.at[donor].add(-moved).at[receiver].add(moved)
    members = jnp.searchsorted(jnp.cumsum(sizes), jnp.arange(rows * top), side="right").astype(jnp.int32)
    grid = members.reshape(top, rows).T
    grid = grid[jax.random.permutation(jax.random.fold_in(own, 1), rows)]
    turn = jax.random.randint(jax.random.fold_in(own, 2), (rows, 1), 0, top)
    return jnp.take_along_axis(grid, (jnp.arange(top)[None, :] + turn) % top, axis=1)


def portions_of(count, total, most, slope, full):
    weights = [(1 << 20) // math.isqrt(standing ** slope) + 1 for standing in range(1, count + 1)]
    largest = most if full else min(most, max(-(-total // count), total * weights[0] // sum(weights)))
    least = 1 if total - largest >= count - 1 else 0
    counts, surplus = [largest] + [least] * (count - 1), total - largest - least * (count - 1)
    while surplus > 0:
        candidates = [i for i in range(1, count) if counts[i] < largest] or [i for i in range(1, count) if counts[i] < most]
        mass, left = sum([weights[i] for i in candidates]), surplus
        for i in candidates:
            more = min(most - counts[i], max(1, left * weights[i] // mass), surplus)
            counts[i] = counts[i] + more
            surplus = surplus - more
    return np.array(counts)


def bell_draw(own_key, shape, spread, limit, shards=(), kind=jnp.bfloat16):
    level = block_scale(own_key, shape, shards, -0.22, 0.18) if shards else 1.0
    drawn = jax.random.normal(own_key, shape, jnp.float32) * spread * level
    return jnp.minimum(jnp.maximum(drawn, -limit), limit).astype(kind)


def setup_inputs(seed: int = 0) -> dict:
    arg_keys = jax.random.split(jax.random.key(seed), 19)
    tokens_in = bell_draw(arg_keys[0], (SEQS, LENGTH, D), 1.0, 6.0, ((0, 4), (1, 8)))
    segments = draw_segments(jax.random.fold_in(arg_keys[18], 71), 0)
    routes_keys = jax.random.split(jax.random.fold_in(arg_keys[2], 1), SEQS * LENGTH // TOK)
    routes_turns = jax.random.permutation(jax.random.fold_in(arg_keys[2], 3), SEQS * LENGTH // TOK)
    routes = jax.vmap(lambda own, number: routed_block(jax.random.fold_in(arg_keys[2], 2), own, number, TOK, EXPERTS, TOP, CAP, 1))(routes_keys, routes_turns).reshape((SEQS, LENGTH, TOP))
    cotangent = bell_draw(arg_keys[3], (SEQS, LENGTH, D), 1.0, 6.0, ((0, 4), (1, 8)))
    g_attn = jnp.clip(1.0 + 0.1 * jax.random.normal(arg_keys[4], (D,), jnp.float32), 0.5, 1.5).astype(jnp.bfloat16)
    g_kv = jnp.clip(1.0 + 0.1 * jax.random.normal(arg_keys[5], (KVR,), jnp.float32), 0.5, 1.5).astype(jnp.bfloat16)
    g_moe = jnp.clip(1.0 + 0.1 * jax.random.normal(arg_keys[6], (D,), jnp.float32), 0.5, 1.5).astype(jnp.bfloat16)
    w_query = bell_draw(arg_keys[7], (D, HEADS * (NOPE + ROPE)), D ** -0.5, 0.125, ((0, 32),))
    w_kv_down = bell_draw(arg_keys[8], (D, KVR + ROPE), D ** -0.5, 0.125, ((0, 32),))
    w_kv_up = bell_draw(arg_keys[9], (KVR, HEADS * (NOPE + VDIM)), KVR ** -0.5, 0.25, ((1, 32),))
    w_out = bell_draw(arg_keys[10], (HEADS * VDIM, D), (HEADS * VDIM // 16) ** -0.5, 0.5, ((1, 32),))
    w_router = bell_draw(arg_keys[11], (D, EXPERTS), (4 * D) ** -0.5, 0.0625, ((0, 32),))
    w_shared_gate = bell_draw(arg_keys[12], (D, FFS), D ** -0.5, 0.125, ((0, 32),))
    w_shared_up = bell_draw(arg_keys[13], (D, FFS), D ** -0.5, 0.125, ((0, 32),))
    w_shared_down = bell_draw(arg_keys[14], (FFS, D), FFS ** -0.5, 0.109375, ((1, 32),))
    w_expert_gate = bell_draw(arg_keys[15], (DEVICES, D, HALF), D ** -0.5, 0.125, ((0, 32),))
    w_expert_up = bell_draw(arg_keys[16], (DEVICES, D, HALF), D ** -0.5, 0.125, ((0, 32),))
    w_expert_down = bell_draw(arg_keys[17], (DEVICES, HALF, D), (max(1, FFE // 1024)) ** -0.5, 6.0, ((0, 32),))
    return dict(tokens_in=tokens_in, segments=segments, routes=routes, cotangent=cotangent, g_attn=g_attn, g_kv=g_kv, g_moe=g_moe, w_query=w_query, w_kv_down=w_kv_down, w_kv_up=w_kv_up, w_out=w_out, w_router=w_router, w_shared_gate=w_shared_gate, w_shared_up=w_shared_up, w_shared_down=w_shared_down, w_expert_gate=w_expert_gate, w_expert_up=w_expert_up, w_expert_down=w_expert_down)


@jax.custom_vjp
def low(v):
    return lax.optimization_barrier(v.astype(jnp.bfloat16)).astype(jnp.float32)

@jax.custom_vjp
def low_back(v):
    return v

def low_keep(v):
    return (low(v), None)

def low_pass(kept, grad):
    return (grad,)

def back_keep(v):
    return (v, None)

def back_low(kept, grad):
    return (low(grad),)
low.defvjp(low_keep, low_pass)
low_back.defvjp(back_keep, back_low)
EPS = 1e-06
THETA = 10000.0
NEGATIVE = -1e+30
HIGHEST = lax.Precision.HIGHEST

def product(left, right):
    return jnp.matmul(left, right, precision=HIGHEST)

def normed(value, gain):
    return value * lax.rsqrt(lax.optimization_barrier(jnp.mean(value * value, axis=-1, keepdims=True)) + EPS) * gain

def rotate(value, angles):
    middle = value.shape[-1] // 2
    cosine = jnp.cos(angles)
    sine = jnp.sin(angles)
    first = value[..., :middle]
    second = value[..., middle:]
    return jnp.concatenate([first * cosine - second * sine, second * cosine + first * sine], axis=-1)

def silu(value):
    return value * jax.nn.sigmoid(value)

def softmax_rows(scores):
    shifted = jnp.exp(scores - lax.optimization_barrier(jnp.max(scores, axis=-1, keepdims=True)))
    return shifted / lax.optimization_barrier(jnp.sum(shifted, axis=-1, keepdims=True))

def attend(pieces):
    query, keys, values, segment = pieces
    scores = jnp.einsum('qhd,khd->hqk', query, keys, precision=HIGHEST) * (NOPE + ROPE) ** (-0.5)
    scores = low_back(scores)
    places = jnp.arange(LENGTH)
    allowed = (segment[:, None] == segment[None, :]) & (places[None, :] <= places[:, None])
    scores = jnp.where(allowed[None], scores, NEGATIVE)
    weights = low(softmax_rows(scores))
    return jnp.einsum('hqk,khd->qhd', weights, values, precision=HIGHEST)

def forward(tokens, weights, segments, routes):
    gain_one, gain_latent, gain_two, query_weight, down_weight, up_weight, out_weight, router_weight, shared_gate, shared_up, shared_down, expert_gate_output, expert_up_output, expert_down = weights
    count = SEQS * LENGTH
    flat = tokens.reshape(count, D)
    frequency = THETA ** (-jnp.arange(ROPE // 2, dtype=jnp.float32) * 2.0 / ROPE)
    angles = jnp.arange(LENGTH, dtype=jnp.float32)[:, None] * frequency[None, :]
    normed_one = low(normed(flat, gain_one))
    query_raw = low_back(product(normed_one, query_weight)).reshape(SEQS, LENGTH, HEADS, NOPE + ROPE)
    query = low(jnp.concatenate([query_raw[..., :NOPE], rotate(query_raw[..., NOPE:], angles[None, :, None, :])], axis=-1))
    latent = low_back(product(normed_one, down_weight))
    latent_norm = low(normed(latent[:, :KVR], gain_latent))
    key_rope = low(rotate(latent[:, KVR:].reshape(SEQS, LENGTH, ROPE), angles[None]))
    key_value = low(product(latent_norm, up_weight)).reshape(SEQS, LENGTH, HEADS, NOPE + VDIM)
    keys = jnp.concatenate([key_value[..., :NOPE], jnp.broadcast_to(key_rope[:, :, None, :], (SEQS, LENGTH, HEADS, ROPE))], axis=-1)
    values = key_value[..., NOPE:]
    attended = lax.map(jax.checkpoint(attend), (query, keys, values, segments))
    attended = low(low_back(attended)).reshape(count, HEADS * VDIM)
    residual = flat + low_back(product(attended, out_weight))
    normed_two = low(normed(residual, gain_two))
    logits = low_back(product(normed_two, router_weight))
    router = softmax_rows(logits)
    picks = routes.reshape(count, TOP)
    gates = jnp.take_along_axis(router, picks, axis=1)
    shared_gate_pre = low_back(product(normed_two, shared_gate))
    shared_up_pre = low_back(product(normed_two, shared_up))
    shared_out = product(low(silu(shared_gate_pre) * shared_up_pre), shared_down)
    blocks = count // TOK
    block_ids = picks.reshape(blocks, TOK * TOP)
    marks = (block_ids[:, :, None] == jnp.arange(EXPERTS)[None, None, :]).astype(jnp.int32)
    ranks = lax.optimization_barrier(jnp.sum(jnp.cumsum(marks, axis=1) * marks, axis=2)) - 1
    slots = (jnp.arange(blocks)[:, None] * CAP + ranks).reshape(-1)
    expert_ids = block_ids.reshape(-1)
    owners = (jnp.arange(count * TOP) // TOP).astype(jnp.int32)
    slot_token = jnp.zeros((EXPERTS, blocks * CAP), jnp.int32).at[expert_ids, slots].set(owners)
    slot_live = jnp.zeros((EXPERTS, blocks * CAP), jnp.float32).at[expert_ids, slots].set(1.0)

    def expert_rows(pieces):
        index, live, gate_pair, up_pair, down_pair = pieces
        rows = normed_two[index] * live[:, None]
        total = jnp.zeros((blocks * CAP, D), jnp.float32)
        for member in range(2):
            gate_pre = low_back(product(rows, gate_pair[member]))
            up_pre = low_back(product(rows, up_pair[member]))
            total = total + low(product(low(silu(gate_pre) * up_pre), down_pair[member]))
        return low_back(total)
    results = lax.map(jax.checkpoint(expert_rows), (slot_token, slot_live, expert_gate_output.reshape(EXPERTS, 2, D, HALF), expert_up_output.reshape(EXPERTS, 2, D, HALF), expert_down.reshape(EXPERTS, 2, HALF, D)))
    route_out = results[expert_ids, slots].reshape(count, TOP, D)
    routed = lax.optimization_barrier(jnp.sum(gates[:, :, None] * route_out, axis=1))
    return (residual + shared_out + routed).reshape(SEQS, LENGTH, D)

def reference(tokens_in, segments, routes, cotangent, g_attn, g_kv, g_moe, w_query, w_kv_down, w_kv_up, w_out, w_router, w_shared_gate, w_shared_up, w_shared_down, w_expert_gate, w_expert_up, w_expert_down):
    weights = tuple((w.astype(jnp.float32) for w in (g_attn, g_kv, g_moe, w_query, w_kv_down, w_kv_up, w_out, w_router, w_shared_gate, w_shared_up, w_shared_down, w_expert_gate, w_expert_up, w_expert_down)))

    def apply_block(tokens, params):
        return forward(tokens, params, segments, routes)
    result, pullback = jax.vjp(apply_block, tokens_in.astype(jnp.float32), weights)
    grad_tokens, grads = pullback(cotangent.astype(jnp.float32))
    return (result.astype(jnp.bfloat16), grad_tokens, grads[0], grads[1], grads[2], grads[3], grads[4], grads[5], grads[6], grads[7], grads[8], grads[9], grads[10], grads[11], grads[12], grads[13])
```

```python
import functools

import jax
import jax.numpy as jnp
from jax import lax
from jax.experimental import pallas as pl
from jax.experimental.pallas import tpu as pltpu
from jax.sharding import PartitionSpec as P

HEADS = 16
NOPE = 128
ROPE = 64
VDIM = 128
KVR = 512

EPS = 1e-06
THETA = 10000.0
NEGATIVE = -1e30
BOTH = ("seq", "fsdp")
VMEM_LIMIT = 60 * 2**20
F32 = jnp.float32
BF16 = jnp.bfloat16


def product(left, right):
    return jnp.dot(left, right, preferred_element_type=F32)


def left_product(left, right):
    return lax.dot_general(left, right, (((0,), (0,)), ((), ())), preferred_element_type=F32)


def right_product(left, right):
    return lax.dot_general(left, right, (((1,), (1,)), ((), ())), preferred_element_type=F32)


def normed(value):
    factor = lax.rsqrt(jnp.mean(value * value, axis=-1, keepdims=True) + EPS)
    return (value * factor, factor)


def norm_back(grad_unit, unit, factor):
    return factor * (grad_unit - unit * jnp.mean(grad_unit * unit, axis=-1, keepdims=True))


def rotate(value, angles):
    middle = value.shape[-1] // 2
    cosine = jnp.cos(angles)
    sine = jnp.sin(angles)
    first = value[..., :middle]
    second = value[..., middle:]
    return jnp.concatenate(
        [first * cosine - second * sine, second * cosine + first * sine], axis=-1
    )


def silu_parts(value):
    logistic = jax.nn.sigmoid(value)
    return (value * logistic, logistic * (1.0 + value * (1.0 - logistic)))


def halve(value, axis, bit):
    count = lax.axis_size("seq")
    keep = lax.index_in_dim(value, 0, axis, keepdims=False)
    send = lax.index_in_dim(value, 1, axis, keepdims=False)
    return add_pair(keep, lax.ppermute(send, "seq", [(i, i ^ (1 << bit)) for i in range(count)]))


def add_pair(left, right):
    return (left.astype(F32) + right.astype(F32)).astype(BF16)


def line_reduce(value, axis):
    count = lax.axis_size("fsdp")
    place = lax.axis_index("fsdp")

    def piece(index):
        return lax.dynamic_index_in_dim(
            value, jnp.clip(index, 0, count - 1), axis, keepdims=False
        )

    up = down = None
    for step in range(1, count):
        send_up = piece(place + count - step)
        send_down = piece(place - count + step)
        if up is not None:
            send_up = add_pair(send_up, up)
            send_down = add_pair(send_down, down)
        up = lax.ppermute(send_up, "fsdp", [(i, i + 1) for i in range(step)])
        down = lax.ppermute(send_down, "fsdp", [(i, i - 1) for i in range(count - step, count)])
    total = piece(place).astype(F32) + up.astype(F32) + down.astype(F32)
    return total.astype(BF16)


def cuts_of(width):
    unit = width // 8
    return (0, 3 * unit, 6 * unit, width)


def reduce_home(keeps, sends, rows):
    seqs, line = lax.axis_size("seq"), lax.axis_size("fsdp")
    bits = list(range(1, seqs.bit_length() - 1))
    orders = (
        bits[:1] + ["line"] + bits[1:],
        bits[::-1] + ["line"],
        ["line"] + bits[::-1],
    )
    results = []
    for order, keep, send in zip(orders, keeps, sends):
        got = lax.ppermute(send, "seq", [(i, i ^ 1) for i in range(seqs)])
        part = add_pair(keep, got).reshape((2,) * len(bits) + (line, rows, keep.shape[-1]))
        names = bits[::-1] + ["line"]
        for step in order:
            axis = names.index(step)
            part = line_reduce(part, axis) if step == "line" else halve(part, axis, step)
            names.pop(axis)
        results.append(part)
    return jnp.concatenate(results, axis=-1)


def one_hot(slots, capacity):
    rows = slots.shape[-1]
    return lax.broadcasted_iota(jnp.int32, (capacity, rows), 0) == slots


def hidden_kernel(
    blocks,
    capacity,
    experts,
    hidden,
    place_ref,
    slots_ref,
    tokens_ref,
    top_ref,
    wide_ref,
    shared_ref,
    gate_ref,
    up_ref,
    down_ref,
    taken_ref,
    taken_top_ref,
    hidden_ref,
    pre_ref,
    post_ref,
    shared_hidden_ref,
    shared_grad_ref,
    gate_grad_ref,
):
    rows = slots_ref.shape[-1]
    lanes = shared_ref.shape[-1]
    expert = place_ref[0]
    wide = jnp.dot(tokens_ref[...], wide_ref[...], preferred_element_type=F32)
    back = jnp.dot(top_ref[...], shared_ref[...], preferred_element_type=F32)
    first = wide[:, :lanes]
    second = wide[:, lanes:]
    silu, slope = silu_parts(first)
    shared_hidden_ref[...] = (silu * second).astype(BF16)
    shared_grad_ref[:, :lanes] = (back * second * slope).astype(BF16)
    shared_grad_ref[:, lanes:] = (back * silu).astype(BF16)
    lane = lax.broadcasted_iota(jnp.int32, first.shape, 1)
    logits = jnp.where((lane >= hidden) & (lane < hidden + experts), first, NEGATIVE)
    powers = jnp.exp(logits - jnp.max(logits, axis=-1, keepdims=True))
    total = jnp.sum(powers, axis=-1, keepdims=True)
    gates = jnp.sum(jnp.where(lane == hidden + expert, powers, 0.0), axis=-1, keepdims=True)
    gates = jnp.broadcast_to(gates / total, first.shape)
    slot_gates = []
    for block in range(blocks):
        chosen = one_hot(slots_ref[block], capacity)
        low = chosen.astype(BF16)
        own = pl.ds(block * rows, rows)
        there = pl.ds(block * capacity, capacity)
        taken_ref[there, :] = jnp.dot(
            low, tokens_ref[own, :], preferred_element_type=F32
        ).astype(BF16)
        taken_top_ref[there, :] = jnp.dot(
            low, top_ref[own, :], preferred_element_type=F32
        ).astype(BF16)
        slot_gates.append(
            jnp.dot(
                chosen.astype(F32),
                gates[block * rows : (block + 1) * rows],
                precision=lax.Precision.HIGHEST,
                preferred_element_type=F32,
            )[:, :1]
        )
    slot_gates = jnp.concatenate(slot_gates, axis=0)
    gate_pre = jnp.dot(taken_ref[...], gate_ref[...], preferred_element_type=F32)
    up_pre = jnp.dot(taken_ref[...], up_ref[...], preferred_element_type=F32)
    grad = jnp.dot(taken_top_ref[...], down_ref[...], preferred_element_type=F32)
    swish, slope = silu_parts(gate_pre)
    made = swish * up_pre
    hidden_ref[...] = (made * slot_gates).astype(BF16)
    slot_grads = jnp.sum(made * grad, axis=-1, keepdims=True)
    grad = grad * slot_gates
    pre_ref[...] = (grad * up_pre * slope).astype(BF16)
    post_ref[...] = (grad * swish).astype(BF16)
    for block in range(blocks):
        chosen = one_hot(slots_ref[block], capacity)
        gate_grad_ref[block] = jnp.sum(
            jnp.where(chosen, slot_grads[block * capacity : (block + 1) * capacity], 0.0),
            axis=0,
            keepdims=True,
        )


def whole_spec(array):
    return pl.BlockSpec(
        array.shape, lambda i, *_: (0,) * array.ndim, pipeline_mode=pl.Buffered(1)
    )


def hidden_stage(place, slots, tokens, top, weights, capacity, experts, hidden):
    wide_weight, shared_down, gate_weight, up_weight, down_weight = weights
    devices, _, rows = slots.shape
    blocks = 2 * lax.axis_size("fsdp")
    steps = devices // blocks
    width = tokens.shape[1]
    half = gate_weight.shape[1]
    lanes = shared_down.shape[1]
    count = blocks * capacity

    def rows_spec(size, columns):
        return pl.BlockSpec((size, columns), lambda i, *_: (i, 0))

    slots_spec = pl.BlockSpec((blocks, 1, rows), lambda i, *_: (i, 0, 0))
    flops = devices * 2 * (3 * capacity * width * half + rows * width * 3 * lanes)
    return pl.pallas_call(
        functools.partial(hidden_kernel, blocks, capacity, experts, hidden),
        grid_spec=pltpu.PrefetchScalarGridSpec(
            num_scalar_prefetch=1,
            grid=(steps,),
            in_specs=[
                slots_spec,
                rows_spec(blocks * rows, width),
                rows_spec(blocks * rows, width),
                *[whole_spec(weight) for weight in weights],
            ],
            out_specs=[
                rows_spec(count, width),
                rows_spec(count, width),
                rows_spec(count, half),
                rows_spec(count, half),
                rows_spec(count, half),
                rows_spec(blocks * rows, lanes),
                rows_spec(blocks * rows, 2 * lanes),
                slots_spec,
            ],
        ),
        out_shape=[
            jax.ShapeDtypeStruct((steps * count, width), BF16),
            jax.ShapeDtypeStruct((steps * count, width), BF16),
            jax.ShapeDtypeStruct((steps * count, half), BF16),
            jax.ShapeDtypeStruct((steps * count, half), BF16),
            jax.ShapeDtypeStruct((steps * count, half), BF16),
            jax.ShapeDtypeStruct((devices * rows, lanes), BF16),
            jax.ShapeDtypeStruct((devices * rows, 2 * lanes), BF16),
            jax.ShapeDtypeStruct(slots.shape, F32),
        ],
        compiler_params=pltpu.CompilerParams(vmem_limit_bytes=VMEM_LIMIT),
        cost_estimate=pl.CostEstimate(
            flops=flops, bytes_accessed=3 * devices * rows * width * 2, transcendentals=0
        ),
        name="hidden_stage",
    )(place, slots, tokens, top, *weights)


def combine_kernel(blocks, capacity, cuts, count, place_ref, slots_ref, *refs):
    lefts, rights = refs[:count], refs[count : 2 * count]
    shared_ref, shared_weight_ref = refs[2 * count : 2 * count + 2]
    outs = refs[2 * count + 2 : -1]
    rows_ref = refs[-1]
    rows = slots_ref.shape[-1]
    total = None
    for left, right in zip(lefts, rights):
        term = jnp.dot(left[...], right[...], preferred_element_type=F32)
        total = term if total is None else total + term
    rows_ref[...] = total.astype(BF16)
    half = blocks // 2
    for side in range(2):
        core = place_ref[1] ^ side
        for block in range(half):
            index = core * half + block
            chosen = one_hot(slots_ref[index], capacity).astype(BF16)
            there = pl.ds(pl.multiple_of(index * capacity, capacity), capacity)
            own = pl.ds(pl.multiple_of(index * rows, rows), rows)
            value = lax.dot_general(
                chosen,
                rows_ref[there, :],
                (((0,), (0,)), ((), ())),
                preferred_element_type=F32,
            ) + jnp.dot(
                shared_ref[own, :], shared_weight_ref[...], preferred_element_type=F32
            )
            value = value.astype(BF16)
            for part in range(3):
                outs[3 * side + part][pl.ds(block * rows, rows), :] = value[
                    :, cuts[part] : cuts[part + 1]
                ]


def combine_stage(place, slots, lefts, rights, shared, shared_weight, capacity):
    devices, _, rows = slots.shape
    blocks = 2 * lax.axis_size("fsdp")
    steps = devices // blocks
    width = rights[0].shape[1]
    cuts = cuts_of(width)
    half = blocks // 2 * rows

    def rows_spec(size, columns):
        return pl.BlockSpec((size, columns), lambda i, *_: (i, 0))

    out_specs = [
        pl.BlockSpec((half, high - low), lambda i, place: (i ^ place[2], 0))
        for _ in range(2)
        for low, high in zip(cuts[:-1], cuts[1:])
    ]
    out_shape = [
        jax.ShapeDtypeStruct((steps * half, high - low), BF16)
        for _ in range(2)
        for low, high in zip(cuts[:-1], cuts[1:])
    ]
    flops = 2 * devices * width * (
        capacity * sum(left.shape[1] for left in lefts) + rows * (capacity + shared.shape[1])
    )
    outs = pl.pallas_call(
        functools.partial(combine_kernel, blocks, capacity, cuts, len(lefts)),
        grid_spec=pltpu.PrefetchScalarGridSpec(
            num_scalar_prefetch=1,
            grid=(steps,),
            in_specs=[
                pl.BlockSpec((blocks, 1, rows), lambda i, *_: (i, 0, 0)),
                *[rows_spec(blocks * capacity, left.shape[1]) for left in lefts],
                *[whole_spec(right) for right in rights],
                rows_spec(blocks * rows, shared.shape[1]),
                whole_spec(shared_weight),
            ],
            out_specs=out_specs,
            scratch_shapes=[pltpu.VMEM((blocks * capacity, width), BF16)],
        ),
        out_shape=out_shape,
        compiler_params=pltpu.CompilerParams(vmem_limit_bytes=VMEM_LIMIT),
        cost_estimate=pl.CostEstimate(
            flops=flops, bytes_accessed=devices * rows * width * 3, transcendentals=0
        ),
        name="combine_stage",
    )(place, slots, *lefts, *rights, shared, shared_weight)
    return outs[:3], outs[3:]


def per_device(
    tokens_in,
    segments,
    routes,
    cotangent,
    g_attn,
    g_kv,
    g_moe,
    w_query,
    w_kv_down,
    w_kv_up,
    w_out,
    w_router,
    w_shared_gate,
    w_shared_up,
    w_shared_down,
    w_expert_gate,
    w_expert_up,
    w_expert_down,
):
    micro_count, rows, width = tokens_in.shape
    seqs, line = lax.axis_size("seq"), lax.axis_size("fsdp")
    devices = seqs * line
    length = rows * seqs
    experts = devices // 2
    picked = routes.shape[2]
    capacity = max(2, rows * picked * 4 // (experts * 3))
    capacity = -(-capacity // 16) * 16
    heads = HEADS // seqs
    me_seq = lax.axis_index("seq")
    me = me_seq * line + lax.axis_index("fsdp")
    expert = me // 2
    factor = (NOPE + ROPE) ** (-0.5)
    frequency = THETA ** (-jnp.arange(ROPE // 2, dtype=F32) * 2.0 / ROPE)
    places = jnp.arange(length)
    angles = places.astype(F32)[:, None] * frequency[None, :]
    own_angles = (me_seq * rows + jnp.arange(rows)).astype(F32)[:, None] * frequency[None, :]
    micros = range(micro_count)

    piece = w_kv_down.shape[0]
    kv_columns = w_kv_down.shape[1]
    small = jnp.concatenate(
        [
            w_kv_down,
            w_router,
            g_attn[:, None],
            g_moe[:, None],
            jnp.pad(g_kv, (0, piece - g_kv.shape[0]))[:, None],
            routes.reshape(piece, -1).astype(BF16),
        ],
        axis=1,
    )
    small = lax.all_gather(small, BOTH, axis=0, tiled=True)
    down_weight = small[:, :kv_columns]
    router_weight = small[:, kv_columns : kv_columns + experts]
    last = kv_columns + experts
    gain_one = small[:, last].astype(F32)
    gain_two = small[:, last + 1].astype(F32)
    gain_latent = small[:, last + 2].reshape(devices, piece)[:, : g_kv.shape[0]].reshape(-1)
    routes_all = small[:, last + 3 :].astype(jnp.int32).reshape((devices,) + routes.shape)
    gain_latent = gain_latent.astype(F32)

    query_width = heads * (NOPE + ROPE)
    out_width = heads * VDIM
    for_query = w_query.reshape(piece, seqs, query_width).transpose(1, 0, 2)
    for_out = w_out.reshape(seqs, out_width, piece).transpose(0, 2, 1)
    for_heads = jnp.concatenate([for_query, for_out], axis=2)
    for_heads = jnp.broadcast_to(
        for_heads[:, None], (seqs, line, piece, query_width + out_width)
    ).reshape(devices, piece, query_width + out_width)
    for_heads = lax.all_to_all(for_heads, BOTH, 0, 0, tiled=True)
    for_heads = for_heads.reshape(width, query_width + out_width)
    query_weight = for_heads[:, :query_width]
    out_weight = for_heads[:, query_width:]
    up_weight = lax.all_to_all(
        jnp.broadcast_to(w_kv_up[None], (line,) + w_kv_up.shape), "fsdp", 0, 0, tiled=True
    )
    up_weight = up_weight.transpose(1, 0, 2).reshape(KVR, -1)

    hidden = w_shared_gate.shape[1] // devices
    for_shared = jnp.concatenate(
        [
            w_shared_gate.reshape(piece, devices, hidden).transpose(1, 0, 2),
            w_shared_up.reshape(piece, devices, hidden).transpose(1, 0, 2),
            w_shared_down.reshape(devices, hidden, piece).transpose(0, 2, 1),
        ],
        axis=2,
    )
    for_shared = lax.all_to_all(for_shared, BOTH, 0, 0, tiled=True).reshape(width, 3 * hidden)
    lanes = -(-(hidden + experts) // 128) * 128

    def padded(parts):
        parts = jnp.concatenate(parts, axis=1)
        return jnp.pad(parts, ((0, 0), (0, lanes - parts.shape[1])))

    shared_gate = for_shared[:, :hidden]
    shared_up = for_shared[:, hidden : 2 * hidden]
    shared_down = padded([for_shared[:, 2 * hidden :]])
    wide_weight = jnp.concatenate(
        [padded([shared_gate, router_weight]), padded([shared_up])], axis=1
    )
    shared_in = jnp.concatenate([padded([shared_gate]), padded([shared_up])], axis=1)
    gate_weight = w_expert_gate[0]
    up_expert = w_expert_up[0]
    down_expert = w_expert_down[0]
    hidden_weights = (wide_weight, shared_down, gate_weight, up_expert, down_expert.T)
    place = jnp.stack([expert, me_seq & 1, me_seq >> 1]).astype(jnp.int32)

    attention = []
    residuals = []
    normed_alls = []
    top_alls = []
    tokens_all = [
        lax.all_gather(tokens_in[micro], "seq", axis=0, tiled=True) for micro in micros
    ]
    for micro in micros:
        unit_one, _ = normed(tokens_all[micro].astype(F32))
        normed_one = (unit_one * gain_one).astype(BF16)
        query_raw = product(normed_one, query_weight).reshape(length, heads, NOPE + ROPE)
        query = jnp.concatenate(
            [query_raw[..., :NOPE], rotate(query_raw[..., NOPE:], angles[:, None, :])], axis=-1
        ).astype(BF16)
        latent = product(normed_one, down_weight)
        unit_latent, _ = normed(latent[:, :KVR])
        latent_norm = (unit_latent * gain_latent).astype(BF16)
        key_rope = rotate(latent[:, KVR:], angles).astype(BF16)
        key_value = product(latent_norm, up_weight).astype(BF16)
        key_heads = key_value.reshape(length, heads, NOPE + VDIM)
        keys = jnp.concatenate(
            [
                key_heads[..., :NOPE],
                jnp.broadcast_to(key_rope[:, None, :], (length, heads, ROPE)),
            ],
            axis=-1,
        )
        values = key_heads[..., NOPE:]
        segment = segments[micro]
        allowed = (segment[:, None] == segment[None, :]) & (places[None, :] <= places[:, None])
        scores = jnp.einsum("qhd,khd->hqk", query, keys, preferred_element_type=F32) * factor
        scores = jnp.where(allowed[None], scores, NEGATIVE)
        largest = jnp.max(scores, axis=-1, keepdims=True)
        powers = jnp.exp(scores - largest)
        total = jnp.sum(powers, axis=-1, keepdims=True)
        log_total = largest + jnp.log(total)
        probs = (powers / total).astype(BF16)
        attended = (
            jnp.einsum("hqk,khd->qhd", probs, values, preferred_element_type=F32)
            .astype(BF16)
            .reshape(length, out_width)
        )
        out_part = right_product(attended, out_weight).astype(BF16)
        summed = lax.psum_scatter(out_part, "seq", scatter_dimension=0, tiled=True)
        residual = tokens_in[micro].astype(F32) + summed.astype(F32)
        unit_two, factor_two = normed(residual)
        normed_two = (unit_two * gain_two).astype(BF16)
        attention.append(
            (normed_one, latent_norm, query, keys, values, allowed, log_total, attended)
        )
        residuals.append((residual, unit_two, factor_two, normed_two))
        top_alls.append(lax.all_gather(cotangent[micro], BOTH, axis=0, tiled=True))
        normed_alls.append(lax.all_gather(normed_two, BOTH, axis=0, tiled=True))

    outputs = []
    grads_two = []
    gate_grads = []
    expert_grads = None
    for micro in micros:
        tokens_two = normed_alls[micro]
        top = top_alls[micro]
        hit = jnp.any(routes_all[:, micro] == expert, axis=-1)
        rank = jnp.cumsum(hit.astype(jnp.int32), axis=1) - 1
        slots = jnp.where(hit, rank, -1)[:, None, :]
        (
            taken,
            taken_top,
            hidden_gated,
            pre_grad,
            up_grad,
            shared_hidden,
            shared_pre_grad,
            gate_grad,
        ) = hidden_stage(
            place, slots, tokens_two, top, hidden_weights, capacity, experts, hidden
        )
        gate_grads.append(
            lax.all_to_all(gate_grad.reshape(devices, rows), BOTH, 0, 0, tiled=True)
        )
        keeps, sends = combine_stage(
            place,
            slots,
            (pre_grad, up_grad),
            (gate_weight.T, up_expert.T),
            shared_pre_grad,
            shared_in.T,
            capacity,
        )
        grads_two.append(reduce_home(keeps, sends, rows))
        keeps, sends = combine_stage(
            place, slots, (hidden_gated,), (down_expert,), shared_hidden, shared_down.T, capacity
        )
        outputs.append(
            (residuals[micro][0] + reduce_home(keeps, sends, rows).astype(F32)).astype(BF16)
        )
        grads = (
            left_product(taken, pre_grad),
            left_product(taken, up_grad),
            left_product(hidden_gated, taken_top),
            left_product(tokens_two, shared_pre_grad),
            left_product(top, shared_hidden),
        )
        expert_grads = (
            grads
            if expert_grads is None
            else tuple(old + new for old, new in zip(expert_grads, grads))
        )

    shared_grads = jnp.concatenate(
        [
            expert_grads[3][:, :hidden],
            expert_grads[3][:, lanes : lanes + hidden],
            expert_grads[4][:, :hidden],
        ],
        axis=1,
    ).astype(BF16)
    shared_grads = lax.all_to_all(
        shared_grads.reshape(devices, piece, 3 * hidden), BOTH, 0, 0, tiled=True
    ).astype(F32)
    grad_shared_gate = shared_grads[:, :, :hidden].transpose(1, 0, 2).reshape(piece, -1)
    grad_shared_up = shared_grads[:, :, hidden : 2 * hidden].transpose(1, 0, 2).reshape(piece, -1)
    grad_shared_down = shared_grads[:, :, 2 * hidden :].transpose(0, 2, 1).reshape(-1, piece)

    grad_gain_one = grad_gain_two = grad_gain_latent = grad_router = 0.0
    grad_heads = grad_up_weight = 0.0
    input_grads = []
    latent_grads = []
    for micro in micros:
        normed_one, latent_norm, query, keys, values, allowed, log_total, attended = attention[
            micro
        ]
        residual, unit_two, factor_two, normed_two = residuals[micro]
        logits = product(normed_two, router_weight)
        shifted = jnp.exp(logits - jnp.max(logits, axis=-1, keepdims=True))
        router = shifted / jnp.sum(shifted, axis=-1, keepdims=True)
        router_in = jnp.sum(gate_grads[micro].reshape(experts, 2, rows), axis=1).T
        grad_logits = (
            router * (router_in - jnp.sum(router * router_in, axis=-1, keepdims=True))
        ).astype(BF16)
        grad_router = grad_router + left_product(normed_two, grad_logits)
        grad_two = grads_two[micro].astype(F32) + right_product(grad_logits, router_weight)
        grad_gain_two = grad_gain_two + jnp.sum(grad_two * unit_two, axis=0)
        grad_residual = cotangent[micro].astype(F32) + norm_back(
            grad_two * gain_two, unit_two, factor_two
        )
        grad_attn_out = lax.all_gather(grad_residual.astype(BF16), "seq", axis=0, tiled=True)

        grad_attended = (
            product(grad_attn_out, out_weight).astype(BF16).reshape(length, heads, VDIM)
        )
        scores = jnp.einsum("qhd,khd->hqk", query, keys, preferred_element_type=F32) * factor
        probs_full = jnp.exp(jnp.where(allowed[None], scores, NEGATIVE) - log_total)
        probs = probs_full.astype(BF16)
        grad_probs = jnp.einsum("qhd,khd->hqk", grad_attended, values, preferred_element_type=F32)
        grad_values = jnp.einsum("hqk,qhd->khd", probs, grad_attended, preferred_element_type=F32)
        grad_scores = (
            probs_full * (grad_probs - jnp.sum(probs_full * grad_probs, axis=-1, keepdims=True))
        ).astype(BF16)
        grad_query = (
            jnp.einsum("hqk,khd->qhd", grad_scores, keys, preferred_element_type=F32) * factor
        )
        grad_keys = (
            jnp.einsum("hqk,qhd->khd", grad_scores, query, preferred_element_type=F32) * factor
        )
        grad_rope = jnp.sum(grad_keys[..., NOPE:], axis=1)
        grad_key_value = (
            jnp.concatenate([grad_keys[..., :NOPE], grad_values], axis=-1)
            .astype(BF16)
            .reshape(length, heads * (NOPE + VDIM))
        )
        grad_query_raw = (
            jnp.concatenate(
                [grad_query[..., :NOPE], rotate(grad_query[..., NOPE:], -angles[:, None, :])],
                axis=-1,
            )
            .astype(BF16)
            .reshape(length, query_width)
        )
        grad_one_part = right_product(grad_query_raw, query_weight)
        grad_latent_part = right_product(grad_key_value, up_weight)
        back = jnp.concatenate([grad_one_part, grad_latent_part, grad_rope], axis=1).astype(BF16)
        back = lax.psum_scatter(back, "seq", scatter_dimension=0, tiled=True).astype(F32)
        grad_heads = grad_heads + jnp.concatenate(
            [left_product(normed_one, grad_query_raw), left_product(grad_attn_out, attended)],
            axis=1,
        )
        grad_up_weight = grad_up_weight + left_product(grad_key_value, latent_norm)

        unit_one, factor_one = normed(tokens_in[micro].astype(F32))
        own_normed = (unit_one * gain_one).astype(BF16)
        latent = product(own_normed, down_weight)
        unit_latent, factor_latent = normed(latent[:, :KVR])
        grad_latent_norm = back[:, width : width + KVR]
        grad_gain_latent = grad_gain_latent + jnp.sum(grad_latent_norm * unit_latent, axis=0)
        grad_compressed = norm_back(grad_latent_norm * gain_latent, unit_latent, factor_latent)
        grad_latent = jnp.concatenate(
            [grad_compressed, rotate(back[:, width + KVR :], -own_angles)], axis=-1
        ).astype(BF16)
        latent_grads.append(grad_latent)
        grad_one = back[:, :width] + right_product(grad_latent, down_weight)
        grad_gain_one = grad_gain_one + jnp.sum(grad_one * unit_one, axis=0)
        input_grads.append(
            grad_residual + norm_back(grad_one * gain_one, unit_one, factor_one)
        )

    latents_all = lax.all_gather(jnp.concatenate(latent_grads, axis=1), "seq", axis=0, tiled=True)
    grad_down = 0.0
    for micro in micros:
        own_columns = lax.dynamic_slice_in_dim(
            attention[micro][0], me_seq * (width // seqs), width // seqs, axis=1
        )
        grad_down = grad_down + left_product(
            own_columns, latents_all[:, micro * kv_columns : (micro + 1) * kv_columns]
        )

    def sum_line(value):
        value = value.astype(BF16).reshape(line, -1, value.shape[-1])
        value = lax.all_to_all(value, "fsdp", 0, 0, tiled=True)
        return jnp.sum(value.astype(F32), axis=0)

    grad_kv_down = sum_line(grad_down)
    grad_kv_up = sum_line(grad_up_weight).T
    grad_heads = lax.all_to_all(
        grad_heads.astype(BF16).reshape(devices, piece, -1), BOTH, 0, 0, tiled=True
    )
    grad_heads = jnp.sum(grad_heads.reshape(seqs, line, piece, -1).astype(F32), axis=1)
    grad_query_weight = grad_heads[:, :, :query_width].transpose(1, 0, 2).reshape(piece, -1)
    grad_out_weight = grad_heads[:, :, query_width:].transpose(0, 2, 1).reshape(-1, piece)
    tiny = jnp.concatenate(
        [
            grad_router.reshape(devices, -1),
            grad_gain_one.reshape(devices, -1),
            grad_gain_two.reshape(devices, -1),
            grad_gain_latent.reshape(devices, -1),
        ],
        axis=1,
    )
    tiny = jnp.sum(lax.all_to_all(tiny, BOTH, 0, 0, tiled=True), axis=0)
    first = piece * experts
    return (
        jnp.stack(outputs),
        jnp.stack(input_grads),
        tiny[first : first + piece],
        tiny[first + 2 * piece :],
        tiny[first + piece : first + 2 * piece],
        grad_query_weight,
        grad_kv_down,
        grad_kv_up,
        grad_out_weight,
        tiny[:first].reshape(piece, experts),
        grad_shared_gate,
        grad_shared_up,
        grad_shared_down,
        expert_grads[0][None],
        expert_grads[1][None],
        expert_grads[2][None],
    )


def solution(mesh):
    return jax.shard_map(
        per_device,
        mesh=mesh,
        in_specs=(
            P("fsdp", "seq", None),
            P("fsdp", None),
            P("fsdp", "seq", None),
            P("fsdp", "seq", None),
            P(BOTH),
            P(BOTH),
            P(BOTH),
            P(BOTH, None),
            P(BOTH, None),
            P(None, BOTH),
            P(None, BOTH),
            P(BOTH, None),
            P(BOTH, None),
            P(BOTH, None),
            P(None, BOTH),
            P(BOTH, None, None),
            P(BOTH, None, None),
            P(BOTH, None, None),
        ),
        out_specs=(
            P("fsdp", "seq", None),
            P("fsdp", "seq", None),
            P(BOTH),
            P(BOTH),
            P(BOTH),
            P(BOTH, None),
            P(BOTH, None),
            P(None, BOTH),
            P(None, BOTH),
            P(BOTH, None),
            P(BOTH, None),
            P(BOTH, None),
            P(None, BOTH),
            P(BOTH, None, None),
            P(BOTH, None, None),
            P(BOTH, None, None),
        ),
        check_vma=False,
    )
```

```python
import functools

import jax
import jax.numpy as jnp
from jax import lax
from jax.experimental import pallas as pl
from jax.experimental.pallas import tpu as pltpu
from jax.sharding import PartitionSpec as P

HEADS = 16
NOPE = 128
ROPE = 64
VDIM = 128
KVR = 512

EPS = 1e-06
THETA = 10000.0
NEGATIVE = -1e30
BOTH = ("seq", "fsdp")
VMEM_LIMIT = 60 * 2**20
F32 = jnp.float32
BF16 = jnp.bfloat16


def product(left, right):
    return jnp.dot(left, right, preferred_element_type=F32)


def left_product(left, right):
    return lax.dot_general(left, right, (((0,), (0,)), ((), ())), preferred_element_type=F32)


def right_product(left, right):
    return lax.dot_general(left, right, (((1,), (1,)), ((), ())), preferred_element_type=F32)


def normed(value):
    factor = lax.rsqrt(jnp.mean(value * value, axis=-1, keepdims=True) + EPS)
    return (value * factor, factor)


def norm_back(grad_unit, unit, factor):
    return factor * (grad_unit - unit * jnp.mean(grad_unit * unit, axis=-1, keepdims=True))


def rotate(value, angles):
    middle = value.shape[-1] // 2
    cosine = jnp.cos(angles)
    sine = jnp.sin(angles)
    first = value[..., :middle]
    second = value[..., middle:]
    return jnp.concatenate(
        [first * cosine - second * sine, second * cosine + first * sine], axis=-1
    )


def silu_parts(value):
    logistic = jax.nn.sigmoid(value)
    return (value * logistic, logistic * (1.0 + value * (1.0 - logistic)))


def add_pair(left, right):
    return (left.astype(F32) + right.astype(F32)).astype(BF16)


def swap(value, bit):
    count = lax.axis_size("seq")
    return lax.ppermute(value, "seq", [(i, i ^ (1 << bit)) for i in range(count)])


def chip_bits():
    return list(range(1, lax.axis_size("seq").bit_length() - 1))


def halves_of(width):
    middle = -(-width // 256) * 128
    return ((0, middle), (middle, width))


class Flow:
    def __init__(self, steps):
        self.steps = steps
        self.value = None
        self.pending = next(steps)

    def arrive(self, arrived):
        try:
            self.pending = self.steps.send(arrived)
        except StopIteration as stop:
            self.pending = None
            self.value = stop.value


class Slots:
    def __init__(self):
        self.token = jnp.zeros((8, 128), F32)

    def tie(self, values):
        return lax.optimization_barrier((values, self.token))[0]

    def run(self, flows, compute=None, *inputs):
        flows = [flow for flow in flows if flow.pending is not None]
        pending = [flow.pending for flow in flows]
        made = compute(*self.tie(inputs)) if compute else ()
        pending, made, self.token = lax.optimization_barrier((pending, made, self.token))
        for flow, arrived in zip(flows, pending):
            flow.arrive(arrived)
        return made

    def finish(self, flow, *others):
        while flow.pending is not None:
            self.run((flow,) + others)
        return flow.value


def stacked(value, names):
    lead = len(names)
    axes = [names.index(bit) for bit in sorted(names, reverse=True)]
    value = value.transpose(axes + list(range(lead, value.ndim)))
    return value.reshape((-1,) + value.shape[lead:])


def spread(parts):
    bits = chip_bits()
    orders = (bits, bits[::-1])
    for step in range(len(bits)):
        arrived = yield [swap(part, order[step]) for part, order in zip(parts, orders)]
        parts = [jnp.stack(pair) for pair in zip(parts, arrived)]
    return [stacked(part, order[::-1]) for part, order in zip(parts, orders)]


def fold(parts, lead):
    bits = chip_bits()
    for step in range(len(bits)):
        kept, sent = [], []
        for part, order in zip(parts, (bits, bits[::-1])):
            names = sorted(order[step:], reverse=True)
            part = part.reshape((2,) * len(names) + part.shape[lead:])
            axis = names.index(order[step])
            kept.append(lax.index_in_dim(part, 0, axis, keepdims=False))
            sent.append(swap(lax.index_in_dim(part, 1, axis, keepdims=False), order[step]))
        arrived = yield sent
        parts = [add_pair(keep, got) for keep, got in zip(kept, arrived)]
        lead = len(bits) - step - 1
    return parts


def gather_seq(own):
    parts = yield from spread([own[:, low:high] for low, high in halves_of(own.shape[1])])
    near = jnp.concatenate(parts, axis=-1)
    (far,) = yield [swap(near, 0)]
    return jnp.concatenate([near, far], axis=0).reshape(-1, own.shape[1])


def scatter_seq(value, rows):
    half = value.shape[0] // 2
    (far,) = yield [swap(value[half:], 0)]
    near = add_pair(value[:half], far).reshape(-1, rows, value.shape[1])
    parts = yield from fold(
        [near[..., low:high] for low, high in halves_of(value.shape[1])], 1
    )
    return jnp.concatenate(parts, axis=-1)


def exchange(value, axes):
    (arrived,) = yield [lax.all_to_all(value, axes, 0, 0, tiled=True)]
    return arrived


def line_reduce(value):
    count = lax.axis_size("fsdp")
    place = lax.axis_index("fsdp")

    def piece(index):
        return lax.dynamic_index_in_dim(value, jnp.clip(index, 0, count - 1), 0, keepdims=False)

    up = down = None
    for step in range(1, count):
        send_up = piece(place + count - step)
        send_down = piece(place - count + step)
        if up is not None:
            send_up = add_pair(send_up, up)
            send_down = add_pair(send_down, down)
        up, down = yield [
            lax.ppermute(send_up, "fsdp", [(i, i + 1) for i in range(step)]),
            lax.ppermute(send_down, "fsdp", [(i, i - 1) for i in range(count - step, count)]),
        ]
    return piece(place).astype(F32) + up.astype(F32) + down.astype(F32)


def reduce_all(keeps, sends, rows):
    arrived = yield [swap(send, 0) for send in sends]
    line = lax.axis_size("fsdp")
    parts = [
        add_pair(keep, got).reshape(-1, line, rows, keep.shape[-1])
        for keep, got in zip(keeps, arrived)
    ]
    parts = yield from fold(parts, 1)
    return (yield from line_reduce(jnp.concatenate(parts, axis=-1)))


def one_hot(slots, capacity):
    rows = slots.shape[-1]
    return lax.broadcasted_iota(jnp.int32, (capacity, rows), 0) == slots


def hidden_kernel(
    blocks,
    capacity,
    experts,
    hidden,
    place_ref,
    slots_ref,
    tokens_ref,
    top_ref,
    wide_ref,
    shared_ref,
    gate_ref,
    up_ref,
    down_ref,
    taken_ref,
    taken_top_ref,
    hidden_ref,
    pre_ref,
    post_ref,
    shared_hidden_ref,
    shared_grad_ref,
    gate_grad_ref,
):
    rows = slots_ref.shape[-1]
    lanes = shared_ref.shape[-1]
    expert = place_ref[0]
    wide = jnp.dot(tokens_ref[...], wide_ref[...], preferred_element_type=F32)
    back = jnp.dot(top_ref[...], shared_ref[...], preferred_element_type=F32)
    first = wide[:, :lanes]
    second = wide[:, lanes:]
    silu, slope = silu_parts(first)
    shared_hidden_ref[...] = (silu * second).astype(BF16)
    shared_grad_ref[:, :lanes] = (back * second * slope).astype(BF16)
    shared_grad_ref[:, lanes:] = (back * silu).astype(BF16)
    lane = lax.broadcasted_iota(jnp.int32, first.shape, 1)
    logits = jnp.where((lane >= hidden) & (lane < hidden + experts), first, NEGATIVE)
    powers = jnp.exp(logits - jnp.max(logits, axis=-1, keepdims=True))
    total = jnp.sum(powers, axis=-1, keepdims=True)
    gates = jnp.sum(jnp.where(lane == hidden + expert, powers, 0.0), axis=-1, keepdims=True)
    gates = jnp.broadcast_to(gates / total, first.shape)
    slot_gates = []
    for block in range(blocks):
        chosen = one_hot(slots_ref[block], capacity)
        low = chosen.astype(BF16)
        own = pl.ds(block * rows, rows)
        there = pl.ds(block * capacity, capacity)
        taken_ref[there, :] = jnp.dot(
            low, tokens_ref[own, :], preferred_element_type=F32
        ).astype(BF16)
        taken_top_ref[there, :] = jnp.dot(
            low, top_ref[own, :], preferred_element_type=F32
        ).astype(BF16)
        slot_gates.append(
            jnp.dot(
                chosen.astype(F32),
                gates[block * rows : (block + 1) * rows],
                precision=lax.Precision.HIGHEST,
                preferred_element_type=F32,
            )[:, :1]
        )
    slot_gates = jnp.concatenate(slot_gates, axis=0)
    gate_pre = jnp.dot(taken_ref[...], gate_ref[...], preferred_element_type=F32)
    up_pre = jnp.dot(taken_ref[...], up_ref[...], preferred_element_type=F32)
    grad = jnp.dot(taken_top_ref[...], down_ref[...], preferred_element_type=F32)
    swish, slope = silu_parts(gate_pre)
    made = swish * up_pre
    hidden_ref[...] = (made * slot_gates).astype(BF16)
    slot_grads = jnp.sum(made * grad, axis=-1, keepdims=True)
    grad = grad * slot_gates
    pre_ref[...] = (grad * up_pre * slope).astype(BF16)
    post_ref[...] = (grad * swish).astype(BF16)
    for block in range(blocks):
        chosen = one_hot(slots_ref[block], capacity)
        gate_grad_ref[block] = jnp.sum(
            jnp.where(chosen, slot_grads[block * capacity : (block + 1) * capacity], 0.0),
            axis=0,
            keepdims=True,
        )


def scores_of(qn_ref, qr_ref, kv_ref, kr_ref, seg_q, seg_k, pos_q, pos_k, head, factor):
    lane = lax.broadcasted_iota(jnp.int32, qr_ref.shape, 1)
    turned = jnp.where(lane // ROPE == head, qr_ref[...], jnp.zeros((), BF16))
    query = jnp.concatenate([qn_ref[...], turned], axis=1)
    keys = jnp.concatenate([kv_ref[:, :NOPE], kr_ref[...]], axis=1)
    scores = lax.dot_general(
        query, keys, (((1,), (1,)), ((), ())), preferred_element_type=F32
    )
    allowed = (seg_q[...] == seg_k[...]) & (pos_k[...] <= pos_q[...])
    scores = jnp.where(allowed, scores * factor, NEGATIVE)
    powers = jnp.exp(scores - jnp.max(scores, axis=-1, keepdims=True))
    return query, keys, powers / jnp.sum(powers, axis=-1, keepdims=True)


def attend_kernel(
    factor, qn_ref, qr_ref, kv_ref, kr_ref, seg_q, seg_k, pos_q, pos_k, out_ref
):
    _, _, probs = scores_of(
        qn_ref, qr_ref, kv_ref, kr_ref, seg_q, seg_k, pos_q, pos_k, pl.program_id(1), factor
    )
    out_ref[...] = jnp.dot(
        probs.astype(BF16), kv_ref[:, NOPE:], preferred_element_type=F32
    ).astype(BF16)


def attend_back_kernel(
    factor,
    qn_ref,
    qr_ref,
    kv_ref,
    kr_ref,
    seg_q,
    seg_k,
    pos_q,
    pos_k,
    top_ref,
    grad_qn_ref,
    grad_qr_ref,
    grad_kv_ref,
    grad_kr_ref,
    sum_ref,
):
    step, head = pl.program_id(0), pl.program_id(1)
    last = pl.num_programs(0) - 1
    query, keys, probs = scores_of(
        qn_ref, qr_ref, kv_ref, kr_ref, seg_q, seg_k, pos_q, pos_k, head, factor
    )
    top = top_ref[...]
    grad_probs = lax.dot_general(
        top, kv_ref[:, NOPE:], (((1,), (1,)), ((), ())), preferred_element_type=F32
    )
    mean = jnp.sum(probs * grad_probs, axis=-1, keepdims=True)
    grad_scores = (probs * (grad_probs - mean)).astype(BF16)
    low = probs.astype(BF16)
    grad_query = jnp.dot(grad_scores, keys, preferred_element_type=F32) * factor
    grad_qn_ref[...] = grad_query[:, :NOPE].astype(BF16)
    turned = grad_query[:, NOPE:]
    lane = lax.broadcasted_iota(jnp.int32, turned.shape, 1)
    turned = jnp.where(lane // ROPE == head, turned, 0.0)
    grad_keys = left_product(grad_scores, query) * factor
    grad_values = left_product(low, top)

    @pl.when(head == 0)
    def _():
        grad_qr_ref[...] = turned

    @pl.when(head != 0)
    def _():
        grad_qr_ref[...] += turned

    @pl.when((step == 0) & (head == 0))
    def _():
        grad_kr_ref[...] = grad_keys[:, NOPE:]

    @pl.when((step != 0) | (head != 0))
    def _():
        grad_kr_ref[...] += grad_keys[:, NOPE:]

    @pl.when(step == 0)
    def _():
        sum_ref[head, :, :NOPE] = grad_keys[:, :NOPE]
        sum_ref[head, :, NOPE:] = grad_values

    @pl.when(step != 0)
    def _():
        sum_ref[head, :, :NOPE] += grad_keys[:, :NOPE]
        sum_ref[head, :, NOPE:] += grad_values

    @pl.when(step == last)
    def _():
        grad_kv_ref[head] = sum_ref[head].astype(BF16)


def attend_specs(length, heads, turned, block):
    return [
        pl.BlockSpec((block, NOPE), lambda i, h: (i, h)),
        pl.BlockSpec((block, turned), lambda i, h: (i, 0)),
        pl.BlockSpec((length, NOPE + VDIM), lambda i, h: (0, h)),
        pl.BlockSpec((length, turned), lambda i, h: (0, 0)),
        pl.BlockSpec((block, 1), lambda i, h: (i, 0)),
        pl.BlockSpec((1, length), lambda i, h: (0, 0)),
        pl.BlockSpec((block, 1), lambda i, h: (i, 0)),
        pl.BlockSpec((1, length), lambda i, h: (0, 0)),
    ]


def attend_stage(factor, heads, inputs):
    length, turned = inputs[1].shape
    block = min(length, 256)
    return pl.pallas_call(
        functools.partial(attend_kernel, factor),
        grid=(length // block, heads),
        in_specs=attend_specs(length, heads, turned, block),
        out_specs=pl.BlockSpec((block, VDIM), lambda i, h: (i, h)),
        out_shape=jax.ShapeDtypeStruct((length, heads * VDIM), BF16),
        compiler_params=pltpu.CompilerParams(vmem_limit_bytes=VMEM_LIMIT),
        cost_estimate=pl.CostEstimate(
            flops=2 * heads * length * length * 384,
            bytes_accessed=8 * length * heads * NOPE,
            transcendentals=heads * length * length,
        ),
        name="attend_stage",
    )(*inputs)


def attend_back_stage(factor, heads, inputs, top):
    length, turned = inputs[1].shape
    block = min(length, 256)
    return pl.pallas_call(
        functools.partial(attend_back_kernel, factor),
        grid=(length // block, heads),
        in_specs=attend_specs(length, heads, turned, block)
        + [pl.BlockSpec((block, VDIM), lambda i, h: (i, h))],
        out_specs=[
            pl.BlockSpec((block, NOPE), lambda i, h: (i, h)),
            pl.BlockSpec((block, turned), lambda i, h: (i, 0)),
            pl.BlockSpec((heads, length, NOPE + VDIM), lambda i, h: (0, 0, 0)),
            pl.BlockSpec((length, turned), lambda i, h: (0, 0)),
        ],
        out_shape=[
            jax.ShapeDtypeStruct((length, heads * NOPE), BF16),
            jax.ShapeDtypeStruct((length, turned), F32),
            jax.ShapeDtypeStruct((heads, length, NOPE + VDIM), BF16),
            jax.ShapeDtypeStruct((length, turned), F32),
        ],
        scratch_shapes=[pltpu.VMEM((heads, length, NOPE + VDIM), F32)],
        compiler_params=pltpu.CompilerParams(vmem_limit_bytes=VMEM_LIMIT),
        cost_estimate=pl.CostEstimate(
            flops=2 * heads * length * length * 1024,
            bytes_accessed=16 * length * heads * NOPE,
            transcendentals=heads * length * length,
        ),
        name="attend_back_stage",
    )(*inputs, top)


def whole_spec(array):
    return pl.BlockSpec(
        array.shape, lambda i, *_: (0,) * array.ndim, pipeline_mode=pl.Buffered(1)
    )


def hidden_stage(place, slots, tokens, top, weights, capacity, experts, hidden):
    wide_weight, shared_down, gate_weight, up_weight, down_weight = weights
    devices, _, rows = slots.shape
    blocks = 2 * lax.axis_size("fsdp")
    steps = devices // blocks
    width = tokens.shape[1]
    half = gate_weight.shape[1]
    lanes = shared_down.shape[1]
    count = blocks * capacity

    def rows_spec(size, columns):
        return pl.BlockSpec((size, columns), lambda i, *_: (i, 0))

    slots_spec = pl.BlockSpec((blocks, 1, rows), lambda i, *_: (i, 0, 0))
    flops = devices * 2 * (3 * capacity * width * half + rows * width * 3 * lanes)
    return pl.pallas_call(
        functools.partial(hidden_kernel, blocks, capacity, experts, hidden),
        grid_spec=pltpu.PrefetchScalarGridSpec(
            num_scalar_prefetch=1,
            grid=(steps,),
            in_specs=[
                slots_spec,
                rows_spec(blocks * rows, width),
                rows_spec(blocks * rows, width),
                *[whole_spec(weight) for weight in weights],
            ],
            out_specs=[
                rows_spec(count, width),
                rows_spec(count, width),
                rows_spec(count, half),
                rows_spec(count, half),
                rows_spec(count, half),
                rows_spec(blocks * rows, lanes),
                rows_spec(blocks * rows, 2 * lanes),
                slots_spec,
            ],
        ),
        out_shape=[
            jax.ShapeDtypeStruct((steps * count, width), BF16),
            jax.ShapeDtypeStruct((steps * count, width), BF16),
            jax.ShapeDtypeStruct((steps * count, half), BF16),
            jax.ShapeDtypeStruct((steps * count, half), BF16),
            jax.ShapeDtypeStruct((steps * count, half), BF16),
            jax.ShapeDtypeStruct((devices * rows, lanes), BF16),
            jax.ShapeDtypeStruct((devices * rows, 2 * lanes), BF16),
            jax.ShapeDtypeStruct(slots.shape, F32),
        ],
        compiler_params=pltpu.CompilerParams(vmem_limit_bytes=VMEM_LIMIT),
        cost_estimate=pl.CostEstimate(
            flops=flops, bytes_accessed=3 * devices * rows * width * 2, transcendentals=0
        ),
        name="hidden_stage",
    )(place, slots, tokens, top, *weights)


def combine_kernel(blocks, capacity, cuts, count, place_ref, slots_ref, *refs):
    lefts, rights = refs[:count], refs[count : 2 * count]
    shared_ref, shared_weight_ref = refs[2 * count : 2 * count + 2]
    outs = refs[2 * count + 2 : -1]
    rows_ref = refs[-1]
    rows = slots_ref.shape[-1]
    total = None
    for left, right in zip(lefts, rights):
        term = jnp.dot(left[...], right[...], preferred_element_type=F32)
        total = term if total is None else total + term
    rows_ref[...] = total.astype(BF16)
    half = blocks // 2
    for side in range(2):
        core = place_ref[1] ^ side
        for block in range(half):
            index = core * half + block
            chosen = one_hot(slots_ref[index], capacity).astype(BF16)
            there = pl.ds(pl.multiple_of(index * capacity, capacity), capacity)
            own = pl.ds(pl.multiple_of(index * rows, rows), rows)
            value = lax.dot_general(
                chosen,
                rows_ref[there, :],
                (((0,), (0,)), ((), ())),
                preferred_element_type=F32,
            ) + jnp.dot(
                shared_ref[own, :], shared_weight_ref[...], preferred_element_type=F32
            )
            value = value.astype(BF16)
            for part, (low, high) in enumerate(cuts):
                outs[2 * side + part][pl.ds(block * rows, rows), :] = value[:, low:high]


def combine_stage(place, slots, lefts, rights, shared, shared_weight, capacity):
    devices, _, rows = slots.shape
    blocks = 2 * lax.axis_size("fsdp")
    steps = devices // blocks
    width = rights[0].shape[1]
    cuts = halves_of(width)
    half = blocks // 2 * rows

    def rows_spec(size, columns):
        return pl.BlockSpec((size, columns), lambda i, *_: (i, 0))

    out_specs = [
        pl.BlockSpec((half, high - low), lambda i, place: (i ^ place[2], 0))
        for _ in range(2)
        for low, high in cuts
    ]
    out_shape = [
        jax.ShapeDtypeStruct((steps * half, high - low), BF16)
        for _ in range(2)
        for low, high in cuts
    ]
    flops = 2 * devices * width * (
        capacity * sum(left.shape[1] for left in lefts) + rows * (capacity + shared.shape[1])
    )
    outs = pl.pallas_call(
        functools.partial(combine_kernel, blocks, capacity, cuts, len(lefts)),
        grid_spec=pltpu.PrefetchScalarGridSpec(
            num_scalar_prefetch=1,
            grid=(steps,),
            in_specs=[
                pl.BlockSpec((blocks, 1, rows), lambda i, *_: (i, 0, 0)),
                *[rows_spec(blocks * capacity, left.shape[1]) for left in lefts],
                *[whole_spec(right) for right in rights],
                rows_spec(blocks * rows, shared.shape[1]),
                whole_spec(shared_weight),
            ],
            out_specs=out_specs,
            scratch_shapes=[pltpu.VMEM((blocks * capacity, width), BF16)],
        ),
        out_shape=out_shape,
        compiler_params=pltpu.CompilerParams(vmem_limit_bytes=VMEM_LIMIT),
        cost_estimate=pl.CostEstimate(
            flops=flops, bytes_accessed=devices * rows * width * 3, transcendentals=0
        ),
        name="combine_stage",
    )(place, slots, *lefts, *rights, shared, shared_weight)
    return outs[:2], outs[2:]


def per_device(
    tokens_in,
    segments,
    routes,
    cotangent,
    g_attn,
    g_kv,
    g_moe,
    w_query,
    w_kv_down,
    w_kv_up,
    w_out,
    w_router,
    w_shared_gate,
    w_shared_up,
    w_shared_down,
    w_expert_gate,
    w_expert_up,
    w_expert_down,
):
    micro_count, rows, width = tokens_in.shape
    seqs, line = lax.axis_size("seq"), lax.axis_size("fsdp")
    devices = seqs * line
    length = rows * seqs
    experts = devices // 2
    picked = routes.shape[2]
    capacity = max(2, rows * picked * 4 // (experts * 3))
    capacity = -(-capacity // 16) * 16
    heads = HEADS // seqs
    me_seq = lax.axis_index("seq")
    me = me_seq * line + lax.axis_index("fsdp")
    expert = me // 2
    factor = (NOPE + ROPE) ** (-0.5)
    frequency = THETA ** (-jnp.arange(ROPE // 2, dtype=F32) * 2.0 / ROPE)
    order = jnp.arange(seqs)
    ranks = (order ^ me_seq) >> 1 | ((order ^ me_seq) & 1) * (seqs // 2)
    order = me_seq ^ ((order % (seqs // 2)) * 2 + order // (seqs // 2))

    def to_relative(value):
        return value.reshape(seqs, rows, -1)[order].reshape(value.shape)

    def to_absolute(value):
        return value.reshape(seqs, rows, -1)[ranks].reshape(value.shape)

    places = (order[:, None] * rows + jnp.arange(rows)[None, :]).reshape(-1)
    angles = places.astype(F32)[:, None] * frequency[None, :]
    own_angles = angles[:rows]
    micros = range(micro_count)

    slots = Slots()
    place = jnp.stack([expert, me_seq & 1, me_seq >> 1]).astype(jnp.int32)
    tokens = [Flow(gather_seq(tokens_in[micro])) for micro in micros]

    piece = w_kv_down.shape[0]
    kv_columns = w_kv_down.shape[1]
    small = jnp.concatenate(
        [
            w_kv_down,
            w_router,
            g_attn[:, None],
            g_moe[:, None],
            jnp.pad(g_kv, (0, piece - g_kv.shape[0]))[:, None],
            routes.reshape(piece, -1).astype(BF16),
        ],
        axis=1,
    )
    small = lax.all_gather(small, BOTH, axis=0, tiled=True)

    query_width = heads * (NOPE + ROPE)
    out_width = heads * VDIM
    for_query = w_query.reshape(piece, seqs, heads, NOPE + ROPE)
    for_query = jnp.concatenate(
        [
            for_query[..., :NOPE].reshape(piece, seqs, -1),
            for_query[..., NOPE:].reshape(piece, seqs, -1),
        ],
        axis=2,
    ).transpose(1, 0, 2)
    for_out = w_out.reshape(seqs, out_width, piece).transpose(0, 2, 1)
    for_heads = jnp.concatenate([for_query, for_out], axis=2)
    for_heads = jnp.broadcast_to(
        for_heads[:, None], (seqs, line, piece, query_width + out_width)
    ).reshape(devices, piece, query_width + out_width)
    for_heads = lax.all_to_all(for_heads, BOTH, 0, 0, tiled=True)
    up_weight = lax.all_to_all(
        jnp.broadcast_to(w_kv_up[None], (line,) + w_kv_up.shape), "fsdp", 0, 0, tiled=True
    )
    hidden = w_shared_gate.shape[1] // devices
    for_shared = jnp.concatenate(
        [
            w_shared_gate.reshape(piece, devices, hidden).transpose(1, 0, 2),
            w_shared_up.reshape(piece, devices, hidden).transpose(1, 0, 2),
            w_shared_down.reshape(devices, hidden, piece).transpose(0, 2, 1),
        ],
        axis=2,
    )
    for_shared = Flow(exchange(for_shared, BOTH))
    slots.finish(tokens[0], tokens[1])
    slots.finish(tokens[1])
    small, for_heads, up_weight = slots.run([], lambda *given: given, small, for_heads, up_weight)
    tops = [lax.all_gather(slots.tie(cotangent[0]), BOTH, axis=0, tiled=True), None]
    for_heads = for_heads.reshape(width, query_width + out_width)
    query_weight = for_heads[:, :query_width]
    out_weight = for_heads[:, query_width:]
    up_weight = up_weight.transpose(1, 0, 2).reshape(KVR, -1)
    down_weight = small[:, :kv_columns]
    router_weight = small[:, kv_columns : kv_columns + experts]
    last = kv_columns + experts
    gain_one = small[:, last].astype(F32)
    gain_two = small[:, last + 1].astype(F32)
    gain_latent = small[:, last + 2].reshape(devices, piece)[:, : g_kv.shape[0]].reshape(-1)
    routes_all = small[:, last + 3 :].astype(jnp.int32).reshape((devices,) + routes.shape)
    gain_latent = gain_latent.astype(F32)

    def projections(tokens):
        unit_one, _ = normed(tokens.astype(F32))
        normed_one = (unit_one * gain_one).astype(BF16)
        query_raw = product(normed_one, query_weight)
        query = query_raw[:, : heads * NOPE].astype(BF16)
        turned = query_raw[:, heads * NOPE :].reshape(length, heads, ROPE)
        turned = turned_lanes(rotate(turned, angles[:, None, :]).reshape(length, -1))
        latent = product(normed_one, down_weight)
        unit_latent, factor_latent = normed(latent[:, :KVR])
        latent_norm = (unit_latent * gain_latent).astype(BF16)
        key_rope = rotate(latent[:, KVR:], angles).astype(BF16)
        key_value = product(latent_norm, up_weight).astype(BF16)
        key_rope = turned_lanes(jnp.tile(key_rope, (1, heads)))
        return (
            normed_one,
            latent_norm,
            (query, turned, key_value, key_rope),
            unit_latent[:rows],
            factor_latent[:rows],
        )

    def turned_lanes(value):
        return jnp.pad(value.astype(BF16), ((0, 0), (0, -value.shape[1] % 128)))

    def marks_of(micro):
        segment = segments[micro].reshape(seqs, rows)[order].reshape(-1)
        return segment[:, None], segment[None, :], places[:, None], places[None, :]

    def attend(projected, marks):
        attended = attend_stage(factor, heads, projected[2] + marks)
        return attended, right_product(attended, out_weight).astype(BF16)

    def home_forward(micro, summed):
        residual = tokens_in[micro].astype(F32) + summed.astype(F32)
        unit_two, factor_two = normed(residual)
        normed_two = (unit_two * gain_two).astype(BF16)
        return residual, unit_two, factor_two, normed_two

    marks = [marks_of(micro) for micro in micros]
    projected = [None, None]
    attended = [None, None]
    residuals = [None, None]
    normed_alls = [None, None]
    projected[0] = slots.run([], projections, tokens[0].value)
    attended[0] = slots.run([], attend, projected[0], marks[0])
    summed = Flow(scatter_seq(attended[0][1], rows))
    projected[1] = slots.run([summed, for_shared], projections, tokens[1].value)
    attended[1] = slots.run([summed], attend, projected[1], marks[1])
    summed_two = Flow(scatter_seq(attended[1][1], rows))
    slots.finish(summed, summed_two)
    residuals[0] = home_forward(0, summed.value)
    normed_alls[0] = lax.all_gather(residuals[0][3], BOTH, axis=0, tiled=True)
    slots.finish(summed_two)
    residuals[1] = home_forward(1, summed_two.value)
    normed_alls[1] = lax.all_gather(residuals[1][3], BOTH, axis=0, tiled=True)
    later, _ = lax.optimization_barrier((cotangent[1], residuals[1][3]))
    tops[1] = lax.all_gather(later, BOTH, axis=0, tiled=True)

    lanes = -(-(hidden + experts) // 128) * 128

    def padded(parts):
        parts = jnp.concatenate(parts, axis=1)
        return jnp.pad(parts, ((0, 0), (0, lanes - parts.shape[1])))

    for_shared = for_shared.value.reshape(width, 3 * hidden)
    shared_gate = for_shared[:, :hidden]
    shared_up = for_shared[:, hidden : 2 * hidden]
    shared_down = padded([for_shared[:, 2 * hidden :]])
    wide_weight = jnp.concatenate(
        [padded([shared_gate, router_weight]), padded([shared_up])], axis=1
    )
    shared_in = jnp.concatenate([padded([shared_gate]), padded([shared_up])], axis=1)
    gate_weight = w_expert_gate[0]
    up_expert = w_expert_up[0]
    down_expert = w_expert_down[0]
    hidden_weights = (wide_weight, shared_down, gate_weight, up_expert, down_expert.T)
    transposed = (gate_weight.T, up_expert.T, shared_in.T, shared_down.T)

    def slots_of(micro):
        hit = jnp.any(routes_all[:, micro] == expert, axis=-1)
        rank = jnp.cumsum(hit.astype(jnp.int32), axis=1) - 1
        return jnp.where(hit, rank, -1)[:, None, :]

    def hidden_of(seats, tokens, top):
        return hidden_stage(
            place, seats, tokens, top, hidden_weights, capacity, experts, hidden
        )

    def grads_to_tokens(seats, made):
        return combine_stage(
            place, seats, made[3:5], transposed[:2], made[6], transposed[2], capacity
        )

    def outputs_to_tokens(seats, made):
        return combine_stage(
            place, seats, made[2:3], (down_expert,), made[5], transposed[3], capacity
        )

    def routed_grads(made):
        taken, taken_top, hidden_gated, pre_grad, up_grad, _, _, _ = made
        return (
            left_product(taken, pre_grad),
            left_product(taken, up_grad),
            left_product(hidden_gated, taken_top),
        )

    def shared_grads_of(tokens, top, made):
        return left_product(tokens, made[6]), left_product(top, made[5])

    def added(function):
        def call(before, *values):
            return tuple(old + new for old, new in zip(before, function(*values)))

        return call

    def gate_grads_home(made):
        return Flow(exchange(made[-1].reshape(devices, rows), BOTH))

    def home_backward(micro, grad_two, gate_grad):
        _, unit_two, factor_two, normed_two = residuals[micro]
        logits = product(normed_two, router_weight)
        shifted = jnp.exp(logits - jnp.max(logits, axis=-1, keepdims=True))
        router = shifted / jnp.sum(shifted, axis=-1, keepdims=True)
        router_in = jnp.sum(gate_grad.reshape(experts, 2, rows), axis=1).T
        grad_logits = (
            router * (router_in - jnp.sum(router * router_in, axis=-1, keepdims=True))
        ).astype(BF16)
        grad_two = grad_two + right_product(grad_logits, router_weight)
        grad_residual = cotangent[micro].astype(F32) + norm_back(
            grad_two * gain_two, unit_two, factor_two
        )
        return (
            grad_residual,
            left_product(normed_two, grad_logits),
            jnp.sum(grad_two * unit_two, axis=0),
        )

    def attend_backward(grad_attn_out, projected, marks):
        grad_attended = to_relative(product(grad_attn_out, out_weight).astype(BF16))
        return attend_back_stage(factor, heads, projected[2] + marks, grad_attended)

    def projections_backward(grad_query, grad_turned, grad_key_value, grad_rope):
        grad_turned = grad_turned[:, : heads * ROPE].reshape(length, heads, ROPE)
        grad_turned = rotate(grad_turned, -angles[:, None, :]).reshape(length, -1)
        grad_query_raw = jnp.concatenate([grad_query, grad_turned.astype(BF16)], axis=1)
        grad_rope = jnp.sum(grad_rope[:, : heads * ROPE].reshape(length, heads, ROPE), axis=1)
        grad_key_value = grad_key_value.transpose(1, 0, 2).reshape(length, -1)
        grad_one_part = right_product(grad_query_raw, query_weight)
        grad_latent_part = right_product(grad_key_value, up_weight)
        back = jnp.concatenate([grad_one_part, grad_latent_part, grad_rope], axis=1)
        return back.astype(BF16), grad_query_raw, grad_key_value

    def head_grads(projected, attended, grad_attn_out, grad_query_raw, grad_key_value):
        return (
            left_product(projected[0], grad_query_raw),
            left_product(grad_attn_out, to_absolute(attended)),
            left_product(grad_key_value, projected[1]),
        )

    def latent_backward(back, projected):
        unit_latent, factor_latent = projected[3:]
        grad_latent_norm = back[:, width : width + KVR].astype(F32)
        grad_compressed = norm_back(grad_latent_norm * gain_latent, unit_latent, factor_latent)
        grad_latent = jnp.concatenate(
            [grad_compressed, rotate(back[:, width + KVR :].astype(F32), -own_angles)], axis=-1
        ).astype(BF16)
        return grad_latent, jnp.sum(grad_latent_norm * unit_latent, axis=0)

    def input_backward(micro, back, grad_latent, grad_residual):
        unit_one, factor_one = normed(tokens_in[micro].astype(F32))
        grad_one = back[:, :width].astype(F32) + right_product(grad_latent, down_weight)
        return (
            grad_residual + norm_back(grad_one * gain_one, unit_one, factor_one),
            jnp.sum(grad_one * unit_one, axis=0),
        )

    def line_blocks(value):
        return value.astype(BF16).reshape(line, -1, value.shape[-1])

    def down_grads(normed_one, latents):
        columns = lax.dynamic_slice_in_dim(
            normed_one, me_seq * (width // seqs), width // seqs, axis=1
        )
        return left_product(columns, latents)

    seats = [slots_of(micro) for micro in micros]
    made = [None, None]
    def home_and_out(micro):
        home = home_backward(micro, grads[micro].value, gate_grad[micro].value)
        return home, lax.all_gather(home[0].astype(BF16), "seq", axis=0, tiled=True)

    def attention_back(*given):
        return projections_backward(*attend_backward(*given))

    gate_grad = [None, None]
    grads = [None, None]
    sums = [None, None]
    homes = [None, None]
    attn_out = [None, None]
    backs = [None, None]
    back_sums = [None, None]
    latents = [None, None]
    latent_flows = [None, None]
    made[0] = slots.run([], hidden_of, seats[0], normed_alls[0], tops[0])
    gate_grad[0] = gate_grads_home(made[0])
    sides = slots.run([gate_grad[0]], grads_to_tokens, seats[0], made[0])
    grads[0] = Flow(reduce_all(*sides, rows))
    sides = slots.run([grads[0]], outputs_to_tokens, seats[0], made[0])
    sums[0] = Flow(reduce_all(*sides, rows))
    routed = slots.run([grads[0]], routed_grads, made[0])
    shared = slots.run([grads[0], sums[0]], shared_grads_of, normed_alls[0], tops[0], made[0])
    slots.run([grads[0]])
    slots.run([grads[0]])
    made[1] = slots.run([grads[0], sums[0]], hidden_of, seats[1], normed_alls[1], tops[1])
    slots.finish(grads[0])
    homes[0], attn_out[0] = home_and_out(0)
    gate_grad[1] = gate_grads_home(made[1])
    sides = slots.run([gate_grad[1], sums[0]], grads_to_tokens, seats[1], made[1])
    grads[1] = Flow(reduce_all(*sides, rows))
    sides = slots.run([grads[1], sums[0]], outputs_to_tokens, seats[1], made[1])
    sums[1] = Flow(reduce_all(*sides, rows))
    backs[0] = slots.run([grads[1]], attention_back, attn_out[0], projected[0], marks[0])
    back_sums[0] = Flow(scatter_seq(backs[0][0], rows))
    head_sums = slots.run(
        [grads[1], back_sums[0]],
        head_grads,
        projected[0],
        attended[0][0],
        attn_out[0],
        *backs[0][1:],
    )
    taken, taken_top, hidden_gated, pre_grad, up_grad, _, _, _ = made[1]
    parts = []
    for pair in ((taken, pre_grad), (taken, up_grad), (hidden_gated, taken_top)):
        parts.append(
            slots.run(
                [grads[1], back_sums[0], sums[0]],
                lambda old, left, right: old + left_product(left, right),
                routed[len(parts)],
                *pair,
            )
        )
    slots.finish(grads[1], back_sums[0])
    homes[1], attn_out[1] = home_and_out(1)
    slots.finish(back_sums[0])
    latents[0] = latent_backward(back_sums[0].value, projected[0])
    latent_flows[0] = Flow(gather_seq(latents[0][0]))
    slots.run([sums[1], sums[0], latent_flows[0]])
    shared = slots.run(
        [sums[1], latent_flows[0]],
        added(shared_grads_of),
        shared,
        normed_alls[1],
        tops[1],
        made[1],
    )
    shared = jnp.concatenate(
        [shared[0][:, :hidden], shared[0][:, lanes : lanes + hidden], shared[1][:, :hidden]],
        axis=1,
    )
    shared = Flow(exchange(shared.astype(BF16).reshape(devices, piece, 3 * hidden), BOTH))
    backs[1] = slots.run(
        [sums[1], latent_flows[0], shared], attention_back, attn_out[1], projected[1], marks[1]
    )
    back_sums[1] = Flow(scatter_seq(backs[1][0], rows))
    head_sums = slots.run(
        [back_sums[1], sums[1], sums[0]],
        added(head_grads),
        head_sums,
        projected[1],
        attended[1][0],
        attn_out[1],
        *backs[1][1:],
    )
    grad_heads = jnp.concatenate(head_sums[:2], axis=1).astype(BF16)
    grad_heads = Flow(exchange(grad_heads.reshape(devices, piece, -1), BOTH))
    grad_up = Flow(exchange(line_blocks(head_sums[2]), "fsdp"))
    slots.run([back_sums[1], sums[1], sums[0], grad_up])
    slots.finish(back_sums[1], sums[1], sums[0])
    latents[1] = latent_backward(back_sums[1].value, projected[1])
    latent_flows[1] = Flow(gather_seq(latents[1][0]))
    finals = [
        input_backward(micro, back_sums[micro].value, latents[micro][0], homes[micro][0])
        for micro in micros
    ]
    tiny = jnp.concatenate(
        [
            sum(home[1] for home in homes).reshape(devices, -1),
            sum(final[1] for final in finals).reshape(devices, -1),
            sum(home[2] for home in homes).reshape(devices, -1),
            sum(latent[1] for latent in latents).reshape(devices, -1),
        ],
        axis=1,
    )
    tiny = Flow(exchange(tiny, BOTH))
    slots.run([latent_flows[1], sums[1], sums[0]])
    slots.run([latent_flows[1], sums[1], sums[0], tiny])
    slots.finish(latent_flows[1], grad_heads)
    for flow in (sums[0], sums[1], latent_flows[0], tiny, grad_heads, shared, grad_up):
        slots.finish(flow)
    outputs = [
        (residuals[micro][0] + sums[micro].value).astype(BF16) for micro in micros
    ]
    grad_kv_down = sum(
        down_grads(projected[micro][0], latent_flows[micro].value) for micro in micros
    )
    grad_kv_down = lax.all_to_all(line_blocks(grad_kv_down), "fsdp", 0, 0, tiled=True)
    grad_kv_down = jnp.sum(grad_kv_down.astype(F32), axis=0)
    grad_kv_up = jnp.sum(grad_up.value.astype(F32), axis=0).T
    shared_grads = shared.value.astype(F32)
    grad_shared_gate = shared_grads[:, :, :hidden].transpose(1, 0, 2).reshape(piece, -1)
    grad_shared_up = shared_grads[:, :, hidden : 2 * hidden].transpose(1, 0, 2).reshape(piece, -1)
    grad_shared_down = shared_grads[:, :, 2 * hidden :].transpose(0, 2, 1).reshape(-1, piece)
    grad_heads = grad_heads.value.reshape(seqs, line, piece, -1)
    grad_heads = jnp.sum(grad_heads.astype(F32), axis=1)
    grad_query_weight = jnp.concatenate(
        [
            grad_heads[:, :, : heads * NOPE].reshape(seqs, piece, heads, NOPE),
            grad_heads[:, :, heads * NOPE : query_width].reshape(seqs, piece, heads, ROPE),
        ],
        axis=3,
    )
    grad_query_weight = grad_query_weight.transpose(1, 0, 2, 3).reshape(piece, -1)
    grad_out_weight = grad_heads[:, :, query_width:].transpose(0, 2, 1).reshape(-1, piece)
    tiny = jnp.sum(tiny.value, axis=0)
    first = piece * experts
    return (
        jnp.stack(outputs),
        jnp.stack([final[0] for final in finals]),
        tiny[first : first + piece],
        tiny[first + 2 * piece :],
        tiny[first + piece : first + 2 * piece],
        grad_query_weight,
        grad_kv_down,
        grad_kv_up,
        grad_out_weight,
        tiny[:first].reshape(piece, experts),
        grad_shared_gate,
        grad_shared_up,
        grad_shared_down,
        parts[0][None],
        parts[1][None],
        parts[2][None],
    )


def solution(mesh):
    return jax.shard_map(
        per_device,
        mesh=mesh,
        in_specs=(
            P("fsdp", "seq", None),
            P("fsdp", None),
            P("fsdp", "seq", None),
            P("fsdp", "seq", None),
            P(BOTH),
            P(BOTH),
            P(BOTH),
            P(BOTH, None),
            P(BOTH, None),
            P(None, BOTH),
            P(None, BOTH),
            P(BOTH, None),
            P(BOTH, None),
            P(BOTH, None),
            P(None, BOTH),
            P(BOTH, None, None),
            P(BOTH, None, None),
            P(BOTH, None, None),
        ),
        out_specs=(
            P("fsdp", "seq", None),
            P("fsdp", "seq", None),
            P(BOTH),
            P(BOTH),
            P(BOTH),
            P(BOTH, None),
            P(BOTH, None),
            P(None, BOTH),
            P(None, BOTH),
            P(BOTH, None),
            P(BOTH, None),
            P(BOTH, None),
            P(None, BOTH),
            P(BOTH, None, None),
            P(BOTH, None, None),
            P(BOTH, None, None),
        ),
        check_vma=False,
    )
```

```python
import functools

import jax
import jax.numpy as jnp
from jax import lax
from jax.experimental import pallas as pl
from jax.experimental.pallas import tpu as pltpu
from jax.sharding import PartitionSpec as P

HEADS = 16
NOPE = 128
ROPE = 64
VDIM = 128
KVR = 512

EPS = 1e-06
THETA = 10000.0
NEGATIVE = -1e30
BOTH = ("seq", "fsdp")
VMEM_LIMIT = 60 * 2**20
F32 = jnp.float32
BF16 = jnp.bfloat16


def product(left, right):
    return jnp.dot(left, right, preferred_element_type=F32)


def left_product(left, right):
    return lax.dot_general(left, right, (((0,), (0,)), ((), ())), preferred_element_type=F32)


def right_product(left, right):
    return lax.dot_general(left, right, (((1,), (1,)), ((), ())), preferred_element_type=F32)


def normed(value):
    factor = lax.rsqrt(jnp.mean(value * value, axis=-1, keepdims=True) + EPS)
    return (value * factor, factor)


def norm_back(grad_unit, unit, factor):
    return factor * (grad_unit - unit * jnp.mean(grad_unit * unit, axis=-1, keepdims=True))


def rotate(value, angles):
    middle = value.shape[-1] // 2
    cosine = jnp.cos(angles)
    sine = jnp.sin(angles)
    first = value[..., :middle]
    second = value[..., middle:]
    return jnp.concatenate(
        [first * cosine - second * sine, second * cosine + first * sine], axis=-1
    )


def silu_parts(value):
    logistic = jax.nn.sigmoid(value)
    return (value * logistic, logistic * (1.0 + value * (1.0 - logistic)))


def swap(value, bit):
    count = lax.axis_size("seq")
    return lax.ppermute(value, "seq", [(i, i ^ (1 << bit)) for i in range(count)])


def chip_bits():
    return list(range(1, lax.axis_size("seq").bit_length() - 1))


def halves_of(width):
    middle = -(-width // 256) * 128
    return ((0, middle), (middle, width))


class Flow:
    def __init__(self, steps):
        self.steps = steps
        self.value = None
        self.pending = next(steps)

    def arrive(self, arrived):
        try:
            self.pending = self.steps.send(arrived)
        except StopIteration as stop:
            self.pending = None
            self.value = stop.value


class Slots:
    def __init__(self):
        self.token = jnp.zeros((8, 128), F32)

    def tie(self, values):
        return lax.optimization_barrier((values, self.token))[0]

    def run(self, flows, compute=None, *inputs):
        flows = [flow for flow in flows if flow.pending is not None]
        pending = [flow.pending for flow in flows]
        made = compute(*self.tie(inputs)) if compute else ()
        pending, made, self.token = lax.optimization_barrier((pending, made, self.token))
        for flow, arrived in zip(flows, pending):
            flow.arrive(arrived)
        return made

    def finish(self, flow, *others):
        while flow.pending is not None:
            self.run((flow,) + others)
        return flow.value


def stacked(value, names):
    lead = len(names)
    axes = [names.index(bit) for bit in sorted(names, reverse=True)]
    value = value.transpose(axes + list(range(lead, value.ndim)))
    return value.reshape((-1,) + value.shape[lead:])


def spread(parts):
    bits = chip_bits()
    orders = (bits, bits[::-1])
    for step in range(len(bits)):
        arrived = yield [swap(part, order[step]) for part, order in zip(parts, orders)]
        parts = [jnp.stack(pair) for pair in zip(parts, arrived)]
    return [stacked(part, order[::-1]) for part, order in zip(parts, orders)]


def total_of(terms):
    return sum((term.astype(F32) for term in terms[1:]), terms[0].astype(F32))


def fold(parts):
    bits = chip_bits()
    for step in range(len(bits)):
        kept, sent = [], []
        for terms, order in zip(parts, (bits, bits[::-1])):
            axis = sorted(order[step:], reverse=True).index(order[step])
            kept.append([lax.index_in_dim(term, 0, axis, keepdims=False) for term in terms])
            send = total_of([lax.index_in_dim(term, 1, axis, keepdims=False) for term in terms])
            sent.append(swap(send.astype(BF16), order[step]))
        arrived = yield sent
        parts = [terms + [got] for terms, got in zip(kept, arrived)]
    return [total_of(terms) for terms in parts]


def gather_seq(own):
    parts = yield from spread([own[:, low:high] for low, high in halves_of(own.shape[1])])
    near = jnp.concatenate(parts, axis=-1)
    (far,) = yield [swap(near, 0)]
    return jnp.concatenate([near, far], axis=0).reshape(-1, own.shape[1])


def scatter_seq(value, rows):
    half = value.shape[0] // 2
    (far,) = yield [swap(value[half:], 0)]
    shape = (2,) * len(chip_bits()) + (rows, value.shape[1])
    terms = [value[:half].reshape(shape), far.reshape(shape)]
    parts = yield from fold(
        [[term[..., low:high] for term in terms] for low, high in halves_of(value.shape[1])]
    )
    return jnp.concatenate(parts, axis=-1)


def exchange(value, axes):
    (arrived,) = yield [lax.all_to_all(value, axes, 0, 0, tiled=True)]
    return arrived


def exchange_line(value):
    count = lax.axis_size("fsdp")
    place = lax.axis_index("fsdp")

    def piece(index):
        return lax.dynamic_index_in_dim(value, index % count, 0, keepdims=False)

    arrived = yield [
        lax.ppermute(
            piece(place + turn), "fsdp", [(i, (i + turn) % count) for i in range(count)]
        )
        for turn in range(1, count)
    ]
    return sum((part.astype(F32) for part in arrived), piece(place).astype(F32))


def line_gather(own):
    count = lax.axis_size("fsdp")
    ups, downs = [], []
    up = down = own
    for step in range(1, count):
        up, down = yield [
            lax.ppermute(up, "fsdp", [(i, i + 1) for i in range(step - 1, count - 1)]),
            lax.ppermute(down, "fsdp", [(i, i - 1) for i in range(1, count - step + 1)]),
        ]
        ups.append(up)
        downs.append(down)
    around = jnp.stack(ups[::-1] + [own] + downs)
    return lax.dynamic_slice_in_dim(around, count - 1 - lax.axis_index("fsdp"), count, 0)


def gather_all(own, place):
    width = own.shape[1]
    block = yield from line_gather(own)
    block = block.reshape(-1, width)
    near = [block[:, low:high] for low, high in halves_of(width)]
    fresh, far = near, None
    bits = chip_bits()
    orders = (bits, bits[::-1])
    for step in range(len(bits)):
        arrived = yield [swap(part, order[step]) for part, order in zip(near, orders)] + [
            swap(part, 0) for part in fresh
        ]
        fresh, crossed = arrived[:2], arrived[2:]
        near = [jnp.stack(pair) for pair in zip(near, fresh)]
        far = crossed if far is None else [jnp.stack(pair) for pair in zip(far, crossed)]
    crossed = yield [swap(part, 0) for part in fresh]
    far = [jnp.stack(pair) for pair in zip(far, crossed)]
    parts = [stacked(part, order[::-1]) for part, order in zip(near + far, orders + orders)]
    return assemble(place, parts)


def reduce_all(keeps, sends, rows):
    arrived = yield [swap(send, 0) for send in sends]
    shape = (2,) * len(chip_bits()) + (lax.axis_size("fsdp"), rows, keeps[0].shape[-1])
    parts = yield from fold(
        [[keep.reshape(shape), got.reshape(shape)] for keep, got in zip(keeps, arrived)]
    )
    parts = [part.astype(BF16) for part in parts]
    return (yield from exchange_line(jnp.concatenate(parts, axis=-1)))


def assemble_kernel(place_ref, low_ref, high_ref, other_low_ref, other_high_ref, out_ref):
    count, middle = low_ref.shape[1:]
    core = place_ref[1]
    own = pl.ds(pl.multiple_of(core * count, count), count)
    other = pl.ds(pl.multiple_of((1 - core) * count, count), count)
    out_ref[own, :middle] = low_ref[0]
    out_ref[own, middle:] = high_ref[0]
    out_ref[other, :middle] = other_low_ref[0]
    out_ref[other, middle:] = other_high_ref[0]


def assemble(place, parts):
    chips, count, _ = parts[0].shape
    width = parts[0].shape[2] + parts[1].shape[2]
    return pl.pallas_call(
        assemble_kernel,
        grid_spec=pltpu.PrefetchScalarGridSpec(
            num_scalar_prefetch=1,
            grid=(chips,),
            in_specs=[
                pl.BlockSpec((1,) + part.shape[1:], lambda i, place: (i ^ place[2], 0, 0))
                for part in parts
            ],
            out_specs=pl.BlockSpec((2 * count, width), lambda i, _: (i, 0)),
        ),
        out_shape=jax.ShapeDtypeStruct((2 * chips * count, width), BF16),
        compiler_params=pltpu.CompilerParams(vmem_limit_bytes=VMEM_LIMIT),
        cost_estimate=pl.CostEstimate(
            flops=0, bytes_accessed=8 * chips * count * width, transcendentals=0
        ),
        name="assemble",
    )(place, *parts)


def one_hot(slots, capacity):
    rows = slots.shape[-1]
    return lax.broadcasted_iota(jnp.int32, (capacity, rows), 0) == slots


def forward_kernel(
    blocks,
    capacity,
    experts,
    hidden,
    place_ref,
    slots_ref,
    tokens_ref,
    wide_ref,
    gate_ref,
    up_ref,
    taken_ref,
    hidden_ref,
    to_pre_ref,
    to_up_ref,
    made_ref,
    shared_hidden_ref,
    shared_to_pre_ref,
    shared_to_up_ref,
):
    rows = slots_ref.shape[-1]
    lanes = shared_hidden_ref.shape[-1]
    expert = place_ref[0]
    wide = jnp.dot(tokens_ref[...], wide_ref[...], preferred_element_type=F32)
    first = wide[:, :lanes]
    second = wide[:, lanes:]
    silu, slope = silu_parts(first)
    shared_hidden_ref[...] = (silu * second).astype(BF16)
    shared_to_pre_ref[...] = (second * slope).astype(BF16)
    shared_to_up_ref[...] = silu.astype(BF16)
    lane = lax.broadcasted_iota(jnp.int32, first.shape, 1)
    logits = jnp.where((lane >= hidden) & (lane < hidden + experts), first, NEGATIVE)
    powers = jnp.exp(logits - jnp.max(logits, axis=-1, keepdims=True))
    total = jnp.sum(powers, axis=-1, keepdims=True)
    gates = jnp.sum(jnp.where(lane == hidden + expert, powers, 0.0), axis=-1, keepdims=True)
    gates = jnp.broadcast_to(gates / total, first.shape)
    slot_gates = []
    for block in range(blocks):
        chosen = one_hot(slots_ref[block], capacity)
        taken_ref[pl.ds(block * capacity, capacity), :] = jnp.dot(
            chosen.astype(BF16),
            tokens_ref[pl.ds(block * rows, rows), :],
            preferred_element_type=F32,
        ).astype(BF16)
        slot_gates.append(
            jnp.dot(
                chosen.astype(F32),
                gates[block * rows : (block + 1) * rows],
                precision=lax.Precision.HIGHEST,
                preferred_element_type=F32,
            )[:, :1]
        )
    slot_gates = jnp.concatenate(slot_gates, axis=0)
    gate_pre = jnp.dot(taken_ref[...], gate_ref[...], preferred_element_type=F32)
    up_pre = jnp.dot(taken_ref[...], up_ref[...], preferred_element_type=F32)
    swish, slope = silu_parts(gate_pre)
    made = swish * up_pre
    made_ref[...] = made.astype(BF16)
    hidden_ref[...] = (made * slot_gates).astype(BF16)
    to_pre_ref[...] = (up_pre * slope * slot_gates).astype(BF16)
    to_up_ref[...] = (swish * slot_gates).astype(BF16)


def backward_kernel(
    blocks,
    capacity,
    slots_ref,
    top_ref,
    to_pre_ref,
    to_up_ref,
    made_ref,
    shared_to_pre_ref,
    shared_to_up_ref,
    shared_ref,
    down_ref,
    taken_top_ref,
    pre_ref,
    post_ref,
    shared_grad_ref,
    gate_grad_ref,
):
    rows = slots_ref.shape[-1]
    lanes = shared_ref.shape[-1]
    back = jnp.dot(top_ref[...], shared_ref[...], preferred_element_type=F32)
    shared_grad_ref[:, :lanes] = (back * shared_to_pre_ref[...].astype(F32)).astype(BF16)
    shared_grad_ref[:, lanes:] = (back * shared_to_up_ref[...].astype(F32)).astype(BF16)
    for block in range(blocks):
        chosen = one_hot(slots_ref[block], capacity).astype(BF16)
        taken_top_ref[pl.ds(block * capacity, capacity), :] = jnp.dot(
            chosen, top_ref[pl.ds(block * rows, rows), :], preferred_element_type=F32
        ).astype(BF16)
    grad = jnp.dot(taken_top_ref[...], down_ref[...], preferred_element_type=F32)
    pre_ref[...] = (grad * to_pre_ref[...].astype(F32)).astype(BF16)
    post_ref[...] = (grad * to_up_ref[...].astype(F32)).astype(BF16)
    slot_grads = jnp.sum(made_ref[...].astype(F32) * grad, axis=-1, keepdims=True)
    for block in range(blocks):
        chosen = one_hot(slots_ref[block], capacity)
        gate_grad_ref[block] = jnp.sum(
            jnp.where(chosen, slot_grads[block * capacity : (block + 1) * capacity], 0.0),
            axis=0,
            keepdims=True,
        )


def scores_of(qn_ref, qr_ref, kv_ref, kr_ref, seg_q, seg_k, pos_q, pos_k, head, factor):
    lane = lax.broadcasted_iota(jnp.int32, qr_ref.shape, 1)
    turned = jnp.where(lane // ROPE == head, qr_ref[...], jnp.zeros((), BF16))
    query = jnp.concatenate([qn_ref[...], turned], axis=1)
    keys = jnp.concatenate([kv_ref[:, :NOPE], kr_ref[...]], axis=1)
    scores = lax.dot_general(
        query, keys, (((1,), (1,)), ((), ())), preferred_element_type=F32
    )
    allowed = (seg_q[...] == seg_k[...]) & (pos_k[...] <= pos_q[...])
    scores = jnp.where(allowed, scores * factor, NEGATIVE)
    powers = jnp.exp(scores - jnp.max(scores, axis=-1, keepdims=True))
    return query, keys, powers / jnp.sum(powers, axis=-1, keepdims=True)


def attend_kernel(
    factor, qn_ref, qr_ref, kv_ref, kr_ref, seg_q, seg_k, pos_q, pos_k, out_ref
):
    _, _, probs = scores_of(
        qn_ref, qr_ref, kv_ref, kr_ref, seg_q, seg_k, pos_q, pos_k, pl.program_id(1), factor
    )
    out_ref[...] = jnp.dot(
        probs.astype(BF16), kv_ref[:, NOPE:], preferred_element_type=F32
    ).astype(BF16)


def attend_back_kernel(
    factor,
    qn_ref,
    qr_ref,
    kv_ref,
    kr_ref,
    seg_q,
    seg_k,
    pos_q,
    pos_k,
    top_ref,
    grad_qn_ref,
    grad_qr_ref,
    grad_kv_ref,
    grad_kr_ref,
    sum_ref,
):
    step, head = pl.program_id(0), pl.program_id(1)
    last = pl.num_programs(0) - 1
    query, keys, probs = scores_of(
        qn_ref, qr_ref, kv_ref, kr_ref, seg_q, seg_k, pos_q, pos_k, head, factor
    )
    top = top_ref[...]
    grad_probs = lax.dot_general(
        top, kv_ref[:, NOPE:], (((1,), (1,)), ((), ())), preferred_element_type=F32
    )
    mean = jnp.sum(probs * grad_probs, axis=-1, keepdims=True)
    grad_scores = (probs * (grad_probs - mean)).astype(BF16)
    low = probs.astype(BF16)
    grad_query = jnp.dot(grad_scores, keys, preferred_element_type=F32) * factor
    grad_qn_ref[...] = grad_query[:, :NOPE].astype(BF16)
    turned = grad_query[:, NOPE:]
    lane = lax.broadcasted_iota(jnp.int32, turned.shape, 1)
    turned = jnp.where(lane // ROPE == head, turned, 0.0)
    grad_keys = left_product(grad_scores, query) * factor
    grad_values = left_product(low, top)

    @pl.when(head == 0)
    def _():
        grad_qr_ref[...] = turned

    @pl.when(head != 0)
    def _():
        grad_qr_ref[...] += turned

    @pl.when((step == 0) & (head == 0))
    def _():
        grad_kr_ref[...] = grad_keys[:, NOPE:]

    @pl.when((step != 0) | (head != 0))
    def _():
        grad_kr_ref[...] += grad_keys[:, NOPE:]

    @pl.when(step == 0)
    def _():
        sum_ref[head, :, :NOPE] = grad_keys[:, :NOPE]
        sum_ref[head, :, NOPE:] = grad_values

    @pl.when(step != 0)
    def _():
        sum_ref[head, :, :NOPE] += grad_keys[:, :NOPE]
        sum_ref[head, :, NOPE:] += grad_values

    @pl.when(step == last)
    def _():
        grad_kv_ref[head] = sum_ref[head].astype(BF16)


def attend_specs(length, heads, turned, block):
    return [
        pl.BlockSpec((block, NOPE), lambda i, h: (i, h)),
        pl.BlockSpec((block, turned), lambda i, h: (i, 0)),
        pl.BlockSpec((length, NOPE + VDIM), lambda i, h: (0, h)),
        pl.BlockSpec((length, turned), lambda i, h: (0, 0)),
        pl.BlockSpec((block, 1), lambda i, h: (i, 0)),
        pl.BlockSpec((1, length), lambda i, h: (0, 0)),
        pl.BlockSpec((block, 1), lambda i, h: (i, 0)),
        pl.BlockSpec((1, length), lambda i, h: (0, 0)),
    ]


def attend_stage(factor, heads, inputs):
    length, turned = inputs[1].shape
    block = min(length, 256)
    return pl.pallas_call(
        functools.partial(attend_kernel, factor),
        grid=(length // block, heads),
        in_specs=attend_specs(length, heads, turned, block),
        out_specs=pl.BlockSpec((block, VDIM), lambda i, h: (i, h)),
        out_shape=jax.ShapeDtypeStruct((length, heads * VDIM), BF16),
        compiler_params=pltpu.CompilerParams(vmem_limit_bytes=VMEM_LIMIT),
        cost_estimate=pl.CostEstimate(
            flops=2 * heads * length * length * 384,
            bytes_accessed=8 * length * heads * NOPE,
            transcendentals=heads * length * length,
        ),
        name="attend_stage",
    )(*inputs)


def attend_back_stage(factor, heads, inputs, top):
    length, turned = inputs[1].shape
    block = min(length, 256)
    return pl.pallas_call(
        functools.partial(attend_back_kernel, factor),
        grid=(length // block, heads),
        in_specs=attend_specs(length, heads, turned, block)
        + [pl.BlockSpec((block, VDIM), lambda i, h: (i, h))],
        out_specs=[
            pl.BlockSpec((block, NOPE), lambda i, h: (i, h)),
            pl.BlockSpec((block, turned), lambda i, h: (i, 0)),
            pl.BlockSpec((heads, length, NOPE + VDIM), lambda i, h: (0, 0, 0)),
            pl.BlockSpec((length, turned), lambda i, h: (0, 0)),
        ],
        out_shape=[
            jax.ShapeDtypeStruct((length, heads * NOPE), BF16),
            jax.ShapeDtypeStruct((length, turned), F32),
            jax.ShapeDtypeStruct((heads, length, NOPE + VDIM), BF16),
            jax.ShapeDtypeStruct((length, turned), F32),
        ],
        scratch_shapes=[pltpu.VMEM((heads, length, NOPE + VDIM), F32)],
        compiler_params=pltpu.CompilerParams(vmem_limit_bytes=VMEM_LIMIT),
        cost_estimate=pl.CostEstimate(
            flops=2 * heads * length * length * 1024,
            bytes_accessed=16 * length * heads * NOPE,
            transcendentals=heads * length * length,
        ),
        name="attend_back_stage",
    )(*inputs, top)


def whole_spec(array):
    return pl.BlockSpec(
        array.shape, lambda i, *_: (0,) * array.ndim, pipeline_mode=pl.Buffered(1)
    )


def rows_spec(size, columns):
    return pl.BlockSpec((size, columns), lambda i, *_: (i, 0))


def forward_stage(place, slots, tokens, weights, capacity, experts, hidden, lanes):
    devices, _, rows = slots.shape
    blocks = 2 * lax.axis_size("fsdp")
    steps = devices // blocks
    width = tokens.shape[1]
    half = weights[1].shape[1]
    count = blocks * capacity
    sizes = [(count, width)] + [(count, half)] * 4 + [(blocks * rows, lanes)] * 3
    return pl.pallas_call(
        functools.partial(forward_kernel, blocks, capacity, experts, hidden),
        grid_spec=pltpu.PrefetchScalarGridSpec(
            num_scalar_prefetch=1,
            grid=(steps,),
            in_specs=[
                pl.BlockSpec((blocks, 1, rows), lambda i, *_: (i, 0, 0)),
                rows_spec(blocks * rows, width),
                *[whole_spec(weight) for weight in weights],
            ],
            out_specs=[rows_spec(*size) for size in sizes],
        ),
        out_shape=[
            jax.ShapeDtypeStruct((steps * size, columns), BF16) for size, columns in sizes
        ],
        compiler_params=pltpu.CompilerParams(vmem_limit_bytes=VMEM_LIMIT),
        cost_estimate=pl.CostEstimate(
            flops=devices * 4 * width * (capacity * half + rows * lanes),
            bytes_accessed=3 * devices * rows * width,
            transcendentals=devices * capacity * half,
        ),
        name="forward_stage",
    )(place, slots, tokens, *weights)


def backward_stage(slots, top, saved, weights, capacity):
    devices, _, rows = slots.shape
    blocks = 2 * lax.axis_size("fsdp")
    steps = devices // blocks
    width = top.shape[1]
    lanes, half = (weight.shape[1] for weight in weights)
    count = blocks * capacity
    slots_spec = pl.BlockSpec((blocks, 1, rows), lambda i, *_: (i, 0, 0))
    sizes = [(count, width)] + [(count, half)] * 2 + [(blocks * rows, 2 * lanes)]
    return pl.pallas_call(
        functools.partial(backward_kernel, blocks, capacity),
        grid=(steps,),
        in_specs=[
            slots_spec,
            rows_spec(blocks * rows, width),
            *[rows_spec(count, half) for _ in range(3)],
            *[rows_spec(blocks * rows, lanes) for _ in range(2)],
            *[whole_spec(weight) for weight in weights],
        ],
        out_specs=[rows_spec(*size) for size in sizes] + [slots_spec],
        out_shape=[
            jax.ShapeDtypeStruct((steps * size, columns), BF16) for size, columns in sizes
        ]
        + [jax.ShapeDtypeStruct(slots.shape, F32)],
        compiler_params=pltpu.CompilerParams(vmem_limit_bytes=VMEM_LIMIT),
        cost_estimate=pl.CostEstimate(
            flops=devices * 2 * width * (capacity * half + rows * lanes),
            bytes_accessed=4 * devices * rows * width,
            transcendentals=0,
        ),
        name="backward_stage",
    )(slots, top, *saved, *weights)


def combine_kernel(blocks, capacity, cuts, count, place_ref, slots_ref, *refs):
    lefts, rights = refs[:count], refs[count : 2 * count]
    shared_ref, shared_weight_ref = refs[2 * count : 2 * count + 2]
    outs = refs[2 * count + 2 : -1]
    rows_ref = refs[-1]
    rows = slots_ref.shape[-1]
    total = None
    for left, right in zip(lefts, rights):
        term = jnp.dot(left[...], right[...], preferred_element_type=F32)
        total = term if total is None else total + term
    rows_ref[...] = total.astype(BF16)
    half = blocks // 2
    for side in range(2):
        core = place_ref[1] ^ side
        for block in range(half):
            index = core * half + block
            chosen = one_hot(slots_ref[index], capacity).astype(BF16)
            there = pl.ds(pl.multiple_of(index * capacity, capacity), capacity)
            own = pl.ds(pl.multiple_of(index * rows, rows), rows)
            value = lax.dot_general(
                chosen,
                rows_ref[there, :],
                (((0,), (0,)), ((), ())),
                preferred_element_type=F32,
            ) + jnp.dot(
                shared_ref[own, :], shared_weight_ref[...], preferred_element_type=F32
            )
            value = value.astype(BF16)
            for part, (low, high) in enumerate(cuts):
                outs[2 * side + part][pl.ds(block * rows, rows), :] = value[:, low:high]


def combine_stage(place, slots, lefts, rights, shared, shared_weight, capacity):
    devices, _, rows = slots.shape
    blocks = 2 * lax.axis_size("fsdp")
    steps = devices // blocks
    width = rights[0].shape[1]
    cuts = halves_of(width)
    half = blocks // 2 * rows

    out_specs = [
        pl.BlockSpec((half, high - low), lambda i, place: (i ^ place[2], 0))
        for _ in range(2)
        for low, high in cuts
    ]
    out_shape = [
        jax.ShapeDtypeStruct((steps * half, high - low), BF16)
        for _ in range(2)
        for low, high in cuts
    ]
    flops = 2 * devices * width * (
        capacity * sum(left.shape[1] for left in lefts) + rows * (capacity + shared.shape[1])
    )
    outs = pl.pallas_call(
        functools.partial(combine_kernel, blocks, capacity, cuts, len(lefts)),
        grid_spec=pltpu.PrefetchScalarGridSpec(
            num_scalar_prefetch=1,
            grid=(steps,),
            in_specs=[
                pl.BlockSpec((blocks, 1, rows), lambda i, *_: (i, 0, 0)),
                *[rows_spec(blocks * capacity, left.shape[1]) for left in lefts],
                *[whole_spec(right) for right in rights],
                rows_spec(blocks * rows, shared.shape[1]),
                whole_spec(shared_weight),
            ],
            out_specs=out_specs,
            scratch_shapes=[pltpu.VMEM((blocks * capacity, width), BF16)],
        ),
        out_shape=out_shape,
        compiler_params=pltpu.CompilerParams(vmem_limit_bytes=VMEM_LIMIT),
        cost_estimate=pl.CostEstimate(
            flops=flops, bytes_accessed=devices * rows * width * 3, transcendentals=0
        ),
        name="combine_stage",
    )(place, slots, *lefts, *rights, shared, shared_weight)
    return outs[:2], outs[2:]


def per_device(
    tokens_in,
    segments,
    routes,
    cotangent,
    g_attn,
    g_kv,
    g_moe,
    w_query,
    w_kv_down,
    w_kv_up,
    w_out,
    w_router,
    w_shared_gate,
    w_shared_up,
    w_shared_down,
    w_expert_gate,
    w_expert_up,
    w_expert_down,
):
    micro_count, rows, width = tokens_in.shape
    seqs, line = lax.axis_size("seq"), lax.axis_size("fsdp")
    devices = seqs * line
    length = rows * seqs
    experts = devices // 2
    picked = routes.shape[2]
    capacity = max(2, rows * picked * 4 // (experts * 3))
    capacity = -(-capacity // 16) * 16
    heads = HEADS // seqs
    me_seq = lax.axis_index("seq")
    me = me_seq * line + lax.axis_index("fsdp")
    expert = me // 2
    factor = (NOPE + ROPE) ** (-0.5)
    frequency = THETA ** (-jnp.arange(ROPE // 2, dtype=F32) * 2.0 / ROPE)
    order = jnp.arange(seqs)
    ranks = (order ^ me_seq) >> 1 | ((order ^ me_seq) & 1) * (seqs // 2)
    order = me_seq ^ ((order % (seqs // 2)) * 2 + order // (seqs // 2))

    def to_relative(value):
        return value.reshape(seqs, rows, -1)[order].reshape(value.shape)

    def to_absolute(value):
        return value.reshape(seqs, rows, -1)[ranks].reshape(value.shape)

    places = (order[:, None] * rows + jnp.arange(rows)[None, :]).reshape(-1)
    angles = places.astype(F32)[:, None] * frequency[None, :]
    own_angles = angles[:rows]
    micros = range(micro_count)

    slots = Slots()
    place = jnp.stack([expert, me_seq & 1, me_seq >> 1]).astype(jnp.int32)

    piece = w_kv_down.shape[0]
    kv_columns = w_kv_down.shape[1]
    small = jnp.concatenate(
        [
            w_kv_down,
            w_router,
            g_attn[:, None],
            g_moe[:, None],
            jnp.pad(g_kv, (0, piece - g_kv.shape[0]))[:, None],
            routes.reshape(piece, -1).astype(BF16),
        ],
        axis=1,
    )
    small = lax.all_gather(small, BOTH, axis=0, tiled=True)

    query_width = heads * (NOPE + ROPE)
    out_width = heads * VDIM
    for_query = w_query.reshape(piece, seqs, heads, NOPE + ROPE)
    for_query = jnp.concatenate(
        [
            for_query[..., :NOPE].reshape(piece, seqs, -1),
            for_query[..., NOPE:].reshape(piece, seqs, -1),
        ],
        axis=2,
    ).transpose(1, 0, 2)
    for_out = w_out.reshape(seqs, out_width, piece).transpose(0, 2, 1)
    for_heads = jnp.concatenate([for_query, for_out], axis=2)
    for_heads = jnp.broadcast_to(
        for_heads[:, None], (seqs, line, piece, query_width + out_width)
    ).reshape(devices, piece, query_width + out_width)
    ready, for_heads = lax.optimization_barrier((tokens_in, for_heads))
    tokens = [Flow(gather_seq(ready[micro])) for micro in micros]
    for_heads = Flow(exchange(for_heads, BOTH))
    up_weight = Flow(
        exchange(jnp.broadcast_to(w_kv_up[None], (line,) + w_kv_up.shape), "fsdp")
    )
    hidden = w_shared_gate.shape[1] // devices

    def pack_shared(gate, up, down):
        return jnp.concatenate(
            [
                gate.reshape(piece, devices, hidden).transpose(1, 0, 2),
                up.reshape(piece, devices, hidden).transpose(1, 0, 2),
                down.reshape(devices, hidden, piece).transpose(0, 2, 1),
            ],
            axis=2,
        )

    for_shared = slots.run(tokens, pack_shared, w_shared_gate, w_shared_up, w_shared_down)
    for_shared = Flow(exchange(for_shared, BOTH))
    slots.run([*tokens, for_heads, up_weight])
    tops = [lax.all_gather(slots.tie(cotangent[0]), BOTH, axis=0, tiled=True), None]
    slots.finish(tokens[0], tokens[1])
    slots.finish(tokens[1])
    (small,) = slots.run([], lambda *given: given, small)
    for_heads, up_weight = for_heads.value, up_weight.value
    for_heads = for_heads.reshape(width, query_width + out_width)
    query_weight = for_heads[:, :query_width]
    out_weight = for_heads[:, query_width:]
    up_weight = up_weight.transpose(1, 0, 2).reshape(KVR, -1)
    down_weight = small[:, :kv_columns]
    router_weight = small[:, kv_columns : kv_columns + experts]
    last = kv_columns + experts
    gain_one = small[:, last].astype(F32)
    gain_two = small[:, last + 1].astype(F32)
    gain_latent = small[:, last + 2].reshape(devices, piece)[:, : g_kv.shape[0]].reshape(-1)
    routes_all = small[:, last + 3 :].astype(jnp.int32).reshape((devices,) + routes.shape)
    gain_latent = gain_latent.astype(F32)

    def projections(tokens):
        unit_one, _ = normed(tokens.astype(F32))
        normed_one = (unit_one * gain_one).astype(BF16)
        query_raw = product(normed_one, query_weight)
        query = query_raw[:, : heads * NOPE].astype(BF16)
        turned = query_raw[:, heads * NOPE :].reshape(length, heads, ROPE)
        turned = turned_lanes(rotate(turned, angles[:, None, :]).reshape(length, -1))
        latent = product(normed_one, down_weight)
        unit_latent, factor_latent = normed(latent[:, :KVR])
        latent_norm = (unit_latent * gain_latent).astype(BF16)
        key_rope = rotate(latent[:, KVR:], angles).astype(BF16)
        key_value = product(latent_norm, up_weight).astype(BF16)
        key_rope = turned_lanes(jnp.tile(key_rope, (1, heads)))
        return (
            normed_one,
            latent_norm,
            (query, turned, key_value, key_rope),
            unit_latent[:rows],
            factor_latent[:rows],
        )

    def turned_lanes(value):
        return jnp.pad(value.astype(BF16), ((0, 0), (0, -value.shape[1] % 128)))

    def marks_of(micro):
        segment = segments[micro].reshape(seqs, rows)[order].reshape(-1)
        return segment[:, None], segment[None, :], places[:, None], places[None, :]

    def attend(projected, marks):
        attended = attend_stage(factor, heads, projected[2] + marks)
        return attended, right_product(attended, out_weight).astype(BF16)

    def home_forward(micro, summed):
        residual = tokens_in[micro].astype(F32) + summed.astype(F32)
        unit_two, factor_two = normed(residual)
        normed_two = (unit_two * gain_two).astype(BF16)
        return residual, unit_two, factor_two, normed_two

    marks = [marks_of(micro) for micro in micros]
    projected = [None, None]
    attended = [None, None]
    residuals = [None, None]
    normed_alls = [None, None]
    projected[0] = slots.run([], projections, tokens[0].value)
    attended[0] = slots.run([], attend, projected[0], marks[0])
    summed = Flow(scatter_seq(attended[0][1], rows))
    projected[1] = slots.run([summed, for_shared], projections, tokens[1].value)
    attended[1] = slots.run([summed], attend, projected[1], marks[1])
    summed_two = Flow(scatter_seq(attended[1][1], rows))
    slots.finish(summed, summed_two)
    residuals[0] = home_forward(0, summed.value)
    first, tops[0] = lax.optimization_barrier((residuals[0][3], tops[0]))
    normed_alls[0] = lax.all_gather(first, BOTH, axis=0, tiled=True)
    slots.finish(summed_two)
    residuals[1] = home_forward(1, summed_two.value)
    normed_alls[1] = lax.all_gather(residuals[1][3], BOTH, axis=0, tiled=True)
    top_flow = Flow(gather_all(slots.tie(cotangent[1]), place))
    for _ in range(line):
        slots.run([top_flow])

    lanes = -(-(hidden + experts) // 128) * 128

    def padded(parts):
        parts = jnp.concatenate(parts, axis=1)
        return jnp.pad(parts, ((0, 0), (0, lanes - parts.shape[1])))

    for_shared = for_shared.value.reshape(width, 3 * hidden)
    shared_gate = for_shared[:, :hidden]
    shared_up = for_shared[:, hidden : 2 * hidden]
    shared_down = padded([for_shared[:, 2 * hidden :]])
    wide_weight = jnp.concatenate(
        [padded([shared_gate, router_weight]), padded([shared_up])], axis=1
    )
    shared_in = jnp.concatenate([padded([shared_gate]), padded([shared_up])], axis=1)
    gate_weight = w_expert_gate[0]
    up_expert = w_expert_up[0]
    down_expert = w_expert_down[0]
    forward_weights = (wide_weight, gate_weight, up_expert)
    backward_weights = (shared_down, down_expert.T)
    transposed = (gate_weight.T, up_expert.T, shared_in.T, shared_down.T)

    def slots_of(micro):
        hit = jnp.any(routes_all[:, micro] == expert, axis=-1)
        rank = jnp.cumsum(hit.astype(jnp.int32), axis=1) - 1
        return jnp.where(hit, rank, -1)[:, None, :]

    def forward_of(seats, tokens):
        return forward_stage(
            place, seats, tokens, forward_weights, capacity, experts, hidden, lanes
        )

    def backward_of(seats, top, made):
        return backward_stage(
            seats, top, (made[2], made[3], made[4], made[6], made[7]), backward_weights, capacity
        )

    def grads_to_tokens(seats, back):
        return combine_stage(
            place, seats, back[1:3], transposed[:2], back[3], transposed[2], capacity
        )

    def outputs_to_tokens(seats, made):
        return combine_stage(
            place, seats, made[1:2], (down_expert,), made[5], transposed[3], capacity
        )

    def routed_pairs(made, back):
        return (made[0], back[1]), (made[0], back[2]), (made[1], back[0])

    def routed_grads(*pairs):
        return tuple(left_product(*pair) for pair in pairs)

    def shared_grads_of(tokens, top, made, back):
        return left_product(tokens, back[3]), left_product(top, made[5])

    def added(function):
        def call(before, *values):
            return tuple(old + new for old, new in zip(before, function(*values)))

        return call

    def gate_grads_home(made):
        return Flow(exchange(made.reshape(devices, rows), BOTH))

    def home_backward(micro, grad_two, gate_grad):
        _, unit_two, factor_two, normed_two = residuals[micro]
        logits = product(normed_two, router_weight)
        shifted = jnp.exp(logits - jnp.max(logits, axis=-1, keepdims=True))
        router = shifted / jnp.sum(shifted, axis=-1, keepdims=True)
        router_in = jnp.sum(gate_grad.reshape(experts, 2, rows), axis=1).T
        grad_logits = (
            router * (router_in - jnp.sum(router * router_in, axis=-1, keepdims=True))
        ).astype(BF16)
        grad_two = grad_two + right_product(grad_logits, router_weight)
        grad_residual = cotangent[micro].astype(F32) + norm_back(
            grad_two * gain_two, unit_two, factor_two
        )
        return (
            grad_residual,
            left_product(normed_two, grad_logits),
            jnp.sum(grad_two * unit_two, axis=0),
        )

    def attend_backward(grad_attn_out, projected, marks):
        grad_attended = to_relative(product(grad_attn_out, out_weight).astype(BF16))
        return attend_back_stage(factor, heads, projected[2] + marks, grad_attended)

    def latents_backward(grad_key_value, grad_rope):
        grad_rope = jnp.sum(grad_rope[:, : heads * ROPE].reshape(length, heads, ROPE), axis=1)
        grad_key_value = grad_key_value.transpose(1, 0, 2).reshape(length, -1)
        grad_latent_part = right_product(grad_key_value, up_weight)
        part = jnp.concatenate([grad_latent_part, grad_rope], axis=1).astype(BF16)
        return part, grad_key_value

    def queries_backward(grad_query, grad_turned):
        grad_turned = grad_turned[:, : heads * ROPE].reshape(length, heads, ROPE)
        grad_turned = rotate(grad_turned, -angles[:, None, :]).reshape(length, -1)
        grad_query_raw = jnp.concatenate([grad_query, grad_turned.astype(BF16)], axis=1)
        one_part = right_product(to_absolute(grad_query_raw), query_weight)
        return one_part.astype(BF16), grad_query_raw

    def projections_backward(grad_query, grad_turned, grad_key_value, grad_rope):
        return (
            *latents_backward(grad_key_value, grad_rope),
            *queries_backward(grad_query, grad_turned),
        )

    def head_grads(projected, attended, grad_attn_out, grad_query_raw, grad_key_value):
        return (
            left_product(projected[0], grad_query_raw),
            left_product(grad_attn_out, to_absolute(attended)),
            left_product(grad_key_value, projected[1]),
        )

    def latent_backward(back, projected):
        unit_latent, factor_latent = projected[3:]
        grad_latent_norm = back[:, :KVR].astype(F32)
        grad_compressed = norm_back(grad_latent_norm * gain_latent, unit_latent, factor_latent)
        grad_latent = jnp.concatenate(
            [grad_compressed, rotate(back[:, KVR:].astype(F32), -own_angles)], axis=-1
        ).astype(BF16)
        return grad_latent, jnp.sum(grad_latent_norm * unit_latent, axis=0)

    def input_backward(micro, back, grad_latent, grad_residual):
        unit_one, factor_one = normed(tokens_in[micro].astype(F32))
        grad_one = back.astype(F32) + right_product(grad_latent, down_weight)
        return (
            grad_residual + norm_back(grad_one * gain_one, unit_one, factor_one),
            jnp.sum(grad_one * unit_one, axis=0),
        )

    def line_blocks(value):
        return value.astype(BF16).reshape(line, -1, value.shape[-1])

    def down_grads(normed_one, latents):
        columns = lax.dynamic_slice_in_dim(
            normed_one, me_seq * (width // seqs), width // seqs, axis=1
        )
        return left_product(columns, latents)

    seats = [slots_of(micro) for micro in micros]
    made = [None, None]
    def home_and_out(micro):
        home = home_backward(micro, grads[micro].value, gate_grad[micro].value)
        return home, lax.all_gather(home[0].astype(BF16), "seq", axis=0, tiled=True)

    def attention_back(*given):
        return projections_backward(*attend_backward(*given))

    gate_grad = [None, None]
    grads = [None, None]
    sums = [None, None]
    homes = [None, None]
    attn_out = [None, None]
    backs = [None, None]
    back = [None, None]
    finals = [None, None]

    def shared_home(shared_grads):
        shared_grads = shared_grads.astype(F32)
        return (
            shared_grads[:, :, :hidden].transpose(1, 0, 2).reshape(piece, -1),
            shared_grads[:, :, hidden : 2 * hidden].transpose(1, 0, 2).reshape(piece, -1),
            shared_grads[:, :, 2 * hidden :].transpose(0, 2, 1).reshape(-1, piece),
        )

    made[0] = slots.run([], forward_of, seats[0], normed_alls[0])
    back[0] = slots.run([top_flow], backward_of, seats[0], tops[0], made[0])
    gate_grad[0] = gate_grads_home(back[0][4])
    sides = slots.run([top_flow, gate_grad[0]], grads_to_tokens, seats[0], back[0])
    grads[0] = Flow(reduce_all(*sides, rows))
    tops[1] = slots.finish(top_flow)
    sides = slots.run([grads[0]], outputs_to_tokens, seats[0], made[0])
    sums[0] = Flow(reduce_all(*sides, rows))
    routed, shared = slots.run(
        [grads[0], sums[0]],
        lambda pairs, *given: (routed_grads(*pairs), shared_grads_of(*given)),
        routed_pairs(made[0], back[0]),
        normed_alls[0],
        tops[0],
        made[0],
        back[0],
    )
    made[1] = slots.run([grads[0]], forward_of, seats[1], normed_alls[1])
    back[1] = slots.run([], backward_of, seats[1], tops[1], made[1])
    gate_grad[1] = gate_grads_home(back[1][4])
    sides = slots.run(
        [grads[0], sums[0], gate_grad[1]], grads_to_tokens, seats[1], back[1]
    )
    grads[1] = Flow(reduce_all(*sides, rows))
    slots.finish(grads[0])
    homes[0], attn_out[0] = home_and_out(0)
    sides = slots.run([grads[1], sums[0]], outputs_to_tokens, seats[1], made[1])
    sums[1] = Flow(reduce_all(*sides, rows))
    parts = slots.run(
        [grads[1], sums[0]], added(routed_grads), routed, *routed_pairs(made[1], back[1])
    )
    shared = slots.run(
        [grads[1], sums[1]],
        added(shared_grads_of),
        shared,
        normed_alls[1],
        tops[1],
        made[1],
        back[1],
    )
    shared = jnp.concatenate(
        [shared[0][:, :hidden], shared[0][:, lanes : lanes + hidden], shared[1][:, :hidden]],
        axis=1,
    )
    shared = Flow(exchange(shared.astype(BF16).reshape(devices, piece, 3 * hidden), BOTH))
    parted, grad_key_value, one_part, grad_query_raw = slots.run(
        [grads[1], sums[1]],
        lambda *given: projections_backward(*attend_backward(*given)),
        attn_out[0],
        projected[0],
        marks[0],
    )
    slots.finish(grads[1])
    homes[1], attn_out[1] = home_and_out(1)
    whole_part, _ = lax.optimization_barrier(
        (jnp.concatenate([one_part, to_absolute(parted)], axis=1), homes[1][0])
    )
    whole_part = lax.psum_scatter(whole_part, "seq", scatter_dimension=0, tiled=True)
    head_sums = slots.run(
        [],
        head_grads,
        projected[0],
        attended[0][0],
        attn_out[0],
        grad_query_raw,
        grad_key_value,
    )
    scored = slots.run([sums[1]], attend_backward, attn_out[1], projected[1], marks[1])
    parted, grad_key_value = slots.run([shared], latents_backward, *scored[2:])
    latent_sums = Flow(scatter_seq(parted, rows))
    one_part, grad_query_raw = slots.run([latent_sums], queries_backward, *scored[:2])
    one_part = lax.psum_scatter(one_part, "seq", scatter_dimension=0, tiled=True)
    head_sums = slots.run(
        [latent_sums, sums[1]],
        added(head_grads),
        head_sums,
        projected[1],
        attended[1][0],
        attn_out[1],
        grad_query_raw,
        grad_key_value,
    )
    grad_heads = jnp.concatenate(head_sums[:2], axis=1).astype(BF16)
    grad_heads = Flow(exchange(grad_heads.reshape(devices, piece, -1), BOTH))
    grad_up = Flow(exchange_line(line_blocks(head_sums[2])))
    latents = [latent_backward(whole_part[:, width:], projected[0]), None]
    finals[0] = slots.run(
        [latent_sums, grad_up],
        functools.partial(input_backward, 0),
        whole_part[:, :width],
        latents[0][0],
        homes[0][0],
    )
    slots.finish(latent_sums)
    latents[1] = latent_backward(latent_sums.value, projected[1])
    latent_flow = Flow(gather_seq(jnp.concatenate([latent[0] for latent in latents], axis=1)))
    shared_final = slots.run([latent_flow], shared_home, shared.value)
    finals[1] = slots.run(
        [latent_flow, grad_heads],
        functools.partial(input_backward, 1),
        one_part,
        latents[1][0],
        homes[1][0],
    )
    tiny = jnp.concatenate(
        [
            sum(home[1] for home in homes).reshape(devices, -1),
            sum(final[1] for final in finals).reshape(devices, -1),
            sum(home[2] for home in homes).reshape(devices, -1),
            sum(latent[1] for latent in latents).reshape(devices, -1),
        ],
        axis=1,
    )
    tiny = Flow(exchange(tiny, BOTH))
    slots.finish(latent_flow)
    grad_kv_down = sum(
        down_grads(
            projected[micro][0],
            latent_flow.value[:, micro * kv_columns : (micro + 1) * kv_columns],
        )
        for micro in micros
    )
    grad_kv_down = Flow(exchange_line(line_blocks(grad_kv_down)))
    slots.run([grad_kv_down, tiny, grad_heads, sums[0], sums[1]])
    for flow in (sums[0], sums[1]):
        slots.finish(flow)
    outputs = [
        (residuals[micro][0] + sums[micro].value).astype(BF16) for micro in micros
    ]
    grad_kv_down = grad_kv_down.value
    grad_kv_up = grad_up.value.T
    grad_heads = grad_heads.value.reshape(seqs, line, piece, -1)
    grad_heads = jnp.sum(grad_heads.astype(F32), axis=1)
    grad_query_weight = jnp.concatenate(
        [
            grad_heads[:, :, : heads * NOPE].reshape(seqs, piece, heads, NOPE),
            grad_heads[:, :, heads * NOPE : query_width].reshape(seqs, piece, heads, ROPE),
        ],
        axis=3,
    )
    grad_query_weight = grad_query_weight.transpose(1, 0, 2, 3).reshape(piece, -1)
    grad_out_weight = grad_heads[:, :, query_width:].transpose(0, 2, 1).reshape(-1, piece)
    tiny = jnp.sum(tiny.value, axis=0)
    first = piece * experts
    return (
        jnp.stack(outputs),
        jnp.stack([final[0] for final in finals]),
        tiny[first : first + piece],
        tiny[first + 2 * piece :],
        tiny[first + piece : first + 2 * piece],
        grad_query_weight,
        grad_kv_down,
        grad_kv_up,
        grad_out_weight,
        tiny[:first].reshape(piece, experts),
        *shared_final,
        parts[0][None],
        parts[1][None],
        parts[2][None],
    )


def solution(mesh):
    return jax.shard_map(
        per_device,
        mesh=mesh,
        in_specs=(
            P("fsdp", "seq", None),
            P("fsdp", None),
            P("fsdp", "seq", None),
            P("fsdp", "seq", None),
            P(BOTH),
            P(BOTH),
            P(BOTH),
            P(BOTH, None),
            P(BOTH, None),
            P(None, BOTH),
            P(None, BOTH),
            P(BOTH, None),
            P(BOTH, None),
            P(BOTH, None),
            P(None, BOTH),
            P(BOTH, None, None),
            P(BOTH, None, None),
            P(BOTH, None, None),
        ),
        out_specs=(
            P("fsdp", "seq", None),
            P("fsdp", "seq", None),
            P(BOTH),
            P(BOTH),
            P(BOTH),
            P(BOTH, None),
            P(BOTH, None),
            P(None, BOTH),
            P(None, BOTH),
            P(BOTH, None),
            P(BOTH, None),
            P(BOTH, None),
            P(None, BOTH),
            P(BOTH, None, None),
            P(BOTH, None, None),
            P(BOTH, None, None),
        ),
        check_vma=False,
    )
```

```python
import functools

import jax
import jax.numpy as jnp
from jax import lax
from jax.experimental import pallas as pl
from jax.experimental.pallas import tpu as pltpu
from jax.sharding import PartitionSpec as P

HEADS = 16
NOPE = 128
ROPE = 64
VDIM = 128
KVR = 512

EPS = 1e-06
THETA = 10000.0
NEGATIVE = -1e30
BOTH = ("seq", "fsdp")
VMEM_LIMIT = 60 * 2**20
F32 = jnp.float32
BF16 = jnp.bfloat16


def product(left, right):
    return jnp.dot(left, right, preferred_element_type=F32)


def left_product(left, right):
    return lax.dot_general(left, right, (((0,), (0,)), ((), ())), preferred_element_type=F32)


def right_product(left, right):
    return lax.dot_general(left, right, (((1,), (1,)), ((), ())), preferred_element_type=F32)


def normed(value):
    factor = lax.rsqrt(jnp.mean(value * value, axis=-1, keepdims=True) + EPS)
    return (value * factor, factor)


def norm_back(grad_unit, unit, factor):
    return factor * (grad_unit - unit * jnp.mean(grad_unit * unit, axis=-1, keepdims=True))


def rotate(value, angles):
    middle = value.shape[-1] // 2
    cosine = jnp.cos(angles)
    sine = jnp.sin(angles)
    first = value[..., :middle]
    second = value[..., middle:]
    return jnp.concatenate(
        [first * cosine - second * sine, second * cosine + first * sine], axis=-1
    )


def silu_parts(value):
    logistic = jax.nn.sigmoid(value)
    return (value * logistic, logistic * (1.0 + value * (1.0 - logistic)))


def swap(value, bit):
    count = lax.axis_size("seq")
    return lax.ppermute(value, "seq", [(i, i ^ (1 << bit)) for i in range(count)])


def chip_bits():
    return list(range(1, lax.axis_size("seq").bit_length() - 1))


def halves_of(width):
    middle = -(-width // 256) * 128
    return ((0, middle), (middle, width))


class Flow:
    def __init__(self, steps):
        self.steps = steps
        self.value = None
        self.pending = next(steps)

    def arrive(self, arrived):
        try:
            self.pending = self.steps.send(arrived)
        except StopIteration as stop:
            self.pending = None
            self.value = stop.value


class Slots:
    def __init__(self):
        self.token = jnp.zeros((8, 128), F32)

    def tie(self, values):
        return lax.optimization_barrier((values, self.token))[0]

    def run(self, flows, compute=None, *inputs):
        flows = [flow for flow in flows if flow.pending is not None]
        pending = [flow.pending for flow in flows]
        made = compute(*self.tie(inputs)) if compute else ()
        pending, made, self.token = lax.optimization_barrier((pending, made, self.token))
        for flow, arrived in zip(flows, pending):
            flow.arrive(arrived)
        return made

    def finish(self, flow, *others):
        while flow.pending is not None:
            self.run((flow,) + others)
        return flow.value


def stacked(value, names):
    lead = len(names)
    axes = [names.index(bit) for bit in sorted(names, reverse=True)]
    value = value.transpose(axes + list(range(lead, value.ndim)))
    return value.reshape((-1,) + value.shape[lead:])


def spread(parts):
    bits = chip_bits()
    orders = (bits, bits[::-1])
    for step in range(len(bits)):
        arrived = yield [swap(part, order[step]) for part, order in zip(parts, orders)]
        parts = [jnp.stack(pair) for pair in zip(parts, arrived)]
    return [stacked(part, order[::-1]) for part, order in zip(parts, orders)]


def total_of(terms):
    return sum((term.astype(F32) for term in terms[1:]), terms[0].astype(F32))


def fold(parts):
    bits = chip_bits()
    for step in range(len(bits)):
        kept, sent = [], []
        for terms, order in zip(parts, (bits, bits[::-1])):
            axis = sorted(order[step:], reverse=True).index(order[step])
            kept.append([lax.index_in_dim(term, 0, axis, keepdims=False) for term in terms])
            send = total_of([lax.index_in_dim(term, 1, axis, keepdims=False) for term in terms])
            sent.append(swap(send.astype(BF16), order[step]))
        arrived = yield sent
        parts = [terms + [got] for terms, got in zip(kept, arrived)]
    return [total_of(terms) for terms in parts]


def gather_seq(own):
    parts = yield from spread([own[:, low:high] for low, high in halves_of(own.shape[1])])
    near = jnp.concatenate(parts, axis=-1)
    (far,) = yield [swap(near, 0)]
    return jnp.concatenate([near, far], axis=0).reshape(-1, own.shape[1])


def scatter_seq(value, rows):
    half = value.shape[0] // 2
    (far,) = yield [swap(value[half:], 0)]
    shape = (2,) * len(chip_bits()) + (rows, value.shape[1])
    terms = [value[:half].reshape(shape), far.reshape(shape)]
    parts = yield from fold(
        [[term[..., low:high] for term in terms] for low, high in halves_of(value.shape[1])]
    )
    return jnp.concatenate(parts, axis=-1)


def exchange(value, axes):
    (arrived,) = yield [lax.all_to_all(value, axes, 0, 0, tiled=True)]
    return arrived


def exchange_line(value):
    count = lax.axis_size("fsdp")
    place = lax.axis_index("fsdp")

    def piece(index):
        return lax.dynamic_index_in_dim(value, index % count, 0, keepdims=False)

    arrived = yield [
        lax.ppermute(
            piece(place + turn), "fsdp", [(i, (i + turn) % count) for i in range(count)]
        )
        for turn in range(1, count)
    ]
    return sum((part.astype(F32) for part in arrived), piece(place).astype(F32))


def line_gather(own):
    count = lax.axis_size("fsdp")
    ups, downs = [], []
    up = down = own
    for step in range(1, count):
        up, down = yield [
            lax.ppermute(up, "fsdp", [(i, i + 1) for i in range(step - 1, count - 1)]),
            lax.ppermute(down, "fsdp", [(i, i - 1) for i in range(1, count - step + 1)]),
        ]
        ups.append(up)
        downs.append(down)
    around = jnp.stack(ups[::-1] + [own] + downs)
    return lax.dynamic_slice_in_dim(around, count - 1 - lax.axis_index("fsdp"), count, 0)


def gather_all(own, place):
    width = own.shape[1]
    block = yield from line_gather(own)
    block = block.reshape(-1, width)
    near = [block[:, low:high] for low, high in halves_of(width)]
    fresh, far = near, None
    bits = chip_bits()
    orders = (bits, bits[::-1])
    for step in range(len(bits)):
        arrived = yield [swap(part, order[step]) for part, order in zip(near, orders)] + [
            swap(part, 0) for part in fresh
        ]
        fresh, crossed = arrived[:2], arrived[2:]
        near = [jnp.stack(pair) for pair in zip(near, fresh)]
        far = crossed if far is None else [jnp.stack(pair) for pair in zip(far, crossed)]
    crossed = yield [swap(part, 0) for part in fresh]
    far = [jnp.stack(pair) for pair in zip(far, crossed)]
    parts = [stacked(part, order[::-1]) for part, order in zip(near + far, orders + orders)]
    return assemble(place, parts)


def reduce_all(keeps, sends, rows):
    arrived = yield [swap(send, 0) for send in sends]
    shape = (2,) * len(chip_bits()) + (lax.axis_size("fsdp"), rows, keeps[0].shape[-1])
    parts = yield from fold(
        [[keep.reshape(shape), got.reshape(shape)] for keep, got in zip(keeps, arrived)]
    )
    parts = [part.astype(BF16) for part in parts]
    return (yield from exchange_line(jnp.concatenate(parts, axis=-1)))


def assemble_kernel(place_ref, low_ref, high_ref, other_low_ref, other_high_ref, out_ref):
    count, middle = low_ref.shape[1:]
    core = place_ref[1]
    own = pl.ds(pl.multiple_of(core * count, count), count)
    other = pl.ds(pl.multiple_of((1 - core) * count, count), count)
    out_ref[own, :middle] = low_ref[0]
    out_ref[own, middle:] = high_ref[0]
    out_ref[other, :middle] = other_low_ref[0]
    out_ref[other, middle:] = other_high_ref[0]


def assemble(place, parts):
    chips, count, _ = parts[0].shape
    width = parts[0].shape[2] + parts[1].shape[2]
    return pl.pallas_call(
        assemble_kernel,
        grid_spec=pltpu.PrefetchScalarGridSpec(
            num_scalar_prefetch=1,
            grid=(chips,),
            in_specs=[
                pl.BlockSpec((1,) + part.shape[1:], lambda i, place: (i ^ place[2], 0, 0))
                for part in parts
            ],
            out_specs=pl.BlockSpec((2 * count, width), lambda i, _: (i, 0)),
        ),
        out_shape=jax.ShapeDtypeStruct((2 * chips * count, width), BF16),
        compiler_params=pltpu.CompilerParams(vmem_limit_bytes=VMEM_LIMIT),
        cost_estimate=pl.CostEstimate(
            flops=0, bytes_accessed=8 * chips * count * width, transcendentals=0
        ),
        name="assemble",
    )(place, *parts)


def one_hot(slots, capacity):
    rows = slots.shape[-1]
    return lax.broadcasted_iota(jnp.int32, (capacity, rows), 0) == slots


def forward_kernel(
    blocks,
    capacity,
    experts,
    hidden,
    place_ref,
    slots_ref,
    tokens_ref,
    wide_ref,
    gate_ref,
    up_ref,
    taken_ref,
    hidden_ref,
    to_pre_ref,
    to_up_ref,
    made_ref,
    shared_hidden_ref,
    shared_to_pre_ref,
    shared_to_up_ref,
):
    rows = slots_ref.shape[-1]
    lanes = shared_hidden_ref.shape[-1]
    expert = place_ref[0]
    wide = jnp.dot(tokens_ref[...], wide_ref[...], preferred_element_type=F32)
    first = wide[:, :lanes]
    second = wide[:, lanes:]
    silu, slope = silu_parts(first)
    shared_hidden_ref[...] = (silu * second).astype(BF16)
    shared_to_pre_ref[...] = (second * slope).astype(BF16)
    shared_to_up_ref[...] = silu.astype(BF16)
    lane = lax.broadcasted_iota(jnp.int32, first.shape, 1)
    logits = jnp.where((lane >= hidden) & (lane < hidden + experts), first, NEGATIVE)
    powers = jnp.exp(logits - jnp.max(logits, axis=-1, keepdims=True))
    total = jnp.sum(powers, axis=-1, keepdims=True)
    gates = jnp.sum(jnp.where(lane == hidden + expert, powers, 0.0), axis=-1, keepdims=True)
    gates = jnp.broadcast_to(gates / total, first.shape)
    slot_gates = []
    for block in range(blocks):
        chosen = one_hot(slots_ref[block], capacity)
        taken_ref[pl.ds(block * capacity, capacity), :] = jnp.dot(
            chosen.astype(BF16),
            tokens_ref[pl.ds(block * rows, rows), :],
            preferred_element_type=F32,
        ).astype(BF16)
        slot_gates.append(
            jnp.dot(
                chosen.astype(F32),
                gates[block * rows : (block + 1) * rows],
                precision=lax.Precision.HIGHEST,
                preferred_element_type=F32,
            )[:, :1]
        )
    slot_gates = jnp.concatenate(slot_gates, axis=0)
    gate_pre = jnp.dot(taken_ref[...], gate_ref[...], preferred_element_type=F32)
    up_pre = jnp.dot(taken_ref[...], up_ref[...], preferred_element_type=F32)
    swish, slope = silu_parts(gate_pre)
    made = swish * up_pre
    made_ref[...] = made.astype(BF16)
    hidden_ref[...] = (made * slot_gates).astype(BF16)
    to_pre_ref[...] = (up_pre * slope * slot_gates).astype(BF16)
    to_up_ref[...] = (swish * slot_gates).astype(BF16)


def backward_kernel(
    blocks,
    capacity,
    slots_ref,
    top_ref,
    to_pre_ref,
    to_up_ref,
    made_ref,
    shared_to_pre_ref,
    shared_to_up_ref,
    shared_ref,
    down_ref,
    taken_top_ref,
    pre_ref,
    post_ref,
    shared_grad_ref,
    gate_grad_ref,
):
    rows = slots_ref.shape[-1]
    lanes = shared_ref.shape[-1]
    back = jnp.dot(top_ref[...], shared_ref[...], preferred_element_type=F32)
    shared_grad_ref[:, :lanes] = (back * shared_to_pre_ref[...].astype(F32)).astype(BF16)
    shared_grad_ref[:, lanes:] = (back * shared_to_up_ref[...].astype(F32)).astype(BF16)
    for block in range(blocks):
        chosen = one_hot(slots_ref[block], capacity).astype(BF16)
        taken_top_ref[pl.ds(block * capacity, capacity), :] = jnp.dot(
            chosen, top_ref[pl.ds(block * rows, rows), :], preferred_element_type=F32
        ).astype(BF16)
    grad = jnp.dot(taken_top_ref[...], down_ref[...], preferred_element_type=F32)
    pre_ref[...] = (grad * to_pre_ref[...].astype(F32)).astype(BF16)
    post_ref[...] = (grad * to_up_ref[...].astype(F32)).astype(BF16)
    slot_grads = jnp.sum(made_ref[...].astype(F32) * grad, axis=-1, keepdims=True)
    for block in range(blocks):
        chosen = one_hot(slots_ref[block], capacity)
        gate_grad_ref[block] = jnp.sum(
            jnp.where(chosen, slot_grads[block * capacity : (block + 1) * capacity], 0.0),
            axis=0,
            keepdims=True,
        )


def scores_of(qn_ref, qr_ref, kv_ref, kr_ref, seg_q, seg_k, pos_q, pos_k, head, factor):
    lane = lax.broadcasted_iota(jnp.int32, qr_ref.shape, 1)
    turned = jnp.where(lane // ROPE == head, qr_ref[...], jnp.zeros((), BF16))
    query = jnp.concatenate([qn_ref[...], turned], axis=1)
    keys = jnp.concatenate([kv_ref[:, :NOPE], kr_ref[...]], axis=1)
    scores = lax.dot_general(
        query, keys, (((1,), (1,)), ((), ())), preferred_element_type=F32
    )
    allowed = (seg_q[...] == seg_k[...]) & (pos_k[...] <= pos_q[...])
    scores = jnp.where(allowed, scores * factor, NEGATIVE)
    powers = jnp.exp(scores - jnp.max(scores, axis=-1, keepdims=True))
    return query, keys, powers / jnp.sum(powers, axis=-1, keepdims=True)


def attend_kernel(
    factor, qn_ref, qr_ref, kv_ref, kr_ref, seg_q, seg_k, pos_q, pos_k, out_ref
):
    _, _, probs = scores_of(
        qn_ref, qr_ref, kv_ref, kr_ref, seg_q, seg_k, pos_q, pos_k, pl.program_id(1), factor
    )
    out_ref[...] = jnp.dot(
        probs.astype(BF16), kv_ref[:, NOPE:], preferred_element_type=F32
    ).astype(BF16)


def attend_back_kernel(
    factor,
    qn_ref,
    qr_ref,
    kv_ref,
    kr_ref,
    seg_q,
    seg_k,
    pos_q,
    pos_k,
    top_ref,
    grad_qn_ref,
    grad_qr_ref,
    grad_kv_ref,
    grad_kr_ref,
    sum_ref,
):
    step, head = pl.program_id(0), pl.program_id(1)
    last = pl.num_programs(0) - 1
    query, keys, probs = scores_of(
        qn_ref, qr_ref, kv_ref, kr_ref, seg_q, seg_k, pos_q, pos_k, head, factor
    )
    top = top_ref[...]
    grad_probs = lax.dot_general(
        top, kv_ref[:, NOPE:], (((1,), (1,)), ((), ())), preferred_element_type=F32
    )
    mean = jnp.sum(probs * grad_probs, axis=-1, keepdims=True)
    grad_scores = (probs * (grad_probs - mean)).astype(BF16)
    low = probs.astype(BF16)
    grad_query = jnp.dot(grad_scores, keys, preferred_element_type=F32) * factor
    grad_qn_ref[...] = grad_query[:, :NOPE].astype(BF16)
    turned = grad_query[:, NOPE:]
    lane = lax.broadcasted_iota(jnp.int32, turned.shape, 1)
    turned = jnp.where(lane // ROPE == head, turned, 0.0)
    grad_keys = left_product(grad_scores, query) * factor
    grad_values = left_product(low, top)

    @pl.when(head == 0)
    def _():
        grad_qr_ref[...] = turned

    @pl.when(head != 0)
    def _():
        grad_qr_ref[...] += turned

    @pl.when((step == 0) & (head == 0))
    def _():
        grad_kr_ref[...] = grad_keys[:, NOPE:]

    @pl.when((step != 0) | (head != 0))
    def _():
        grad_kr_ref[...] += grad_keys[:, NOPE:]

    @pl.when(step == 0)
    def _():
        sum_ref[head, :, :NOPE] = grad_keys[:, :NOPE]
        sum_ref[head, :, NOPE:] = grad_values

    @pl.when(step != 0)
    def _():
        sum_ref[head, :, :NOPE] += grad_keys[:, :NOPE]
        sum_ref[head, :, NOPE:] += grad_values

    @pl.when(step == last)
    def _():
        grad_kv_ref[head] = sum_ref[head].astype(BF16)


def attend_specs(length, heads, turned, block):
    return [
        pl.BlockSpec((block, NOPE), lambda i, h: (i, h)),
        pl.BlockSpec((block, turned), lambda i, h: (i, 0)),
        pl.BlockSpec((length, NOPE + VDIM), lambda i, h: (0, h)),
        pl.BlockSpec((length, turned), lambda i, h: (0, 0)),
        pl.BlockSpec((block, 1), lambda i, h: (i, 0)),
        pl.BlockSpec((1, length), lambda i, h: (0, 0)),
        pl.BlockSpec((block, 1), lambda i, h: (i, 0)),
        pl.BlockSpec((1, length), lambda i, h: (0, 0)),
    ]


def attend_stage(factor, heads, inputs):
    length, turned = inputs[1].shape
    block = min(length, 256)
    return pl.pallas_call(
        functools.partial(attend_kernel, factor),
        grid=(length // block, heads),
        in_specs=attend_specs(length, heads, turned, block),
        out_specs=pl.BlockSpec((block, VDIM), lambda i, h: (i, h)),
        out_shape=jax.ShapeDtypeStruct((length, heads * VDIM), BF16),
        compiler_params=pltpu.CompilerParams(vmem_limit_bytes=VMEM_LIMIT),
        cost_estimate=pl.CostEstimate(
            flops=2 * heads * length * length * 384,
            bytes_accessed=8 * length * heads * NOPE,
            transcendentals=heads * length * length,
        ),
        name="attend_stage",
    )(*inputs)


def attend_back_stage(factor, heads, inputs, top):
    length, turned = inputs[1].shape
    block = min(length, 256)
    return pl.pallas_call(
        functools.partial(attend_back_kernel, factor),
        grid=(length // block, heads),
        in_specs=attend_specs(length, heads, turned, block)
        + [pl.BlockSpec((block, VDIM), lambda i, h: (i, h))],
        out_specs=[
            pl.BlockSpec((block, NOPE), lambda i, h: (i, h)),
            pl.BlockSpec((block, turned), lambda i, h: (i, 0)),
            pl.BlockSpec((heads, length, NOPE + VDIM), lambda i, h: (0, 0, 0)),
            pl.BlockSpec((length, turned), lambda i, h: (0, 0)),
        ],
        out_shape=[
            jax.ShapeDtypeStruct((length, heads * NOPE), BF16),
            jax.ShapeDtypeStruct((length, turned), F32),
            jax.ShapeDtypeStruct((heads, length, NOPE + VDIM), BF16),
            jax.ShapeDtypeStruct((length, turned), F32),
        ],
        scratch_shapes=[pltpu.VMEM((heads, length, NOPE + VDIM), F32)],
        compiler_params=pltpu.CompilerParams(vmem_limit_bytes=VMEM_LIMIT),
        cost_estimate=pl.CostEstimate(
            flops=2 * heads * length * length * 1024,
            bytes_accessed=16 * length * heads * NOPE,
            transcendentals=heads * length * length,
        ),
        name="attend_back_stage",
    )(*inputs, top)


def whole_spec(array):
    return pl.BlockSpec(
        array.shape, lambda i, *_: (0,) * array.ndim, pipeline_mode=pl.Buffered(1)
    )


def rows_spec(size, columns):
    return pl.BlockSpec((size, columns), lambda i, *_: (i, 0))


def forward_stage(place, slots, tokens, weights, capacity, experts, hidden, lanes):
    devices, _, rows = slots.shape
    blocks = 2 * lax.axis_size("fsdp")
    steps = devices // blocks
    width = tokens.shape[1]
    half = weights[1].shape[1]
    count = blocks * capacity
    sizes = [(count, width)] + [(count, half)] * 4 + [(blocks * rows, lanes)] * 3
    return pl.pallas_call(
        functools.partial(forward_kernel, blocks, capacity, experts, hidden),
        grid_spec=pltpu.PrefetchScalarGridSpec(
            num_scalar_prefetch=1,
            grid=(steps,),
            in_specs=[
                pl.BlockSpec((blocks, 1, rows), lambda i, *_: (i, 0, 0)),
                rows_spec(blocks * rows, width),
                *[whole_spec(weight) for weight in weights],
            ],
            out_specs=[rows_spec(*size) for size in sizes],
        ),
        out_shape=[
            jax.ShapeDtypeStruct((steps * size, columns), BF16) for size, columns in sizes
        ],
        compiler_params=pltpu.CompilerParams(vmem_limit_bytes=VMEM_LIMIT),
        cost_estimate=pl.CostEstimate(
            flops=devices * 4 * width * (capacity * half + rows * lanes),
            bytes_accessed=3 * devices * rows * width,
            transcendentals=devices * capacity * half,
        ),
        name="forward_stage",
    )(place, slots, tokens, *weights)


def backward_stage(slots, top, saved, weights, capacity):
    devices, _, rows = slots.shape
    blocks = 2 * lax.axis_size("fsdp")
    steps = devices // blocks
    width = top.shape[1]
    lanes, half = (weight.shape[1] for weight in weights)
    count = blocks * capacity
    slots_spec = pl.BlockSpec((blocks, 1, rows), lambda i, *_: (i, 0, 0))
    sizes = [(count, width)] + [(count, half)] * 2 + [(blocks * rows, 2 * lanes)]
    return pl.pallas_call(
        functools.partial(backward_kernel, blocks, capacity),
        grid=(steps,),
        in_specs=[
            slots_spec,
            rows_spec(blocks * rows, width),
            *[rows_spec(count, half) for _ in range(3)],
            *[rows_spec(blocks * rows, lanes) for _ in range(2)],
            *[whole_spec(weight) for weight in weights],
        ],
        out_specs=[rows_spec(*size) for size in sizes] + [slots_spec],
        out_shape=[
            jax.ShapeDtypeStruct((steps * size, columns), BF16) for size, columns in sizes
        ]
        + [jax.ShapeDtypeStruct(slots.shape, F32)],
        compiler_params=pltpu.CompilerParams(vmem_limit_bytes=VMEM_LIMIT),
        cost_estimate=pl.CostEstimate(
            flops=devices * 2 * width * (capacity * half + rows * lanes),
            bytes_accessed=4 * devices * rows * width,
            transcendentals=0,
        ),
        name="backward_stage",
    )(slots, top, *saved, *weights)


def combine_kernel(blocks, capacity, cuts, count, place_ref, slots_ref, *refs):
    lefts, rights = refs[:count], refs[count : 2 * count]
    shared_ref, shared_weight_ref = refs[2 * count : 2 * count + 2]
    outs = refs[2 * count + 2 : -1]
    rows_ref = refs[-1]
    rows = slots_ref.shape[-1]
    total = None
    for left, right in zip(lefts, rights):
        term = jnp.dot(left[...], right[...], preferred_element_type=F32)
        total = term if total is None else total + term
    rows_ref[...] = total.astype(BF16)
    half = blocks // 2
    for side in range(2):
        core = place_ref[1] ^ side
        for block in range(half):
            index = core * half + block
            chosen = one_hot(slots_ref[index], capacity).astype(BF16)
            there = pl.ds(pl.multiple_of(index * capacity, capacity), capacity)
            own = pl.ds(pl.multiple_of(index * rows, rows), rows)
            value = lax.dot_general(
                chosen,
                rows_ref[there, :],
                (((0,), (0,)), ((), ())),
                preferred_element_type=F32,
            ) + jnp.dot(
                shared_ref[own, :], shared_weight_ref[...], preferred_element_type=F32
            )
            value = value.astype(BF16)
            for part, (low, high) in enumerate(cuts):
                outs[2 * side + part][pl.ds(block * rows, rows), :] = value[:, low:high]


def combine_stage(place, slots, lefts, rights, shared, shared_weight, capacity):
    devices, _, rows = slots.shape
    blocks = 2 * lax.axis_size("fsdp")
    steps = devices // blocks
    width = rights[0].shape[1]
    cuts = halves_of(width)
    half = blocks // 2 * rows

    out_specs = [
        pl.BlockSpec((half, high - low), lambda i, place: (i ^ place[2], 0))
        for _ in range(2)
        for low, high in cuts
    ]
    out_shape = [
        jax.ShapeDtypeStruct((steps * half, high - low), BF16)
        for _ in range(2)
        for low, high in cuts
    ]
    flops = 2 * devices * width * (
        capacity * sum(left.shape[1] for left in lefts) + rows * (capacity + shared.shape[1])
    )
    outs = pl.pallas_call(
        functools.partial(combine_kernel, blocks, capacity, cuts, len(lefts)),
        grid_spec=pltpu.PrefetchScalarGridSpec(
            num_scalar_prefetch=1,
            grid=(steps,),
            in_specs=[
                pl.BlockSpec((blocks, 1, rows), lambda i, *_: (i, 0, 0)),
                *[rows_spec(blocks * capacity, left.shape[1]) for left in lefts],
                *[whole_spec(right) for right in rights],
                rows_spec(blocks * rows, shared.shape[1]),
                whole_spec(shared_weight),
            ],
            out_specs=out_specs,
            scratch_shapes=[pltpu.VMEM((blocks * capacity, width), BF16)],
        ),
        out_shape=out_shape,
        compiler_params=pltpu.CompilerParams(vmem_limit_bytes=VMEM_LIMIT),
        cost_estimate=pl.CostEstimate(
            flops=flops, bytes_accessed=devices * rows * width * 3, transcendentals=0
        ),
        name="combine_stage",
    )(place, slots, *lefts, *rights, shared, shared_weight)
    return outs[:2], outs[2:]


def per_device(
    tokens_in,
    segments,
    routes,
    cotangent,
    g_attn,
    g_kv,
    g_moe,
    w_query,
    w_kv_down,
    w_kv_up,
    w_out,
    w_router,
    w_shared_gate,
    w_shared_up,
    w_shared_down,
    w_expert_gate,
    w_expert_up,
    w_expert_down,
):
    micro_count, rows, width = tokens_in.shape
    seqs, line = lax.axis_size("seq"), lax.axis_size("fsdp")
    devices = seqs * line
    length = rows * seqs
    experts = devices // 2
    picked = routes.shape[2]
    capacity = max(2, rows * picked * 4 // (experts * 3))
    capacity = -(-capacity // 16) * 16
    heads = HEADS // seqs
    me_seq = lax.axis_index("seq")
    me = me_seq * line + lax.axis_index("fsdp")
    expert = me // 2
    factor = (NOPE + ROPE) ** (-0.5)
    frequency = THETA ** (-jnp.arange(ROPE // 2, dtype=F32) * 2.0 / ROPE)
    order = jnp.arange(seqs)
    ranks = (order ^ me_seq) >> 1 | ((order ^ me_seq) & 1) * (seqs // 2)
    order = me_seq ^ ((order % (seqs // 2)) * 2 + order // (seqs // 2))

    def to_relative(value):
        return value.reshape(seqs, rows, -1)[order].reshape(value.shape)

    def to_absolute(value):
        return value.reshape(seqs, rows, -1)[ranks].reshape(value.shape)

    places = (order[:, None] * rows + jnp.arange(rows)[None, :]).reshape(-1)
    angles = places.astype(F32)[:, None] * frequency[None, :]
    own_angles = angles[:rows]
    micros = range(micro_count)

    slots = Slots()
    place = jnp.stack([expert, me_seq & 1, me_seq >> 1]).astype(jnp.int32)

    piece = w_kv_down.shape[0]
    kv_columns = w_kv_down.shape[1]
    small = jnp.concatenate(
        [
            w_kv_down,
            w_router,
            g_attn[:, None],
            g_moe[:, None],
            jnp.pad(g_kv, (0, piece - g_kv.shape[0]))[:, None],
            routes.reshape(piece, -1).astype(BF16),
        ],
        axis=1,
    )
    small = lax.all_gather(small, BOTH, axis=0, tiled=True)

    query_width = heads * (NOPE + ROPE)
    out_width = heads * VDIM
    for_query = w_query.reshape(piece, seqs, heads, NOPE + ROPE)
    for_query = jnp.concatenate(
        [
            for_query[..., :NOPE].reshape(piece, seqs, -1),
            for_query[..., NOPE:].reshape(piece, seqs, -1),
        ],
        axis=2,
    ).transpose(1, 0, 2)
    for_out = w_out.reshape(seqs, out_width, piece).transpose(0, 2, 1)
    for_heads = jnp.concatenate([for_query, for_out], axis=2)
    for_heads = jnp.broadcast_to(
        for_heads[:, None], (seqs, line, piece, query_width + out_width)
    ).reshape(devices, piece, query_width + out_width)
    ready, for_heads = lax.optimization_barrier((tokens_in, for_heads))
    tokens = [Flow(gather_seq(ready[micro])) for micro in micros]
    for_heads = Flow(exchange(for_heads, BOTH))
    up_weight = Flow(
        exchange(jnp.broadcast_to(w_kv_up[None], (line,) + w_kv_up.shape), "fsdp")
    )
    hidden = w_shared_gate.shape[1] // devices

    def pack_shared(gate, up, down):
        return jnp.concatenate(
            [
                gate.reshape(piece, devices, hidden).transpose(1, 0, 2),
                up.reshape(piece, devices, hidden).transpose(1, 0, 2),
                down.reshape(devices, hidden, piece).transpose(0, 2, 1),
            ],
            axis=2,
        )

    for_shared = slots.run(tokens, pack_shared, w_shared_gate, w_shared_up, w_shared_down)
    for_shared = Flow(exchange(for_shared, BOTH))
    slots.run([*tokens, for_heads, up_weight])
    tops = [lax.all_gather(slots.tie(cotangent[0]), BOTH, axis=0, tiled=True), None]
    slots.finish(tokens[0], tokens[1])
    slots.finish(tokens[1])
    (small,) = slots.run([], lambda *given: given, small)
    for_heads, up_weight = for_heads.value, up_weight.value
    for_heads = for_heads.reshape(width, query_width + out_width)
    query_weight = for_heads[:, :query_width]
    out_weight = for_heads[:, query_width:]
    up_weight = up_weight.transpose(1, 0, 2).reshape(KVR, -1)
    down_weight = small[:, :kv_columns]
    router_weight = small[:, kv_columns : kv_columns + experts]
    last = kv_columns + experts
    gain_one = small[:, last].astype(F32)
    gain_two = small[:, last + 1].astype(F32)
    gain_latent = small[:, last + 2].reshape(devices, piece)[:, : g_kv.shape[0]].reshape(-1)
    routes_all = small[:, last + 3 :].astype(jnp.int32).reshape((devices,) + routes.shape)
    gain_latent = gain_latent.astype(F32)

    def projections(tokens):
        unit_one, _ = normed(tokens.astype(F32))
        normed_one = (unit_one * gain_one).astype(BF16)
        query_raw = product(normed_one, query_weight)
        query = query_raw[:, : heads * NOPE].astype(BF16)
        turned = query_raw[:, heads * NOPE :].reshape(length, heads, ROPE)
        turned = turned_lanes(rotate(turned, angles[:, None, :]).reshape(length, -1))
        latent = product(normed_one, down_weight)
        unit_latent, factor_latent = normed(latent[:, :KVR])
        latent_norm = (unit_latent * gain_latent).astype(BF16)
        key_rope = rotate(latent[:, KVR:], angles).astype(BF16)
        key_value = product(latent_norm, up_weight).astype(BF16)
        key_rope = turned_lanes(jnp.tile(key_rope, (1, heads)))
        return (
            normed_one,
            latent_norm,
            (query, turned, key_value, key_rope),
            unit_latent[:rows],
            factor_latent[:rows],
        )

    def turned_lanes(value):
        return jnp.pad(value.astype(BF16), ((0, 0), (0, -value.shape[1] % 128)))

    def marks_of(micro):
        segment = segments[micro].reshape(seqs, rows)[order].reshape(-1)
        return segment[:, None], segment[None, :], places[:, None], places[None, :]

    def attend(micro, query):
        inputs = (query,) + projected[micro][2][1:] + marks[micro]
        attended = attend_stage(factor, heads, inputs)
        return attended, right_product(attended, out_weight).astype(BF16)

    def home_forward(micro, summed):
        residual = tokens_in[micro].astype(F32) + summed.astype(F32)
        unit_two, factor_two = normed(residual)
        normed_two = (unit_two * gain_two).astype(BF16)
        return residual, unit_two, factor_two, normed_two

    marks = [marks_of(micro) for micro in micros]
    projected = [None, None]
    attended = [None, None]
    residuals = [None, None]
    normed_alls = [None, None]
    projected[0] = slots.run([], projections, tokens[0].value)
    attended[0] = slots.run([], functools.partial(attend, 0), projected[0][2][0])
    summed = Flow(scatter_seq(attended[0][1], rows))
    projected[1] = slots.run([summed, for_shared], projections, tokens[1].value)
    attended[1] = slots.run([summed], functools.partial(attend, 1), projected[1][2][0])
    summed_two = Flow(scatter_seq(attended[1][1], rows))
    slots.finish(summed, summed_two)
    residuals[0] = home_forward(0, summed.value)
    first, tops[0] = lax.optimization_barrier((residuals[0][3], tops[0]))
    normed_alls[0] = lax.all_gather(first, BOTH, axis=0, tiled=True)
    slots.finish(summed_two)
    residuals[1] = home_forward(1, summed_two.value)
    normed_alls[1] = lax.all_gather(residuals[1][3], BOTH, axis=0, tiled=True)
    top_flow = Flow(gather_all(slots.tie(cotangent[1]), place))
    for _ in range(line):
        slots.run([top_flow])

    lanes = -(-(hidden + experts) // 128) * 128

    def padded(parts):
        parts = jnp.concatenate(parts, axis=1)
        return jnp.pad(parts, ((0, 0), (0, lanes - parts.shape[1])))

    for_shared = for_shared.value.reshape(width, 3 * hidden)
    shared_gate = for_shared[:, :hidden]
    shared_up = for_shared[:, hidden : 2 * hidden]
    shared_down = padded([for_shared[:, 2 * hidden :]])
    wide_weight = jnp.concatenate(
        [padded([shared_gate, router_weight]), padded([shared_up])], axis=1
    )
    shared_in = jnp.concatenate([padded([shared_gate]), padded([shared_up])], axis=1)
    gate_weight = w_expert_gate[0]
    up_expert = w_expert_up[0]
    down_expert = w_expert_down[0]
    forward_weights = (wide_weight, gate_weight, up_expert)
    backward_weights = (shared_down, down_expert.T)
    transposed = (gate_weight.T, up_expert.T, shared_in.T, shared_down.T)

    def slots_of(micro):
        hit = jnp.any(routes_all[:, micro] == expert, axis=-1)
        rank = jnp.cumsum(hit.astype(jnp.int32), axis=1) - 1
        return jnp.where(hit, rank, -1)[:, None, :]

    def forward_of(seats, tokens):
        return forward_stage(
            place, seats, tokens, forward_weights, capacity, experts, hidden, lanes
        )

    def backward_of(seats, top, made):
        return backward_stage(
            seats, top, (made[2], made[3], made[4], made[6], made[7]), backward_weights, capacity
        )

    def grads_to_tokens(seats, back):
        return combine_stage(
            place, seats, back[1:3], transposed[:2], back[3], transposed[2], capacity
        )

    def outputs_to_tokens(seats, made):
        return combine_stage(
            place, seats, made[1:2], (down_expert,), made[5], transposed[3], capacity
        )

    def routed_pairs(made, back):
        return (made[0], back[1]), (made[0], back[2]), (made[1], back[0])

    def routed_grads(*pairs):
        return tuple(left_product(*pair) for pair in pairs)

    def shared_grads_of(tokens, top, made, back):
        return left_product(tokens, back[3]), left_product(top, made[5])

    def added(function):
        def call(before, *values):
            return tuple(old + new for old, new in zip(before, function(*values)))

        return call

    def gate_grads_home(made):
        return Flow(exchange(made.reshape(devices, rows), BOTH))

    def home_backward(micro, grad_two, gate_grad):
        _, unit_two, factor_two, normed_two = residuals[micro]
        logits = product(normed_two, router_weight)
        shifted = jnp.exp(logits - jnp.max(logits, axis=-1, keepdims=True))
        router = shifted / jnp.sum(shifted, axis=-1, keepdims=True)
        router_in = jnp.sum(gate_grad.reshape(experts, 2, rows), axis=1).T
        grad_logits = (
            router * (router_in - jnp.sum(router * router_in, axis=-1, keepdims=True))
        ).astype(BF16)
        grad_two = grad_two + right_product(grad_logits, router_weight)
        grad_residual = cotangent[micro].astype(F32) + norm_back(
            grad_two * gain_two, unit_two, factor_two
        )
        return (
            grad_residual,
            left_product(normed_two, grad_logits),
            jnp.sum(grad_two * unit_two, axis=0),
        )

    def attend_backward(micro, grad_attn_out):
        grad_attended = to_relative(product(grad_attn_out, out_weight).astype(BF16))
        inputs = projected[micro][2] + marks[micro]
        return attend_back_stage(factor, heads, inputs, grad_attended)

    def latents_backward(grad_key_value, grad_rope):
        grad_rope = jnp.sum(grad_rope[:, : heads * ROPE].reshape(length, heads, ROPE), axis=1)
        grad_key_value = grad_key_value.transpose(1, 0, 2).reshape(length, -1)
        grad_latent_part = right_product(grad_key_value, up_weight)
        part = jnp.concatenate([grad_latent_part, grad_rope], axis=1).astype(BF16)
        return part, grad_key_value

    def queries_backward(grad_query, grad_turned):
        grad_turned = grad_turned[:, : heads * ROPE].reshape(length, heads, ROPE)
        grad_turned = rotate(grad_turned, -angles[:, None, :]).reshape(length, -1)
        grad_query_raw = jnp.concatenate([grad_query, grad_turned.astype(BF16)], axis=1)
        one_part = right_product(to_absolute(grad_query_raw), query_weight)
        return one_part.astype(BF16), grad_query_raw

    def projections_backward(grad_query, grad_turned, grad_key_value, grad_rope):
        return (
            *latents_backward(grad_key_value, grad_rope),
            *queries_backward(grad_query, grad_turned),
        )

    def head_grads(projected, attended, grad_attn_out, grad_query_raw, grad_key_value):
        return (
            left_product(projected[0], grad_query_raw),
            left_product(grad_attn_out, to_absolute(attended)),
            left_product(grad_key_value, projected[1]),
        )

    def latent_backward(back, projected):
        unit_latent, factor_latent = projected[3:]
        grad_latent_norm = back[:, :KVR].astype(F32)
        grad_compressed = norm_back(grad_latent_norm * gain_latent, unit_latent, factor_latent)
        grad_latent = jnp.concatenate(
            [grad_compressed, rotate(back[:, KVR:].astype(F32), -own_angles)], axis=-1
        ).astype(BF16)
        return grad_latent, jnp.sum(grad_latent_norm * unit_latent, axis=0)

    def input_backward(micro, back, grad_latent, grad_residual):
        unit_one, factor_one = normed(tokens_in[micro].astype(F32))
        grad_one = back.astype(F32) + right_product(grad_latent, down_weight)
        return (
            grad_residual + norm_back(grad_one * gain_one, unit_one, factor_one),
            jnp.sum(grad_one * unit_one, axis=0),
        )

    def line_blocks(value):
        return value.astype(BF16).reshape(line, -1, value.shape[-1])

    def down_grads(normed_one, latents):
        columns = lax.dynamic_slice_in_dim(
            normed_one, me_seq * (width // seqs), width // seqs, axis=1
        )
        return left_product(columns, latents)

    seats = [slots_of(micro) for micro in micros]
    made = [None, None]
    def home_and_out(micro):
        home = home_backward(micro, grads[micro].value, gate_grad[micro].value)
        return home, lax.all_gather(home[0].astype(BF16), "seq", axis=0, tiled=True)

    def attention_back(*given):
        return projections_backward(*attend_backward(*given))

    gate_grad = [None, None]
    grads = [None, None]
    sums = [None, None]
    homes = [None, None]
    attn_out = [None, None]
    backs = [None, None]
    back = [None, None]
    finals = [None, None]

    def shared_home(shared_grads):
        shared_grads = shared_grads.astype(F32)
        return (
            shared_grads[:, :, :hidden].transpose(1, 0, 2).reshape(piece, -1),
            shared_grads[:, :, hidden : 2 * hidden].transpose(1, 0, 2).reshape(piece, -1),
            shared_grads[:, :, 2 * hidden :].transpose(0, 2, 1).reshape(-1, piece),
        )

    made[0] = slots.run([], forward_of, seats[0], normed_alls[0])
    back[0] = slots.run([top_flow], backward_of, seats[0], tops[0], made[0])
    gate_grad[0] = gate_grads_home(back[0][4])
    sides = slots.run([top_flow, gate_grad[0]], grads_to_tokens, seats[0], back[0])
    grads[0] = Flow(reduce_all(*sides, rows))
    tops[1] = slots.finish(top_flow)
    sides = slots.run([grads[0]], outputs_to_tokens, seats[0], made[0])
    sums[0] = Flow(reduce_all(*sides, rows))
    routed, shared = slots.run(
        [grads[0], sums[0]],
        lambda pairs, *given: (routed_grads(*pairs), shared_grads_of(*given)),
        routed_pairs(made[0], back[0]),
        normed_alls[0],
        tops[0],
        made[0],
        back[0],
    )
    made[1] = slots.run([grads[0]], forward_of, seats[1], normed_alls[1])
    back[1] = slots.run([], backward_of, seats[1], tops[1], made[1])
    gate_grad[1] = gate_grads_home(back[1][4])
    sides = slots.run(
        [grads[0], sums[0], gate_grad[1]], grads_to_tokens, seats[1], back[1]
    )
    grads[1] = Flow(reduce_all(*sides, rows))
    slots.finish(grads[0])
    homes[0], attn_out[0] = home_and_out(0)
    sides = slots.run([grads[1], sums[0]], outputs_to_tokens, seats[1], made[1])
    sums[1] = Flow(reduce_all(*sides, rows))
    parts = slots.run(
        [grads[1], sums[0]], added(routed_grads), routed, *routed_pairs(made[1], back[1])
    )
    shared = slots.run(
        [grads[1], sums[1]],
        added(shared_grads_of),
        shared,
        normed_alls[1],
        tops[1],
        made[1],
        back[1],
    )
    shared = jnp.concatenate(
        [shared[0][:, :hidden], shared[0][:, lanes : lanes + hidden], shared[1][:, :hidden]],
        axis=1,
    )
    shared = Flow(exchange(shared.astype(BF16).reshape(devices, piece, 3 * hidden), BOTH))
    parted, grad_key_value, one_part, grad_query_raw = slots.run(
        [grads[1], sums[1]],
        lambda given: projections_backward(*attend_backward(0, given)),
        attn_out[0],
    )
    slots.finish(grads[1])
    homes[1], attn_out[1] = home_and_out(1)
    whole_part, _ = lax.optimization_barrier(
        (jnp.concatenate([one_part, to_absolute(parted)], axis=1), homes[1][0])
    )
    whole_part = lax.psum_scatter(whole_part, "seq", scatter_dimension=0, tiled=True)
    head_sums = slots.run(
        [],
        head_grads,
        projected[0],
        attended[0][0],
        attn_out[0],
        grad_query_raw,
        grad_key_value,
    )
    scored = slots.run([sums[1]], functools.partial(attend_backward, 1), attn_out[1])
    parted, grad_key_value = slots.run([shared], latents_backward, *scored[2:])
    latent_sums = Flow(scatter_seq(parted, rows))
    one_part, grad_query_raw = slots.run([latent_sums], queries_backward, *scored[:2])
    one_part = lax.psum_scatter(one_part, "seq", scatter_dimension=0, tiled=True)

    def all_head_grads(before, *given):
        query, out, up = added(head_grads)(before, *given)
        packed = jnp.concatenate([query, out], axis=1).astype(BF16)
        return packed.reshape(devices, piece, -1), line_blocks(up)

    grad_heads, grad_up = slots.run(
        [latent_sums, sums[1]],
        all_head_grads,
        head_sums,
        projected[1],
        attended[1][0],
        attn_out[1],
        grad_query_raw,
        grad_key_value,
    )
    grad_heads = Flow(exchange(grad_heads, BOTH))
    grad_up = Flow(exchange_line(grad_up))
    latents = [latent_backward(whole_part[:, width:], projected[0]), None]
    finals[0] = slots.run(
        [latent_sums],
        functools.partial(input_backward, 0),
        whole_part[:, :width],
        latents[0][0],
        homes[0][0],
    )
    slots.finish(latent_sums)
    latents[1] = latent_backward(latent_sums.value, projected[1])
    latent_flow = Flow(gather_seq(jnp.concatenate([latent[0] for latent in latents], axis=1)))
    shared_final = slots.run([latent_flow], shared_home, shared.value)
    finals[1] = slots.run(
        [latent_flow, grad_heads],
        functools.partial(input_backward, 1),
        one_part,
        latents[1][0],
        homes[1][0],
    )
    tiny = jnp.concatenate(
        [
            sum(home[1] for home in homes).reshape(devices, -1),
            sum(final[1] for final in finals).reshape(devices, -1),
            sum(home[2] for home in homes).reshape(devices, -1),
            sum(latent[1] for latent in latents).reshape(devices, -1),
        ],
        axis=1,
    )
    tiny = Flow(exchange(tiny, BOTH))
    slots.finish(latent_flow)
    grad_kv_down = sum(
        down_grads(
            projected[micro][0],
            latent_flow.value[:, micro * kv_columns : (micro + 1) * kv_columns],
        )
        for micro in micros
    )
    grad_kv_down = Flow(exchange_line(line_blocks(grad_kv_down)))
    slots.run([grad_kv_down, grad_up, tiny, grad_heads, sums[0], sums[1]])
    for flow in (sums[0], sums[1]):
        slots.finish(flow)
    outputs = [
        (residuals[micro][0] + sums[micro].value).astype(BF16) for micro in micros
    ]
    grad_kv_down = grad_kv_down.value
    grad_kv_up = grad_up.value.T
    grad_heads = grad_heads.value.reshape(seqs, line, piece, -1)
    grad_heads = jnp.sum(grad_heads.astype(F32), axis=1)
    grad_query_weight = jnp.concatenate(
        [
            grad_heads[:, :, : heads * NOPE].reshape(seqs, piece, heads, NOPE),
            grad_heads[:, :, heads * NOPE : query_width].reshape(seqs, piece, heads, ROPE),
        ],
        axis=3,
    )
    grad_query_weight = grad_query_weight.transpose(1, 0, 2, 3).reshape(piece, -1)
    grad_out_weight = grad_heads[:, :, query_width:].transpose(0, 2, 1).reshape(-1, piece)
    tiny = jnp.sum(tiny.value, axis=0)
    first = piece * experts
    return (
        jnp.stack(outputs),
        jnp.stack([final[0] for final in finals]),
        tiny[first : first + piece],
        tiny[first + 2 * piece :],
        tiny[first + piece : first + 2 * piece],
        grad_query_weight,
        grad_kv_down,
        grad_kv_up,
        grad_out_weight,
        tiny[:first].reshape(piece, experts),
        *shared_final,
        parts[0][None],
        parts[1][None],
        parts[2][None],
    )


def solution(mesh):
    return jax.shard_map(
        per_device,
        mesh=mesh,
        in_specs=(
            P("fsdp", "seq", None),
            P("fsdp", None),
            P("fsdp", "seq", None),
            P("fsdp", "seq", None),
            P(BOTH),
            P(BOTH),
            P(BOTH),
            P(BOTH, None),
            P(BOTH, None),
            P(None, BOTH),
            P(None, BOTH),
            P(BOTH, None),
            P(BOTH, None),
            P(BOTH, None),
            P(None, BOTH),
            P(BOTH, None, None),
            P(BOTH, None, None),
            P(BOTH, None, None),
        ),
        out_specs=(
            P("fsdp", "seq", None),
            P("fsdp", "seq", None),
            P(BOTH),
            P(BOTH),
            P(BOTH),
            P(BOTH, None),
            P(BOTH, None),
            P(None, BOTH),
            P(None, BOTH),
            P(BOTH, None),
            P(BOTH, None),
            P(BOTH, None),
            P(None, BOTH),
            P(BOTH, None, None),
            P(BOTH, None, None),
            P(BOTH, None, None),
        ),
        check_vma=False,
    )
```

```python
import functools

import jax
import jax.numpy as jnp
from jax import lax
from jax.experimental import pallas as pl
from jax.experimental.pallas import tpu as pltpu
from jax.sharding import PartitionSpec as P

HEADS = 16
NOPE = 128
ROPE = 64
VDIM = 128
KVR = 512

EPS = 1e-06
THETA = 10000.0
NEGATIVE = -1e30
BOTH = ("seq", "fsdp")
VMEM_LIMIT = 60 * 2**20
F32 = jnp.float32
BF16 = jnp.bfloat16


def product(left, right):
    return jnp.dot(left, right, preferred_element_type=F32)


def left_product(left, right):
    return lax.dot_general(left, right, (((0,), (0,)), ((), ())), preferred_element_type=F32)


def right_product(left, right):
    return lax.dot_general(left, right, (((1,), (1,)), ((), ())), preferred_element_type=F32)


def normed(value):
    factor = lax.rsqrt(jnp.mean(value * value, axis=-1, keepdims=True) + EPS)
    return (value * factor, factor)


def norm_back(grad_unit, unit, factor):
    return factor * (grad_unit - unit * jnp.mean(grad_unit * unit, axis=-1, keepdims=True))


def rotate(value, angles):
    middle = value.shape[-1] // 2
    cosine = jnp.cos(angles)
    sine = jnp.sin(angles)
    first = value[..., :middle]
    second = value[..., middle:]
    return jnp.concatenate(
        [first * cosine - second * sine, second * cosine + first * sine], axis=-1
    )


def silu_parts(value):
    logistic = jax.nn.sigmoid(value)
    return (value * logistic, logistic * (1.0 + value * (1.0 - logistic)))


def swap(value, bit):
    count = lax.axis_size("seq")
    return lax.ppermute(value, "seq", [(i, i ^ (1 << bit)) for i in range(count)])


def chip_bits():
    return list(range(1, lax.axis_size("seq").bit_length() - 1))


def halves_of(width):
    middle = -(-width // 256) * 128
    return ((0, middle), (middle, width))


class Flow:
    def __init__(self, steps):
        self.steps = steps
        self.value = None
        self.pending = next(steps)

    def arrive(self, arrived):
        try:
            self.pending = self.steps.send(arrived)
        except StopIteration as stop:
            self.pending = None
            self.value = stop.value


class Slots:
    def __init__(self):
        self.token = jnp.zeros((8, 128), F32)

    def tie(self, values):
        return lax.optimization_barrier((values, self.token))[0]

    def run(self, flows, compute=None, *inputs):
        flows = [flow for flow in flows if flow.pending is not None]
        pending = [flow.pending for flow in flows]
        made = compute(*self.tie(inputs)) if compute else ()
        pending, made, self.token = lax.optimization_barrier((pending, made, self.token))
        for flow, arrived in zip(flows, pending):
            flow.arrive(arrived)
        return made

    def finish(self, flow, *others):
        while flow.pending is not None:
            self.run((flow,) + others)
        return flow.value


def stacked(value, names):
    lead = len(names)
    axes = [names.index(bit) for bit in sorted(names, reverse=True)]
    value = value.transpose(axes + list(range(lead, value.ndim)))
    return value.reshape((-1,) + value.shape[lead:])


def spread(parts):
    bits = chip_bits()
    orders = (bits, bits[::-1])
    for step in range(len(bits)):
        arrived = yield [swap(part, order[step]) for part, order in zip(parts, orders)]
        parts = [jnp.stack(pair) for pair in zip(parts, arrived)]
    return [stacked(part, order[::-1]) for part, order in zip(parts, orders)]


def total_of(terms):
    return sum((term.astype(F32) for term in terms[1:]), terms[0].astype(F32))


def fold(parts):
    bits = chip_bits()
    for step in range(len(bits)):
        kept, sent = [], []
        for terms, order in zip(parts, (bits, bits[::-1])):
            axis = sorted(order[step:], reverse=True).index(order[step])
            kept.append([lax.index_in_dim(term, 0, axis, keepdims=False) for term in terms])
            send = total_of([lax.index_in_dim(term, 1, axis, keepdims=False) for term in terms])
            sent.append(swap(send.astype(BF16), order[step]))
        arrived = yield sent
        parts = [terms + [got] for terms, got in zip(kept, arrived)]
    return [total_of(terms) for terms in parts]


def gather_seq(own):
    parts = yield from spread([own[:, low:high] for low, high in halves_of(own.shape[1])])
    near = jnp.concatenate(parts, axis=-1)
    (far,) = yield [swap(near, 0)]
    return jnp.concatenate([near, far], axis=0).reshape(-1, own.shape[1])


def scatter_seq(value, rows):
    half = value.shape[0] // 2
    (far,) = yield [swap(value[half:], 0)]
    shape = (2,) * len(chip_bits()) + (rows, value.shape[1])
    terms = [value[:half].reshape(shape), far.reshape(shape)]
    parts = yield from fold(
        [[term[..., low:high] for term in terms] for low, high in halves_of(value.shape[1])]
    )
    return jnp.concatenate(parts, axis=-1)


def exchange(value, axes):
    (arrived,) = yield [lax.all_to_all(value, axes, 0, 0, tiled=True)]
    return arrived


def exchange_line(value):
    count = lax.axis_size("fsdp")
    place = lax.axis_index("fsdp")

    def piece(index):
        return lax.dynamic_index_in_dim(value, index % count, 0, keepdims=False)

    arrived = yield [
        lax.ppermute(
            piece(place + turn), "fsdp", [(i, (i + turn) % count) for i in range(count)]
        )
        for turn in range(1, count)
    ]
    return sum((part.astype(F32) for part in arrived), piece(place).astype(F32))


def line_gather(own):
    count = lax.axis_size("fsdp")
    ups, downs = [], []
    up = down = own
    for step in range(1, count):
        up, down = yield [
            lax.ppermute(up, "fsdp", [(i, i + 1) for i in range(step - 1, count - 1)]),
            lax.ppermute(down, "fsdp", [(i, i - 1) for i in range(1, count - step + 1)]),
        ]
        ups.append(up)
        downs.append(down)
    around = jnp.stack(ups[::-1] + [own] + downs)
    return lax.dynamic_slice_in_dim(around, count - 1 - lax.axis_index("fsdp"), count, 0)


def gather_all(own, place):
    width = own.shape[1]
    block = yield from line_gather(own)
    block = block.reshape(-1, width)
    near = [block[:, low:high] for low, high in halves_of(width)]
    fresh, far = near, None
    bits = chip_bits()
    orders = (bits, bits[::-1])
    for step in range(len(bits)):
        arrived = yield [swap(part, order[step]) for part, order in zip(near, orders)] + [
            swap(part, 0) for part in fresh
        ]
        fresh, crossed = arrived[:2], arrived[2:]
        near = [jnp.stack(pair) for pair in zip(near, fresh)]
        far = crossed if far is None else [jnp.stack(pair) for pair in zip(far, crossed)]
    crossed = yield [swap(part, 0) for part in fresh]
    far = [jnp.stack(pair) for pair in zip(far, crossed)]
    parts = [stacked(part, order[::-1]) for part, order in zip(near + far, orders + orders)]
    return assemble(place, parts)


def reduce_all(keeps, sends, rows):
    arrived = yield [swap(send, 0) for send in sends]
    shape = (2,) * len(chip_bits()) + (lax.axis_size("fsdp"), rows, keeps[0].shape[-1])
    parts = yield from fold(
        [[keep.reshape(shape), got.reshape(shape)] for keep, got in zip(keeps, arrived)]
    )
    parts = [part.astype(BF16) for part in parts]
    return (yield from exchange_line(jnp.concatenate(parts, axis=-1)))


def assemble_kernel(place_ref, low_ref, high_ref, other_low_ref, other_high_ref, out_ref):
    count, middle = low_ref.shape[1:]
    core = place_ref[1]
    own = pl.ds(pl.multiple_of(core * count, count), count)
    other = pl.ds(pl.multiple_of((1 - core) * count, count), count)
    out_ref[own, :middle] = low_ref[0]
    out_ref[own, middle:] = high_ref[0]
    out_ref[other, :middle] = other_low_ref[0]
    out_ref[other, middle:] = other_high_ref[0]


def assemble(place, parts):
    chips, count, _ = parts[0].shape
    width = parts[0].shape[2] + parts[1].shape[2]
    return pl.pallas_call(
        assemble_kernel,
        grid_spec=pltpu.PrefetchScalarGridSpec(
            num_scalar_prefetch=1,
            grid=(chips,),
            in_specs=[
                pl.BlockSpec((1,) + part.shape[1:], lambda i, place: (i ^ place[2], 0, 0))
                for part in parts
            ],
            out_specs=pl.BlockSpec((2 * count, width), lambda i, _: (i, 0)),
        ),
        out_shape=jax.ShapeDtypeStruct((2 * chips * count, width), BF16),
        compiler_params=pltpu.CompilerParams(vmem_limit_bytes=VMEM_LIMIT),
        cost_estimate=pl.CostEstimate(
            flops=0, bytes_accessed=8 * chips * count * width, transcendentals=0
        ),
        name="assemble",
    )(place, *parts)


def one_hot(slots, capacity):
    rows = slots.shape[-1]
    return lax.broadcasted_iota(jnp.int32, (capacity, rows), 0) == slots


def forward_kernel(
    blocks,
    capacity,
    experts,
    hidden,
    place_ref,
    slots_ref,
    tokens_ref,
    wide_ref,
    gate_ref,
    up_ref,
    taken_ref,
    hidden_ref,
    to_pre_ref,
    to_up_ref,
    made_ref,
    shared_hidden_ref,
    shared_to_pre_ref,
    shared_to_up_ref,
):
    rows = slots_ref.shape[-1]
    lanes = shared_hidden_ref.shape[-1]
    expert = place_ref[0]
    wide = jnp.dot(tokens_ref[...], wide_ref[...], preferred_element_type=F32)
    first = wide[:, :lanes]
    second = wide[:, lanes:]
    silu, slope = silu_parts(first)
    shared_hidden_ref[...] = (silu * second).astype(BF16)
    shared_to_pre_ref[...] = (second * slope).astype(BF16)
    shared_to_up_ref[...] = silu.astype(BF16)
    lane = lax.broadcasted_iota(jnp.int32, first.shape, 1)
    logits = jnp.where((lane >= hidden) & (lane < hidden + experts), first, NEGATIVE)
    powers = jnp.exp(logits - jnp.max(logits, axis=-1, keepdims=True))
    total = jnp.sum(powers, axis=-1, keepdims=True)
    gates = jnp.sum(jnp.where(lane == hidden + expert, powers, 0.0), axis=-1, keepdims=True)
    gates = jnp.broadcast_to(gates / total, first.shape)
    slot_gates = []
    for block in range(blocks):
        chosen = one_hot(slots_ref[block], capacity)
        taken_ref[pl.ds(block * capacity, capacity), :] = jnp.dot(
            chosen.astype(BF16),
            tokens_ref[pl.ds(block * rows, rows), :],
            preferred_element_type=F32,
        ).astype(BF16)
        slot_gates.append(
            jnp.dot(
                chosen.astype(F32),
                gates[block * rows : (block + 1) * rows],
                precision=lax.Precision.HIGHEST,
                preferred_element_type=F32,
            )[:, :1]
        )
    slot_gates = jnp.concatenate(slot_gates, axis=0)
    gate_pre = jnp.dot(taken_ref[...], gate_ref[...], preferred_element_type=F32)
    up_pre = jnp.dot(taken_ref[...], up_ref[...], preferred_element_type=F32)
    swish, slope = silu_parts(gate_pre)
    made = swish * up_pre
    made_ref[...] = made.astype(BF16)
    hidden_ref[...] = (made * slot_gates).astype(BF16)
    to_pre_ref[...] = (up_pre * slope * slot_gates).astype(BF16)
    to_up_ref[...] = (swish * slot_gates).astype(BF16)


def backward_kernel(
    blocks,
    capacity,
    slots_ref,
    top_ref,
    to_pre_ref,
    to_up_ref,
    made_ref,
    shared_to_pre_ref,
    shared_to_up_ref,
    shared_ref,
    down_ref,
    taken_top_ref,
    pre_ref,
    post_ref,
    shared_grad_ref,
    gate_grad_ref,
):
    rows = slots_ref.shape[-1]
    lanes = shared_ref.shape[-1]
    back = jnp.dot(top_ref[...], shared_ref[...], preferred_element_type=F32)
    shared_grad_ref[:, :lanes] = (back * shared_to_pre_ref[...].astype(F32)).astype(BF16)
    shared_grad_ref[:, lanes:] = (back * shared_to_up_ref[...].astype(F32)).astype(BF16)
    for block in range(blocks):
        chosen = one_hot(slots_ref[block], capacity).astype(BF16)
        taken_top_ref[pl.ds(block * capacity, capacity), :] = jnp.dot(
            chosen, top_ref[pl.ds(block * rows, rows), :], preferred_element_type=F32
        ).astype(BF16)
    grad = jnp.dot(taken_top_ref[...], down_ref[...], preferred_element_type=F32)
    pre_ref[...] = (grad * to_pre_ref[...].astype(F32)).astype(BF16)
    post_ref[...] = (grad * to_up_ref[...].astype(F32)).astype(BF16)
    slot_grads = jnp.sum(made_ref[...].astype(F32) * grad, axis=-1, keepdims=True)
    for block in range(blocks):
        chosen = one_hot(slots_ref[block], capacity)
        gate_grad_ref[block] = jnp.sum(
            jnp.where(chosen, slot_grads[block * capacity : (block + 1) * capacity], 0.0),
            axis=0,
            keepdims=True,
        )


def scores_of(qn_ref, qr_ref, kv_ref, kr_ref, seg_q, seg_k, pos_q, pos_k, head, factor):
    lane = lax.broadcasted_iota(jnp.int32, qr_ref.shape, 1)
    turned = jnp.where(lane // ROPE == head, qr_ref[...], jnp.zeros((), BF16))
    query = jnp.concatenate([qn_ref[...], turned], axis=1)
    keys = jnp.concatenate([kv_ref[:, :NOPE], kr_ref[...]], axis=1)
    scores = lax.dot_general(
        query, keys, (((1,), (1,)), ((), ())), preferred_element_type=F32
    )
    allowed = (seg_q[...] == seg_k[...]) & (pos_k[...] <= pos_q[...])
    scores = jnp.where(allowed, scores * factor, NEGATIVE)
    powers = jnp.exp(scores - jnp.max(scores, axis=-1, keepdims=True))
    return query, keys, powers / jnp.sum(powers, axis=-1, keepdims=True)


def attend_kernel(
    factor, qn_ref, qr_ref, kv_ref, kr_ref, seg_q, seg_k, pos_q, pos_k, out_ref
):
    _, _, probs = scores_of(
        qn_ref, qr_ref, kv_ref, kr_ref, seg_q, seg_k, pos_q, pos_k, pl.program_id(1), factor
    )
    out_ref[...] = jnp.dot(
        probs.astype(BF16), kv_ref[:, NOPE:], preferred_element_type=F32
    ).astype(BF16)


def attend_back_kernel(
    factor,
    qn_ref,
    qr_ref,
    kv_ref,
    kr_ref,
    seg_q,
    seg_k,
    pos_q,
    pos_k,
    top_ref,
    grad_qn_ref,
    grad_qr_ref,
    grad_kv_ref,
    grad_kr_ref,
    sum_ref,
):
    step, head = pl.program_id(0), pl.program_id(1)
    last = pl.num_programs(0) - 1
    query, keys, probs = scores_of(
        qn_ref, qr_ref, kv_ref, kr_ref, seg_q, seg_k, pos_q, pos_k, head, factor
    )
    top = top_ref[...]
    grad_probs = lax.dot_general(
        top, kv_ref[:, NOPE:], (((1,), (1,)), ((), ())), preferred_element_type=F32
    )
    mean = jnp.sum(probs * grad_probs, axis=-1, keepdims=True)
    grad_scores = (probs * (grad_probs - mean)).astype(BF16)
    low = probs.astype(BF16)
    grad_query = jnp.dot(grad_scores, keys, preferred_element_type=F32) * factor
    grad_qn_ref[...] = grad_query[:, :NOPE].astype(BF16)
    turned = grad_query[:, NOPE:]
    lane = lax.broadcasted_iota(jnp.int32, turned.shape, 1)
    turned = jnp.where(lane // ROPE == head, turned, 0.0)
    grad_keys = left_product(grad_scores, query) * factor
    grad_values = left_product(low, top)

    @pl.when(head == 0)
    def _():
        grad_qr_ref[...] = turned

    @pl.when(head != 0)
    def _():
        grad_qr_ref[...] += turned

    @pl.when((step == 0) & (head == 0))
    def _():
        grad_kr_ref[...] = grad_keys[:, NOPE:]

    @pl.when((step != 0) | (head != 0))
    def _():
        grad_kr_ref[...] += grad_keys[:, NOPE:]

    @pl.when(step == 0)
    def _():
        sum_ref[head, :, :NOPE] = grad_keys[:, :NOPE]
        sum_ref[head, :, NOPE:] = grad_values

    @pl.when(step != 0)
    def _():
        sum_ref[head, :, :NOPE] += grad_keys[:, :NOPE]
        sum_ref[head, :, NOPE:] += grad_values

    @pl.when(step == last)
    def _():
        grad_kv_ref[head] = sum_ref[head].astype(BF16)


def attend_specs(length, heads, turned, block):
    return [
        pl.BlockSpec((block, NOPE), lambda i, h: (i, h)),
        pl.BlockSpec((block, turned), lambda i, h: (i, 0)),
        pl.BlockSpec((length, NOPE + VDIM), lambda i, h: (0, h)),
        pl.BlockSpec((length, turned), lambda i, h: (0, 0)),
        pl.BlockSpec((block, 1), lambda i, h: (i, 0)),
        pl.BlockSpec((1, length), lambda i, h: (0, 0)),
        pl.BlockSpec((block, 1), lambda i, h: (i, 0)),
        pl.BlockSpec((1, length), lambda i, h: (0, 0)),
    ]


def attend_stage(factor, heads, inputs):
    length, turned = inputs[1].shape
    block = min(length, 256)
    return pl.pallas_call(
        functools.partial(attend_kernel, factor),
        grid=(length // block, heads),
        in_specs=attend_specs(length, heads, turned, block),
        out_specs=pl.BlockSpec((block, VDIM), lambda i, h: (i, h)),
        out_shape=jax.ShapeDtypeStruct((length, heads * VDIM), BF16),
        compiler_params=pltpu.CompilerParams(vmem_limit_bytes=VMEM_LIMIT),
        cost_estimate=pl.CostEstimate(
            flops=2 * heads * length * length * 384,
            bytes_accessed=8 * length * heads * NOPE,
            transcendentals=heads * length * length,
        ),
        name="attend_stage",
    )(*inputs)


def attend_back_stage(factor, heads, inputs, top):
    length, turned = inputs[1].shape
    block = min(length, 256)
    return pl.pallas_call(
        functools.partial(attend_back_kernel, factor),
        grid=(length // block, heads),
        in_specs=attend_specs(length, heads, turned, block)
        + [pl.BlockSpec((block, VDIM), lambda i, h: (i, h))],
        out_specs=[
            pl.BlockSpec((block, NOPE), lambda i, h: (i, h)),
            pl.BlockSpec((block, turned), lambda i, h: (i, 0)),
            pl.BlockSpec((heads, length, NOPE + VDIM), lambda i, h: (0, 0, 0)),
            pl.BlockSpec((length, turned), lambda i, h: (0, 0)),
        ],
        out_shape=[
            jax.ShapeDtypeStruct((length, heads * NOPE), BF16),
            jax.ShapeDtypeStruct((length, turned), F32),
            jax.ShapeDtypeStruct((heads, length, NOPE + VDIM), BF16),
            jax.ShapeDtypeStruct((length, turned), F32),
        ],
        scratch_shapes=[pltpu.VMEM((heads, length, NOPE + VDIM), F32)],
        compiler_params=pltpu.CompilerParams(vmem_limit_bytes=VMEM_LIMIT),
        cost_estimate=pl.CostEstimate(
            flops=2 * heads * length * length * 1024,
            bytes_accessed=16 * length * heads * NOPE,
            transcendentals=heads * length * length,
        ),
        name="attend_back_stage",
    )(*inputs, top)


def whole_spec(array):
    return pl.BlockSpec(
        array.shape, lambda i, *_: (0,) * array.ndim, pipeline_mode=pl.Buffered(1)
    )


def rows_spec(size, columns):
    return pl.BlockSpec((size, columns), lambda i, *_: (i, 0))


def forward_stage(place, slots, tokens, weights, capacity, experts, hidden, lanes):
    devices, _, rows = slots.shape
    blocks = 2 * lax.axis_size("fsdp")
    steps = devices // blocks
    width = tokens.shape[1]
    half = weights[1].shape[1]
    count = blocks * capacity
    sizes = [(count, width)] + [(count, half)] * 4 + [(blocks * rows, lanes)] * 3
    return pl.pallas_call(
        functools.partial(forward_kernel, blocks, capacity, experts, hidden),
        grid_spec=pltpu.PrefetchScalarGridSpec(
            num_scalar_prefetch=1,
            grid=(steps,),
            in_specs=[
                pl.BlockSpec((blocks, 1, rows), lambda i, *_: (i, 0, 0)),
                rows_spec(blocks * rows, width),
                *[whole_spec(weight) for weight in weights],
            ],
            out_specs=[rows_spec(*size) for size in sizes],
        ),
        out_shape=[
            jax.ShapeDtypeStruct((steps * size, columns), BF16) for size, columns in sizes
        ],
        compiler_params=pltpu.CompilerParams(vmem_limit_bytes=VMEM_LIMIT),
        cost_estimate=pl.CostEstimate(
            flops=devices * 4 * width * (capacity * half + rows * lanes),
            bytes_accessed=3 * devices * rows * width,
            transcendentals=devices * capacity * half,
        ),
        name="forward_stage",
    )(place, slots, tokens, *weights)


def backward_stage(slots, top, saved, weights, capacity):
    devices, _, rows = slots.shape
    blocks = 2 * lax.axis_size("fsdp")
    steps = devices // blocks
    width = top.shape[1]
    lanes, half = (weight.shape[1] for weight in weights)
    count = blocks * capacity
    slots_spec = pl.BlockSpec((blocks, 1, rows), lambda i, *_: (i, 0, 0))
    sizes = [(count, width)] + [(count, half)] * 2 + [(blocks * rows, 2 * lanes)]
    return pl.pallas_call(
        functools.partial(backward_kernel, blocks, capacity),
        grid=(steps,),
        in_specs=[
            slots_spec,
            rows_spec(blocks * rows, width),
            *[rows_spec(count, half) for _ in range(3)],
            *[rows_spec(blocks * rows, lanes) for _ in range(2)],
            *[whole_spec(weight) for weight in weights],
        ],
        out_specs=[rows_spec(*size) for size in sizes] + [slots_spec],
        out_shape=[
            jax.ShapeDtypeStruct((steps * size, columns), BF16) for size, columns in sizes
        ]
        + [jax.ShapeDtypeStruct(slots.shape, F32)],
        compiler_params=pltpu.CompilerParams(vmem_limit_bytes=VMEM_LIMIT),
        cost_estimate=pl.CostEstimate(
            flops=devices * 2 * width * (capacity * half + rows * lanes),
            bytes_accessed=4 * devices * rows * width,
            transcendentals=0,
        ),
        name="backward_stage",
    )(slots, top, *saved, *weights)


def combine_kernel(blocks, capacity, cuts, count, place_ref, slots_ref, *refs):
    lefts, rights = refs[:count], refs[count : 2 * count]
    shared_ref, shared_weight_ref = refs[2 * count : 2 * count + 2]
    outs = refs[2 * count + 2 : -1]
    rows_ref = refs[-1]
    rows = slots_ref.shape[-1]
    total = None
    for left, right in zip(lefts, rights):
        term = jnp.dot(left[...], right[...], preferred_element_type=F32)
        total = term if total is None else total + term
    rows_ref[...] = total.astype(BF16)
    half = blocks // 2
    for side in range(2):
        core = place_ref[1] ^ side
        for block in range(half):
            index = core * half + block
            chosen = one_hot(slots_ref[index], capacity).astype(BF16)
            there = pl.ds(pl.multiple_of(index * capacity, capacity), capacity)
            own = pl.ds(pl.multiple_of(index * rows, rows), rows)
            value = lax.dot_general(
                chosen,
                rows_ref[there, :],
                (((0,), (0,)), ((), ())),
                preferred_element_type=F32,
            ) + jnp.dot(
                shared_ref[own, :], shared_weight_ref[...], preferred_element_type=F32
            )
            value = value.astype(BF16)
            for part, (low, high) in enumerate(cuts):
                outs[2 * side + part][pl.ds(block * rows, rows), :] = value[:, low:high]


def combine_stage(place, slots, lefts, rights, shared, shared_weight, capacity):
    devices, _, rows = slots.shape
    blocks = 2 * lax.axis_size("fsdp")
    steps = devices // blocks
    width = rights[0].shape[1]
    cuts = halves_of(width)
    half = blocks // 2 * rows

    out_specs = [
        pl.BlockSpec((half, high - low), lambda i, place: (i ^ place[2], 0))
        for _ in range(2)
        for low, high in cuts
    ]
    out_shape = [
        jax.ShapeDtypeStruct((steps * half, high - low), BF16)
        for _ in range(2)
        for low, high in cuts
    ]
    flops = 2 * devices * width * (
        capacity * sum(left.shape[1] for left in lefts) + rows * (capacity + shared.shape[1])
    )
    outs = pl.pallas_call(
        functools.partial(combine_kernel, blocks, capacity, cuts, len(lefts)),
        grid_spec=pltpu.PrefetchScalarGridSpec(
            num_scalar_prefetch=1,
            grid=(steps,),
            in_specs=[
                pl.BlockSpec((blocks, 1, rows), lambda i, *_: (i, 0, 0)),
                *[rows_spec(blocks * capacity, left.shape[1]) for left in lefts],
                *[whole_spec(right) for right in rights],
                rows_spec(blocks * rows, shared.shape[1]),
                whole_spec(shared_weight),
            ],
            out_specs=out_specs,
            scratch_shapes=[pltpu.VMEM((blocks * capacity, width), BF16)],
        ),
        out_shape=out_shape,
        compiler_params=pltpu.CompilerParams(vmem_limit_bytes=VMEM_LIMIT),
        cost_estimate=pl.CostEstimate(
            flops=flops, bytes_accessed=devices * rows * width * 3, transcendentals=0
        ),
        name="combine_stage",
    )(place, slots, *lefts, *rights, shared, shared_weight)
    return outs[:2], outs[2:]


def per_device(
    tokens_in,
    segments,
    routes,
    cotangent,
    g_attn,
    g_kv,
    g_moe,
    w_query,
    w_kv_down,
    w_kv_up,
    w_out,
    w_router,
    w_shared_gate,
    w_shared_up,
    w_shared_down,
    w_expert_gate,
    w_expert_up,
    w_expert_down,
):
    micro_count, rows, width = tokens_in.shape
    seqs, line = lax.axis_size("seq"), lax.axis_size("fsdp")
    devices = seqs * line
    length = rows * seqs
    experts = devices // 2
    picked = routes.shape[2]
    capacity = max(2, rows * picked * 4 // (experts * 3))
    capacity = -(-capacity // 16) * 16
    heads = HEADS // seqs
    me_seq = lax.axis_index("seq")
    me = me_seq * line + lax.axis_index("fsdp")
    expert = me // 2
    factor = (NOPE + ROPE) ** (-0.5)
    frequency = THETA ** (-jnp.arange(ROPE // 2, dtype=F32) * 2.0 / ROPE)
    order = jnp.arange(seqs)
    ranks = (order ^ me_seq) >> 1 | ((order ^ me_seq) & 1) * (seqs // 2)
    order = me_seq ^ ((order % (seqs // 2)) * 2 + order // (seqs // 2))

    def to_relative(value):
        return value.reshape(seqs, rows, -1)[order].reshape(value.shape)

    def to_absolute(value):
        return value.reshape(seqs, rows, -1)[ranks].reshape(value.shape)

    places = (order[:, None] * rows + jnp.arange(rows)[None, :]).reshape(-1)
    angles = places.astype(F32)[:, None] * frequency[None, :]
    own_angles = angles[:rows]
    micros = range(micro_count)

    slots = Slots()
    place = jnp.stack([expert, me_seq & 1, me_seq >> 1]).astype(jnp.int32)

    piece = w_kv_down.shape[0]
    kv_columns = w_kv_down.shape[1]
    small = jnp.concatenate(
        [
            w_kv_down,
            w_router,
            g_attn[:, None],
            g_moe[:, None],
            jnp.pad(g_kv, (0, piece - g_kv.shape[0]))[:, None],
            routes.reshape(piece, -1).astype(BF16),
        ],
        axis=1,
    )
    small = lax.all_gather(small, BOTH, axis=0, tiled=True)

    query_width = heads * (NOPE + ROPE)
    out_width = heads * VDIM
    for_query = w_query.reshape(piece, seqs, heads, NOPE + ROPE)
    for_query = jnp.concatenate(
        [
            for_query[..., :NOPE].reshape(piece, seqs, -1),
            for_query[..., NOPE:].reshape(piece, seqs, -1),
        ],
        axis=2,
    ).transpose(1, 0, 2)
    for_out = w_out.reshape(seqs, out_width, piece).transpose(0, 2, 1)
    for_heads = jnp.concatenate([for_query, for_out], axis=2)
    for_heads = jnp.broadcast_to(
        for_heads[:, None], (seqs, line, piece, query_width + out_width)
    ).reshape(devices, piece, query_width + out_width)
    ready, for_heads = lax.optimization_barrier((tokens_in, for_heads))
    tokens = [Flow(gather_seq(ready[0])), None]
    for_heads = Flow(exchange(for_heads, BOTH))
    up_weight = Flow(
        exchange(jnp.broadcast_to(w_kv_up[None], (line,) + w_kv_up.shape), "fsdp")
    )
    hidden = w_shared_gate.shape[1] // devices

    def pack_shared(gate, up, down):
        return jnp.concatenate(
            [
                gate.reshape(piece, devices, hidden).transpose(1, 0, 2),
                up.reshape(piece, devices, hidden).transpose(1, 0, 2),
                down.reshape(devices, hidden, piece).transpose(0, 2, 1),
            ],
            axis=2,
        )

    for_shared = slots.run(tokens[:1], pack_shared, w_shared_gate, w_shared_up, w_shared_down)
    for_shared = Flow(exchange(for_shared, BOTH))
    slots.run([tokens[0], for_heads, up_weight])
    tops = [lax.all_gather(slots.tie(cotangent[0]), BOTH, axis=0, tiled=True), None]
    slots.finish(tokens[0])
    (small,) = slots.run([], lambda *given: given, small)
    for_heads, up_weight = for_heads.value, up_weight.value
    for_heads = for_heads.reshape(width, query_width + out_width)
    query_weight = for_heads[:, :query_width]
    out_weight = for_heads[:, query_width:]
    up_weight = up_weight.transpose(1, 0, 2).reshape(KVR, -1)
    down_weight = small[:, :kv_columns]
    router_weight = small[:, kv_columns : kv_columns + experts]
    last = kv_columns + experts
    gain_one = small[:, last].astype(F32)
    gain_two = small[:, last + 1].astype(F32)
    gain_latent = small[:, last + 2].reshape(devices, piece)[:, : g_kv.shape[0]].reshape(-1)
    routes_all = small[:, last + 3 :].astype(jnp.int32).reshape((devices,) + routes.shape)
    gain_latent = gain_latent.astype(F32)

    def projections(tokens):
        unit_one, _ = normed(tokens.astype(F32))
        normed_one = (unit_one * gain_one).astype(BF16)
        query_raw = product(normed_one, query_weight)
        query = query_raw[:, : heads * NOPE].astype(BF16)
        turned = query_raw[:, heads * NOPE :].reshape(length, heads, ROPE)
        turned = turned_lanes(rotate(turned, angles[:, None, :]).reshape(length, -1))
        latent = product(normed_one, down_weight)
        unit_latent, factor_latent = normed(latent[:, :KVR])
        latent_norm = (unit_latent * gain_latent).astype(BF16)
        key_rope = rotate(latent[:, KVR:], angles).astype(BF16)
        key_value = product(latent_norm, up_weight).astype(BF16)
        key_rope = turned_lanes(jnp.tile(key_rope, (1, heads)))
        return (
            normed_one,
            latent_norm,
            (query, turned, key_value, key_rope),
            unit_latent[:rows],
            factor_latent[:rows],
        )

    def turned_lanes(value):
        return jnp.pad(value.astype(BF16), ((0, 0), (0, -value.shape[1] % 128)))

    def marks_of(micro):
        segment = segments[micro].reshape(seqs, rows)[order].reshape(-1)
        return segment[:, None], segment[None, :], places[:, None], places[None, :]

    def attend(micro, query):
        inputs = (query,) + projected[micro][2][1:] + marks[micro]
        attended = attend_stage(factor, heads, inputs)
        return attended, right_product(attended, out_weight).astype(BF16)

    def home_forward(micro, summed):
        residual = tokens_in[micro].astype(F32) + summed.astype(F32)
        unit_two, factor_two = normed(residual)
        normed_two = (unit_two * gain_two).astype(BF16)
        return residual, unit_two, factor_two, normed_two

    marks = [marks_of(micro) for micro in micros]
    projected = [None, None]
    attended = [None, None]
    residuals = [None, None]
    normed_alls = [None, None]
    tokens[1] = Flow(gather_seq(slots.tie(tokens_in[1])))
    projected[0] = slots.run([tokens[1]], projections, tokens[0].value)
    attended[0] = slots.run(
        [tokens[1]], functools.partial(attend, 0), projected[0][2][0]
    )
    summed = Flow(scatter_seq(attended[0][1], rows))
    slots.finish(tokens[1], summed)
    projected[1] = slots.run([summed, for_shared], projections, tokens[1].value)
    attended[1] = slots.run([summed], functools.partial(attend, 1), projected[1][2][0])
    summed_two = Flow(scatter_seq(attended[1][1], rows))
    slots.finish(summed, summed_two)
    residuals[0] = home_forward(0, summed.value)
    first, tops[0] = lax.optimization_barrier((residuals[0][3], tops[0]))
    normed_alls[0] = lax.all_gather(first, BOTH, axis=0, tiled=True)
    slots.finish(summed_two)
    residuals[1] = home_forward(1, summed_two.value)
    normed_alls[1] = lax.all_gather(residuals[1][3], BOTH, axis=0, tiled=True)
    top_flow = Flow(gather_all(slots.tie(cotangent[1]), place))
    for _ in range(line):
        slots.run([top_flow])

    lanes = -(-(hidden + experts) // 128) * 128

    def padded(parts):
        parts = jnp.concatenate(parts, axis=1)
        return jnp.pad(parts, ((0, 0), (0, lanes - parts.shape[1])))

    for_shared = for_shared.value.reshape(width, 3 * hidden)
    shared_gate = for_shared[:, :hidden]
    shared_up = for_shared[:, hidden : 2 * hidden]
    shared_down = padded([for_shared[:, 2 * hidden :]])
    wide_weight = jnp.concatenate(
        [padded([shared_gate, router_weight]), padded([shared_up])], axis=1
    )
    shared_in = jnp.concatenate([padded([shared_gate]), padded([shared_up])], axis=1)
    gate_weight = w_expert_gate[0]
    up_expert = w_expert_up[0]
    down_expert = w_expert_down[0]
    forward_weights = (wide_weight, gate_weight, up_expert)
    backward_weights = (shared_down, down_expert.T)
    transposed = (gate_weight.T, up_expert.T, shared_in.T, shared_down.T)

    def slots_of(micro):
        hit = jnp.any(routes_all[:, micro] == expert, axis=-1)
        rank = jnp.cumsum(hit.astype(jnp.int32), axis=1) - 1
        return jnp.where(hit, rank, -1)[:, None, :]

    def forward_of(seats, tokens):
        return forward_stage(
            place, seats, tokens, forward_weights, capacity, experts, hidden, lanes
        )

    def backward_of(seats, top, made):
        return backward_stage(
            seats, top, (made[2], made[3], made[4], made[6], made[7]), backward_weights, capacity
        )

    def grads_to_tokens(seats, back):
        return combine_stage(
            place, seats, back[1:3], transposed[:2], back[3], transposed[2], capacity
        )

    def outputs_to_tokens(seats, made):
        return combine_stage(
            place, seats, made[1:2], (down_expert,), made[5], transposed[3], capacity
        )

    def routed_pairs(made, back):
        return (made[0], back[1]), (made[0], back[2]), (made[1], back[0])

    def routed_grads(*pairs):
        return tuple(left_product(*pair) for pair in pairs)

    def shared_grads_of(tokens, top, made, back):
        return left_product(tokens, back[3]), left_product(top, made[5])

    def added(function):
        def call(before, *values):
            return tuple(old + new for old, new in zip(before, function(*values)))

        return call

    def gate_grads_home(made):
        return Flow(exchange(made.reshape(devices, rows), BOTH))

    def home_backward(micro, grad_two, gate_grad):
        _, unit_two, factor_two, normed_two = residuals[micro]
        logits = product(normed_two, router_weight)
        shifted = jnp.exp(logits - jnp.max(logits, axis=-1, keepdims=True))
        router = shifted / jnp.sum(shifted, axis=-1, keepdims=True)
        router_in = jnp.sum(gate_grad.reshape(experts, 2, rows), axis=1).T
        grad_logits = (
            router * (router_in - jnp.sum(router * router_in, axis=-1, keepdims=True))
        ).astype(BF16)
        grad_two = grad_two + right_product(grad_logits, router_weight)
        grad_residual = cotangent[micro].astype(F32) + norm_back(
            grad_two * gain_two, unit_two, factor_two
        )
        return (
            grad_residual,
            left_product(normed_two, grad_logits),
            jnp.sum(grad_two * unit_two, axis=0),
        )

    def attend_backward(micro, grad_attn_out):
        grad_attended = to_relative(product(grad_attn_out, out_weight).astype(BF16))
        inputs = projected[micro][2] + marks[micro]
        return attend_back_stage(factor, heads, inputs, grad_attended)

    def latents_backward(grad_key_value, grad_rope):
        grad_rope = jnp.sum(grad_rope[:, : heads * ROPE].reshape(length, heads, ROPE), axis=1)
        grad_key_value = grad_key_value.transpose(1, 0, 2).reshape(length, -1)
        grad_latent_part = right_product(grad_key_value, up_weight)
        part = jnp.concatenate([grad_latent_part, grad_rope], axis=1).astype(BF16)
        return part, grad_key_value

    def queries_backward(grad_query, grad_turned):
        grad_turned = grad_turned[:, : heads * ROPE].reshape(length, heads, ROPE)
        grad_turned = rotate(grad_turned, -angles[:, None, :]).reshape(length, -1)
        grad_query_raw = jnp.concatenate([grad_query, grad_turned.astype(BF16)], axis=1)
        one_part = right_product(to_absolute(grad_query_raw), query_weight)
        return one_part.astype(BF16), grad_query_raw

    def projections_backward(grad_query, grad_turned, grad_key_value, grad_rope):
        return (
            *latents_backward(grad_key_value, grad_rope),
            *queries_backward(grad_query, grad_turned),
        )

    def head_grads(projected, attended, grad_attn_out, grad_query_raw, grad_key_value):
        return (
            left_product(projected[0], grad_query_raw),
            left_product(grad_attn_out, to_absolute(attended)),
            left_product(grad_key_value, projected[1]),
        )

    def latent_backward(back, projected):
        unit_latent, factor_latent = projected[3:]
        grad_latent_norm = back[:, :KVR].astype(F32)
        grad_compressed = norm_back(grad_latent_norm * gain_latent, unit_latent, factor_latent)
        grad_latent = jnp.concatenate(
            [grad_compressed, rotate(back[:, KVR:].astype(F32), -own_angles)], axis=-1
        ).astype(BF16)
        return grad_latent, jnp.sum(grad_latent_norm * unit_latent, axis=0)

    def input_backward(micro, back, grad_latent, grad_residual):
        unit_one, factor_one = normed(tokens_in[micro].astype(F32))
        grad_one = back.astype(F32) + right_product(grad_latent, down_weight)
        return (
            grad_residual + norm_back(grad_one * gain_one, unit_one, factor_one),
            jnp.sum(grad_one * unit_one, axis=0),
        )

    def line_blocks(value):
        return value.astype(BF16).reshape(line, -1, value.shape[-1])

    def down_grads(normed_one, latents):
        columns = lax.dynamic_slice_in_dim(
            normed_one, me_seq * (width // seqs), width // seqs, axis=1
        )
        return left_product(columns, latents)

    seats = [slots_of(micro) for micro in micros]
    made = [None, None]
    def home_and_out(micro):
        home = home_backward(micro, grads[micro].value, gate_grad[micro].value)
        return home, lax.all_gather(home[0].astype(BF16), "seq", axis=0, tiled=True)

    def attention_back(*given):
        return projections_backward(*attend_backward(*given))

    gate_grad = [None, None]
    grads = [None, None]
    sums = [None, None]
    homes = [None, None]
    attn_out = [None, None]
    backs = [None, None]
    back = [None, None]
    finals = [None, None]

    def shared_home(shared_grads):
        shared_grads = shared_grads.astype(F32)
        return (
            shared_grads[:, :, :hidden].transpose(1, 0, 2).reshape(piece, -1),
            shared_grads[:, :, hidden : 2 * hidden].transpose(1, 0, 2).reshape(piece, -1),
            shared_grads[:, :, 2 * hidden :].transpose(0, 2, 1).reshape(-1, piece),
        )

    made[0] = slots.run([], forward_of, seats[0], normed_alls[0])
    back[0] = slots.run([top_flow], backward_of, seats[0], tops[0], made[0])
    gate_grad[0] = gate_grads_home(back[0][4])
    sides = slots.run([top_flow, gate_grad[0]], grads_to_tokens, seats[0], back[0])
    grads[0] = Flow(reduce_all(*sides, rows))
    tops[1] = slots.finish(top_flow)
    sides = slots.run([grads[0]], outputs_to_tokens, seats[0], made[0])
    sums[0] = Flow(reduce_all(*sides, rows))
    routed, shared = slots.run(
        [grads[0], sums[0]],
        lambda pairs, *given: (routed_grads(*pairs), shared_grads_of(*given)),
        routed_pairs(made[0], back[0]),
        normed_alls[0],
        tops[0],
        made[0],
        back[0],
    )
    made[1] = slots.run([grads[0]], forward_of, seats[1], normed_alls[1])
    back[1] = slots.run([], backward_of, seats[1], tops[1], made[1])
    gate_grad[1] = gate_grads_home(back[1][4])
    sides = slots.run(
        [grads[0], sums[0], gate_grad[1]], grads_to_tokens, seats[1], back[1]
    )
    grads[1] = Flow(reduce_all(*sides, rows))
    slots.finish(grads[0])
    homes[0], attn_out[0] = home_and_out(0)
    sides = slots.run([grads[1], sums[0]], outputs_to_tokens, seats[1], made[1])
    sums[1] = Flow(reduce_all(*sides, rows))
    parts = slots.run(
        [grads[1], sums[0]], added(routed_grads), routed, *routed_pairs(made[1], back[1])
    )
    shared = slots.run(
        [grads[1], sums[1]],
        added(shared_grads_of),
        shared,
        normed_alls[1],
        tops[1],
        made[1],
        back[1],
    )
    shared = jnp.concatenate(
        [shared[0][:, :hidden], shared[0][:, lanes : lanes + hidden], shared[1][:, :hidden]],
        axis=1,
    )
    shared = Flow(exchange(shared.astype(BF16).reshape(devices, piece, 3 * hidden), BOTH))
    parted, grad_key_value, one_part, grad_query_raw = slots.run(
        [grads[1], sums[1]],
        lambda given: projections_backward(*attend_backward(0, given)),
        attn_out[0],
    )
    slots.finish(grads[1])
    homes[1], attn_out[1] = home_and_out(1)
    whole_part, _ = lax.optimization_barrier(
        (jnp.concatenate([one_part, to_absolute(parted)], axis=1), homes[1][0])
    )
    whole_part = lax.psum_scatter(whole_part, "seq", scatter_dimension=0, tiled=True)
    head_sums = slots.run(
        [],
        head_grads,
        projected[0],
        attended[0][0],
        attn_out[0],
        grad_query_raw,
        grad_key_value,
    )
    scored = slots.run([sums[1]], functools.partial(attend_backward, 1), attn_out[1])
    parted, grad_key_value = slots.run([shared], latents_backward, *scored[2:])
    latent_sums = Flow(scatter_seq(parted, rows))
    one_part, grad_query_raw = slots.run([latent_sums], queries_backward, *scored[:2])
    one_part = lax.psum_scatter(one_part, "seq", scatter_dimension=0, tiled=True)

    def all_head_grads(before, *given):
        query, out, up = added(head_grads)(before, *given)
        packed = jnp.concatenate([query, out], axis=1).astype(BF16)
        return packed.reshape(devices, piece, -1), line_blocks(up)

    grad_heads, grad_up = slots.run(
        [latent_sums, sums[1]],
        all_head_grads,
        head_sums,
        projected[1],
        attended[1][0],
        attn_out[1],
        grad_query_raw,
        grad_key_value,
    )
    grad_heads = Flow(exchange(grad_heads, BOTH))
    grad_up = Flow(exchange_line(grad_up))
    latents = [latent_backward(whole_part[:, width:], projected[0]), None]
    finals[0] = slots.run(
        [latent_sums],
        functools.partial(input_backward, 0),
        whole_part[:, :width],
        latents[0][0],
        homes[0][0],
    )
    slots.finish(latent_sums)
    latents[1] = latent_backward(latent_sums.value, projected[1])
    latent_flow = Flow(gather_seq(jnp.concatenate([latent[0] for latent in latents], axis=1)))
    shared_final = slots.run([latent_flow], shared_home, shared.value)
    finals[1] = slots.run(
        [latent_flow, grad_heads],
        functools.partial(input_backward, 1),
        one_part,
        latents[1][0],
        homes[1][0],
    )
    tiny = jnp.concatenate(
        [
            sum(home[1] for home in homes).reshape(devices, -1),
            sum(final[1] for final in finals).reshape(devices, -1),
            sum(home[2] for home in homes).reshape(devices, -1),
            sum(latent[1] for latent in latents).reshape(devices, -1),
        ],
        axis=1,
    )
    tiny = Flow(exchange(tiny, BOTH))
    slots.finish(latent_flow)
    grad_kv_down = sum(
        down_grads(
            projected[micro][0],
            latent_flow.value[:, micro * kv_columns : (micro + 1) * kv_columns],
        )
        for micro in micros
    )
    grad_kv_down = Flow(exchange_line(line_blocks(grad_kv_down)))
    slots.run([grad_kv_down, grad_up, tiny, grad_heads, sums[0], sums[1]])
    for flow in (sums[0], sums[1]):
        slots.finish(flow)
    outputs = [
        (residuals[micro][0] + sums[micro].value).astype(BF16) for micro in micros
    ]
    grad_kv_down = grad_kv_down.value
    grad_kv_up = grad_up.value.T
    grad_heads = grad_heads.value.reshape(seqs, line, piece, -1)
    grad_heads = jnp.sum(grad_heads.astype(F32), axis=1)
    grad_query_weight = jnp.concatenate(
        [
            grad_heads[:, :, : heads * NOPE].reshape(seqs, piece, heads, NOPE),
            grad_heads[:, :, heads * NOPE : query_width].reshape(seqs, piece, heads, ROPE),
        ],
        axis=3,
    )
    grad_query_weight = grad_query_weight.transpose(1, 0, 2, 3).reshape(piece, -1)
    grad_out_weight = grad_heads[:, :, query_width:].transpose(0, 2, 1).reshape(-1, piece)
    tiny = jnp.sum(tiny.value, axis=0)
    first = piece * experts
    return (
        jnp.stack(outputs),
        jnp.stack([final[0] for final in finals]),
        tiny[first : first + piece],
        tiny[first + 2 * piece :],
        tiny[first + piece : first + 2 * piece],
        grad_query_weight,
        grad_kv_down,
        grad_kv_up,
        grad_out_weight,
        tiny[:first].reshape(piece, experts),
        *shared_final,
        parts[0][None],
        parts[1][None],
        parts[2][None],
    )


def solution(mesh):
    return jax.shard_map(
        per_device,
        mesh=mesh,
        in_specs=(
            P("fsdp", "seq", None),
            P("fsdp", None),
            P("fsdp", "seq", None),
            P("fsdp", "seq", None),
            P(BOTH),
            P(BOTH),
            P(BOTH),
            P(BOTH, None),
            P(BOTH, None),
            P(None, BOTH),
            P(None, BOTH),
            P(BOTH, None),
            P(BOTH, None),
            P(BOTH, None),
            P(None, BOTH),
            P(BOTH, None, None),
            P(BOTH, None, None),
            P(BOTH, None, None),
        ),
        out_specs=(
            P("fsdp", "seq", None),
            P("fsdp", "seq", None),
            P(BOTH),
            P(BOTH),
            P(BOTH),
            P(BOTH, None),
            P(BOTH, None),
            P(None, BOTH),
            P(None, BOTH),
            P(BOTH, None),
            P(BOTH, None),
            P(BOTH, None),
            P(None, BOTH),
            P(BOTH, None, None),
            P(BOTH, None, None),
            P(BOTH, None, None),
        ),
        check_vma=False,
    )
```
